256 devices in a mesh: inp: 16 (over y, z_lo, core), hid: 16 (over z_hi, x).
Axes of the slice: x: 4, y: 4, z: 8 (z_hi: 4, z_lo: 2; z = z_hi * 2 + z_lo), core: 2. Of those that a mesh axis runs over, the one named last changes fastest.
Arguments:
- inputs: bfloat16 [128, 16384], P(None, 'inp'), may hold values from -6 to 6
- out_grad: bfloat16 [128, 16384], P(None, 'inp'), may hold values from -6 to 6
- gate_index: int32 [8192, 26624], P('inp', 'hid'), may hold values from 0 to 255, as said below
- up_index: int32 [8192, 26624], P('inp', 'hid'), may hold values from 0 to 255, as said below
- down_index: int32 [13312, 16384], P('hid', 'inp'), may hold values from 0 to 255, as said below
- gate_table: float32 [16, 26624], P(None, 'hid'), may hold values from -0.046875 to 0.046875
- up_table: float32 [16, 26624], P(None, 'hid'), may hold values from -0.046875 to 0.046875
- down_table: float32 [16, 16384], P(None, 'inp'), may hold values from -0.0390625 to 0.0390625
Outputs:
- input_grad: bfloat16 [128, 16384], P('hid', 'inp')
- gate_table_grad: float32 [16, 26624], P(None, 'hid')
- up_table_grad: float32 [16, 26624], P(None, 'hid')
- down_table_grad: float32 [16, 16384], P(None, 'inp')
The draws below stay inside these ranges and needn't reach their ends.
Inputs may be any that keep to these rules, and one draw needn't show every extreme that they name: `gate_index`: each word holds two independent 4-bit table entries. `up_index`: each word holds two independent 4-bit table entries. `down_index`: each word holds two independent 4-bit table entries.
All inputs are finite; a program needn't handle non-finite values.
Results may differ from the reference program's by a relative error of at most 0.0072.
Values may be sent and summed in bfloat16 or wider, within the bound.
No kernel may reach another device: no remote copies, remote signals or barrier semaphores. Data moves between devices by JAX's collectives and lax.ppermute only.
A program may use at most 128 MiB of HBM per device.

```python
import jax
import jax.numpy as jnp
from jax import lax

D = 16384
FF = 26624
ENTRIES = 16
TOKENS = 128
N_HID = 16


def packed_words(key, salt, rows, cols):
    sub = jax.random.fold_in(key, salt)
    words = jax.random.randint(sub, (rows, cols), 0, 256, dtype=jnp.int32)
    return words.at[0, 0].set(255).at[0, 1].set(0)


def draw_gate_index(key, part):
    return packed_words(key, 7101, D // 2, FF)


def draw_up_index(key, part):
    return packed_words(key, 7202, D // 2, FF)


def draw_down_index(key, part):
    return packed_words(key, 7303, FF // 2, D)


def levels(rng, shape, split, low, high):
    def one(dim, blocks):
        steps = jax.random.uniform(jax.random.fold_in(jax.random.fold_in(rng, 6), dim), (blocks,), jnp.float32, low / len(split), high / len(split))
        return jnp.repeat(jnp.exp(steps), shape[dim] // blocks).reshape((-1,) + (1,) * (len(shape) - dim - 1))

    gain = one(*split[0])
    for cut in split[1:]:
        gain = gain * one(*cut)
    return gain


def gaussian(stream_key, extent, scale, most, split=(), held_as=jnp.bfloat16):
    values = jax.random.normal(stream_key, extent, jnp.float32) * scale
    if len(split) > 0:
        values = levels(stream_key, extent, split, -0.22, 0.18) * values
    return jnp.clip(values, min=-most, max=most).astype(held_as)


def setup_inputs(seed: int = 0) -> dict:
    key_of = jax.random.split(jax.random.key(seed), 9)
    inputs = gaussian(key_of[0], (TOKENS, D), 1.0, 6.0, ((1, 16),))
    out_grad = gaussian(key_of[1], (TOKENS, D), 1.0, 6.0, ((1, 16),))
    gate_index = draw_gate_index(jax.random.fold_in(key_of[8], 71), 0)
    up_index = draw_up_index(jax.random.fold_in(key_of[8], 71), 0)
    down_index = draw_down_index(jax.random.fold_in(key_of[8], 71), 0)
    gate_table = gaussian(key_of[5], (ENTRIES, FF), D ** -0.5, 0.046875, ((1, 16),), jnp.float32)
    up_table = gaussian(key_of[6], (ENTRIES, FF), D ** -0.5, 0.046875, ((1, 16),), jnp.float32)
    down_table = gaussian(key_of[7], (ENTRIES, D), FF ** -0.5, 0.0390625, ((1, 16),), jnp.float32)
    return {"inputs": inputs, "out_grad": out_grad, "gate_index": gate_index, "up_index": up_index, "down_index": down_index, "gate_table": gate_table, "up_table": up_table, "down_table": down_table}


def unpack(packed):
    parts = [jnp.bitwise_and(jnp.right_shift(packed, 4 * nibble), 15) for nibble in range(2)]
    stacked = jnp.stack(parts, axis=1)
    return stacked.reshape(packed.shape[0] * 2, packed.shape[1]).astype(jnp.int32)


def decode(indices, lookup):
    summed = jnp.zeros(indices.shape, jnp.float32)
    for bucket in range(16):
        summed = summed + jnp.where(indices == bucket, lookup[bucket][None, :], 0.0)
    return summed.astype(jnp.bfloat16)


def binned(grads, indices):
    return jnp.stack([jnp.sum(jnp.where(indices == bucket, grads, 0.0), axis=0) for bucket in range(16)])


def reference(inputs, out_grad, gate_index, up_index, down_index, gate_table, up_table, down_table):
    blocks = N_HID
    block_width = FF // blocks
    scale = 1.0 / TOKENS

    def one_block(carry, block_id):
        input_acc, down_acc = carry
        begin = (block_id * block_width).astype(jnp.int32)
        packed_begin = (block_id * (block_width // 2)).astype(jnp.int32)
        idx_gate = unpack(lax.dynamic_slice_in_dim(gate_index, begin, block_width, 1))
        idx_up = unpack(lax.dynamic_slice_in_dim(up_index, begin, block_width, 1))
        idx_down = unpack(lax.dynamic_slice_in_dim(down_index, packed_begin, block_width // 2, 0))
        w_gate = decode(idx_gate, lax.dynamic_slice_in_dim(gate_table, begin, block_width, 1))
        w_up = decode(idx_up, lax.dynamic_slice_in_dim(up_table, begin, block_width, 1))
        w_down = decode(idx_down, down_table)
        pre_gate = jnp.dot(inputs, w_gate, preferred_element_type=jnp.float32)
        pre_up = jnp.dot(inputs, w_up, preferred_element_type=jnp.float32)
        hidden_grad = jnp.dot(out_grad, w_down.T, preferred_element_type=jnp.float32)
        sig_gate = jax.nn.sigmoid(pre_gate)
        silu_gate = pre_gate * sig_gate
        activ = (silu_gate * pre_up).astype(jnp.bfloat16)
        gate_grad = (hidden_grad * pre_up * sig_gate * (1.0 + pre_gate * (1.0 - sig_gate))).astype(jnp.bfloat16)
        up_grad = (hidden_grad * silu_gate).astype(jnp.bfloat16)
        input_acc = input_acc + jnp.dot(gate_grad, w_gate.T, preferred_element_type=jnp.float32) + jnp.dot(up_grad, w_up.T, preferred_element_type=jnp.float32)
        gate_bins = binned(jnp.dot(inputs.T, gate_grad, preferred_element_type=jnp.float32), idx_gate) * scale
        up_bins = binned(jnp.dot(inputs.T, up_grad, preferred_element_type=jnp.float32), idx_up) * scale
        down_acc = down_acc + binned(jnp.dot(activ.T, out_grad, preferred_element_type=jnp.float32), idx_down)
        return (input_acc, down_acc), (gate_bins, up_bins)

    start_carry = (jnp.zeros((TOKENS, D), jnp.float32), jnp.zeros((16, D), jnp.float32))
    (input_acc, down_acc), (gate_bins, up_bins) = lax.scan(one_block, start_carry, jnp.arange(blocks, dtype=jnp.int32))
    gate_table_grad = jnp.transpose(gate_bins, (1, 0, 2)).reshape(16, FF)
    up_table_grad = jnp.transpose(up_bins, (1, 0, 2)).reshape(16, FF)
    return input_acc.astype(jnp.bfloat16), gate_table_grad, up_table_grad, down_acc * scale
```

```python
import functools

import jax
import jax.numpy as jnp
from jax import lax
from jax.experimental import pallas as pl
from jax.experimental.pallas import tpu as pltpu
from jax.sharding import PartitionSpec as P

BF16 = jnp.bfloat16
F32 = jnp.float32
I32 = jnp.int32
ENTRIES = 16
TOKENS = 128
LANES = 128
HBM_BYTES_PER_US = 3_000_000


def params(mib=40):
    return pltpu.CompilerParams(vmem_limit_bytes=mib * 1024 * 1024)


def cost(us):
    return pl.CostEstimate(flops=0, bytes_accessed=int(us * HBM_BYTES_PER_US), transcendentals=0)


def shape(dims, dtype):
    return jax.ShapeDtypeStruct(dims, dtype)


def whole(dims):
    return pl.BlockSpec(dims, lambda i: (0,) * len(dims))


def dot(a, b):
    return jnp.dot(a, b, preferred_element_type=F32)


def dot_nt(a, b):
    return lax.dot_general(a, b, (((1,), (1,)), ((), ())), preferred_element_type=F32)


def dot_tn(a, b):
    return lax.dot_general(a, b, (((0,), (0,)), ((), ())), preferred_element_type=F32)


def split_order(block):
    rows = lax.broadcasted_iota(I32, (block, block), 0)
    cols = lax.broadcasted_iota(I32, (block, block), 1)
    half = block // 2
    source = jnp.where(cols < half, 2 * cols, 2 * (cols - half) + 1)
    return (rows == source).astype(BF16)


def lookup(low, high, entry):
    at = entry & 7
    from_low = jnp.take_along_axis(low, at, axis=0, mode="promise_in_bounds")
    from_high = jnp.take_along_axis(high, at, axis=0, mode="promise_in_bounds")
    return jnp.where(entry >= 8, from_high, from_low)


def decode_block(index_ref, table_ref, weight_ref):
    words, cols = index_ref.shape

    def tile(j, carry):
        at = pl.ds(pl.multiple_of(j * LANES, LANES), LANES)
        low, high = table_ref[0:8, at], table_ref[8:16, at]
        for row in range(0, words, 16):
            even, odd = [], []
            for part in (row, row + 8):
                word = index_ref[part : part + 8, at]
                even.append(lookup(low, high, word & 15))
                odd.append(lookup(low, high, (word >> 4) & 15))
            weight_ref[row : row + 16, at] = jnp.concatenate(even, axis=0).astype(BF16)
            weight_ref[words + row : words + row + 16, at] = jnp.concatenate(odd, axis=0).astype(BF16)
        return carry

    lax.fori_loop(0, cols // LANES, tile, 0)


def forward_down_kernel(order_ref, merge_ref, grad_ref, index_ref, table_ref, near_ref, far_ref, ordered_ref, weight_ref):
    @pl.when(pl.program_id(0) == 0)
    def _():
        ordered_ref[...] = dot(order_ref[...], grad_ref[...]).astype(BF16)

    decode_block(index_ref, table_ref, weight_ref)
    hidden = dot_nt(ordered_ref[...], weight_ref[...]).astype(BF16)
    hidden = dot(hidden, merge_ref[...]).astype(BF16)
    near_ref[...] = hidden[: TOKENS // 2]
    far_ref[...] = hidden[TOKENS // 2 :]


def forward_down(order, merge, grad, index, table):
    words, width = index.shape
    block = merge.shape[0]
    half = TOKENS // 2
    return pl.pallas_call(
        forward_down_kernel,
        grid=(2 * words // block,),
        in_specs=[
            whole((TOKENS, TOKENS)),
            whole((block, block)),
            whole((TOKENS, width)),
            pl.BlockSpec((block // 2, width), lambda i: (i, 0)),
            whole((ENTRIES, width)),
        ],
        out_specs=[
            pl.BlockSpec((half, block), lambda i: (0, i)),
            pl.BlockSpec((half, block), lambda i: (0, i)),
            whole((TOKENS, width)),
        ],
        out_shape=[
            shape((half, 2 * words), BF16),
            shape((half, 2 * words), BF16),
            shape((TOKENS, width), BF16),
        ],
        scratch_shapes=[pltpu.VMEM((block, width), BF16)],
        compiler_params=params(),
        cost_estimate=cost(5),
        name="forward_down",
    )(order, merge, grad, index, table)


def forward_up_kernel(first, *refs):
    if first:
        order_ref, split_ref, x_ref, index_ref, table_ref, near_ref, far_ref, weight_ref, ordered_ref, sum_ref = refs
        x = dot(order_ref[...], x_ref[...]).astype(BF16)
        x = dot(x, split_ref[...]).astype(BF16)
        ordered_ref[...] = x
    else:
        x_ref, index_ref, table_ref, near_ref, far_ref, weight_ref, sum_ref = refs
        x = x_ref[...]
    decode_block(index_ref, table_ref, weight_ref)
    step = pl.program_id(0)

    @pl.when(step == 0)
    def _():
        sum_ref[...] = jnp.zeros_like(sum_ref)

    sum_ref[...] += dot(x, weight_ref[...])

    @pl.when(step == pl.num_programs(0) - 1)
    def _():
        near_ref[...] = sum_ref[: TOKENS // 2, :].astype(BF16)
        far_ref[...] = sum_ref[TOKENS // 2 :, :].astype(BF16)


def forward_up(order, split, x, index, table, first):
    words, width = index.shape
    block = split.shape[0]
    half = TOKENS // 2
    by_column = pl.BlockSpec((TOKENS, block), lambda i: (0, i))
    head = [whole((TOKENS, TOKENS)), whole((block, block))] if first else []
    tail_specs = [by_column] if first else []
    tail_shapes = [shape((TOKENS, 2 * words), BF16)] if first else []
    args = (order, split, x, index, table) if first else (x, index, table)
    return pl.pallas_call(
        functools.partial(forward_up_kernel, first),
        grid=(2 * words // block,),
        in_specs=head + [by_column, pl.BlockSpec((block // 2, width), lambda i: (i, 0)), whole((ENTRIES, width))],
        out_specs=[whole((half, width)), whole((half, width)), pl.BlockSpec((block, width), lambda i: (i, 0))] + tail_specs,
        out_shape=[
            shape((half, width), BF16),
            shape((half, width), BF16),
            shape((2 * words, width), BF16),
        ]
        + tail_shapes,
        scratch_shapes=[pltpu.VMEM((TOKENS, width), F32)],
        compiler_params=params(),
        cost_estimate=cost(5),
        name="forward_gate" if first else "forward_up",
    )(*args)


def entry_sums_kernel(block, x_ref, index_ref, *refs):
    out_ref, entry_ref = refs[-2:]
    words = index_ref.shape[0]
    half = block // 2
    for row in range(0, words, 16):
        word = index_ref[row : row + 16, :]
        at = row // half * block + row % half
        entry_ref[at : at + 16, :] = (word & 15).astype(jnp.int16)
        entry_ref[at + half : at + half + 16, :] = ((word >> 4) & 15).astype(jnp.int16)
    one, zero = jnp.ones((), BF16), jnp.zeros((), BF16)
    for entry in range(ENTRIES):
        chosen = jnp.where(entry_ref[...] == jnp.int16(entry), one, zero)
        out_ref[entry] = dot(x_ref[...], chosen).astype(BF16)


def entry_sums(x, index, block, begin, end, so_far):
    words, width = index.shape
    wide = 256
    held = [] if so_far is None else [so_far]
    return pl.pallas_call(
        functools.partial(entry_sums_kernel, block),
        grid=(end - begin,),
        in_specs=[
            whole((TOKENS, 2 * words)),
            pl.BlockSpec((words, wide), lambda i: (0, i + begin)),
        ]
        + [pl.BlockSpec(memory_space=pl.ANY)] * len(held),
        out_specs=pl.BlockSpec((ENTRIES, TOKENS, wide), lambda i: (0, 0, i + begin)),
        out_shape=shape((ENTRIES, TOKENS, width), BF16),
        scratch_shapes=[pltpu.VMEM((2 * words, wide), jnp.int16)],
        input_output_aliases={2: 0} if held else {},
        compiler_params=params(),
        cost_estimate=cost(1.7 * (end - begin)),
        name="entry_sums",
    )(x, index, *held)


def table_sums_kernel(near_ref, far_ref, sums_ref, out_ref):
    grad = jnp.concatenate([near_ref[...], far_ref[...]], axis=0).astype(F32)
    for entry in range(ENTRIES):
        product = sums_ref[entry].astype(F32) * grad
        out_ref[entry : entry + 1, :] = jnp.sum(product, axis=0, keepdims=True)


def table_sums(near, far, sums):
    width = near.shape[1]
    wide = 256
    half = TOKENS // 2
    return pl.pallas_call(
        table_sums_kernel,
        grid=(pl.cdiv(width, wide),),
        in_specs=[
            pl.BlockSpec((half, wide), lambda i: (0, i)),
            pl.BlockSpec((half, wide), lambda i: (0, i)),
            pl.BlockSpec((ENTRIES, TOKENS, wide), lambda i: (0, 0, i)),
        ],
        out_specs=pl.BlockSpec((ENTRIES, wide), lambda i: (0, i)),
        out_shape=shape((ENTRIES, width), F32),
        compiler_params=params(),
        cost_estimate=cost(3),
        name="table_sums",
    )(near, far, sums)


def down_bins_kernel(split_ref, near_ref, far_ref, grad_ref, index_ref, out_ref, activ_ref, wgrad_ref):
    block = split_ref.shape[0]
    half = block // 2
    words, wide = index_ref.shape

    @pl.when(pl.program_id(0) == 0)
    def _():
        for at in range(0, 2 * words, block):
            cols = slice(at, at + block)
            activ = jnp.concatenate([near_ref[:, cols], far_ref[:, cols]], axis=0)
            activ_ref[:, cols] = dot(activ, split_ref[...]).astype(BF16)

    wgrad_ref[...] = dot_tn(activ_ref[...], grad_ref[...]).astype(BF16)
    zero = jnp.zeros((), BF16)
    for lane in range(0, wide, LANES):
        cols = slice(lane, lane + LANES)

        def add_block(i, totals):
            part = [None] * ENTRIES
            for row in range(0, half, 16):
                word = index_ref[pl.ds(pl.multiple_of(i * half + row, 16), 16), cols]
                for entries, offset in ((word & 15, 0), ((word >> 4) & 15, half)):
                    entries = entries.astype(jnp.int16)
                    grads = wgrad_ref[pl.ds(pl.multiple_of(i * block + offset + row, 16), 16), cols]
                    for entry in range(ENTRIES):
                        chosen = jnp.where(entries == jnp.int16(entry), grads, zero)
                        part[entry] = chosen if part[entry] is None else part[entry] + chosen
            done = []
            for entry in range(ENTRIES):
                both = part[entry].astype(F32)
                done.append(totals[entry] + both[:8] + both[8:])
            return tuple(done)

        start = tuple(jnp.zeros((8, LANES), F32) for _ in range(ENTRIES))
        totals = lax.fori_loop(0, 2 * words // block, add_block, start)
        for entry in range(ENTRIES):
            out_ref[entry : entry + 1, cols] = jnp.sum(totals[entry], axis=0, keepdims=True)


def down_bins(split, near, far, grad, index):
    words, width = index.shape
    block = split.shape[0]
    wide = 256
    half = TOKENS // 2
    return pl.pallas_call(
        down_bins_kernel,
        grid=(width // wide,),
        in_specs=[
            whole((block, block)),
            whole((half, 2 * words)),
            whole((half, 2 * words)),
            pl.BlockSpec((TOKENS, wide), lambda i: (0, i)),
            pl.BlockSpec((words, wide), lambda i: (0, i)),
        ],
        out_specs=pl.BlockSpec((ENTRIES, wide), lambda i: (0, i)),
        out_shape=shape((ENTRIES, width), F32),
        scratch_shapes=[pltpu.VMEM((TOKENS, 2 * words), BF16), pltpu.VMEM((2 * words, wide), BF16)],
        compiler_params=params(),
        cost_estimate=cost(8),
        name="down_bins",
    )(split, near, far, grad, index)


def input_grad_kernel(order_ref, merge_ref, gn_ref, gf_ref, un_ref, uf_ref, wg_ref, wu_ref, out_ref):
    gate = jnp.concatenate([gn_ref[...], gf_ref[...]], axis=0)
    up = jnp.concatenate([un_ref[...], uf_ref[...]], axis=0)
    part = (dot_nt(gate, wg_ref[...]) + dot_nt(up, wu_ref[...])).astype(BF16)
    part = dot(order_ref[...], part).astype(BF16)
    out_ref[...] = dot(part, merge_ref[...]).astype(BF16)


def input_grads(order, merge, gate, up, w_gate, w_up):
    rows, width = w_gate.shape
    block = merge.shape[0]
    half = TOKENS // 2
    weights = pl.BlockSpec((block, width), lambda i: (i, 0))
    return pl.pallas_call(
        input_grad_kernel,
        grid=(rows // block,),
        in_specs=[whole((TOKENS, TOKENS)), whole((block, block))] + [whole((half, width))] * 4 + [weights] * 2,
        out_specs=pl.BlockSpec((TOKENS, block), lambda i: (0, i)),
        out_shape=shape((TOKENS, rows), BF16),
        compiler_params=params(),
        cost_estimate=cost(3),
        name="input_grad",
    )(order, merge, *gate, *up, w_gate, w_up)


def inp_pairs(y=0, z=0, core=0):
    return [(i, ((i // 4 + y) % 4) * 4 + ((i // 2 % 2) ^ z) * 2 + ((i % 2) ^ core)) for i in range(16)]


def hid_pairs(z=0, x=0):
    return [(i, ((i // 4 + z) % 4) * 4 + (i % 4 + x) % 4) for i in range(16)]


def send_inp(array, **way):
    return lax.ppermute(array, "inp", inp_pairs(**way))


def send_hid(array, **way):
    return lax.ppermute(array, "hid", hid_pairs(**way))


def total(arrays):
    return functools.reduce(jnp.add, [a.astype(F32) for a in arrays])


def scatter_sum(near, far):
    kept = total([near, send_inp(far, core=1)]).astype(BF16)
    kept = total([kept[:32], send_inp(kept[32:], z=1)]).astype(BF16)
    return total([kept[:8]] + [send_inp(kept[8 * k : 8 * k + 8], y=k) for k in (1, 2, 3)])


def gather_rows(own):
    ring = jnp.concatenate([own] + [send_inp(own, y=-k) for k in (1, 2, 3)], axis=0)
    near = jnp.concatenate([ring, send_inp(ring, z=1)], axis=0)
    return near, send_inp(near, core=1)


def sum_inp(part):
    part = total([part, send_inp(part, core=1)]).astype(BF16)
    part = total([part, send_inp(part, z=1)]).astype(BF16)
    return total([part] + [send_inp(part, y=k) for k in (1, 2, 3)])


def sum_hid(part):
    part = total([part] + [send_hid(part, x=k) for k in (1, 2, 3)]).astype(BF16)
    return total([part] + [send_hid(part, z=k) for k in (1, 2, 3)])


def scatter_sum_hid(part):
    part = total([part[:32]] + [send_hid(part[32 * k : 32 * k + 32], x=k) for k in (1, 2, 3)]).astype(BF16)
    return total([part[:8]] + [send_hid(part[8 * k : 8 * k + 8], z=k) for k in (1, 2, 3)])


def local_hidden(pre_gate, pre_up, hidden_grad):
    sig_gate = jax.nn.sigmoid(pre_gate)
    silu_gate = pre_gate * sig_gate
    activ = (silu_gate * pre_up).astype(BF16)
    gate_grad = (hidden_grad * pre_up * sig_gate * (1.0 + pre_gate * (1.0 - sig_gate))).astype(BF16)
    up_grad = (hidden_grad * silu_gate).astype(BF16)
    return activ, gate_grad, up_grad


def shards(inputs, out_grad, gate_index, up_index, down_index, gate_table, up_table, down_table):
    inp, hid = lax.axis_index("inp"), lax.axis_index("hid")
    row = jnp.arange(TOKENS, dtype=I32)
    piece, within = row // 8, row % 8
    core, z, y = piece // 8, piece // 4 % 2, piece % 4
    inp_device = ((inp // 4 + y) % 4) * 4 + ((inp // 2 % 2) ^ z) * 2 + ((inp % 2) ^ core)
    inp_token = inp_device * 8 + within
    hid_device = ((hid // 4 + piece % 4) % 4) * 4 + (hid % 4 + piece // 4) % 4
    hid_token = hid_device * 8 + within
    to_inp = (inp_token[:, None] == row[None, :]).astype(BF16)
    to_hid = (hid_token[:, None] == inp_token[None, :]).astype(BF16)
    split_wide, split_narrow = split_order(256), split_order(128)

    far_near = forward_down(to_inp, split_narrow.T, out_grad, down_index, down_table)
    hidden_near, hidden_far, grad = far_near
    gate_near, gate_far, w_gate, x = forward_up(to_inp, split_wide, inputs, gate_index, gate_table, True)
    up_near, up_far, w_up = forward_up(None, split_wide, x, up_index, up_table, False)
    hidden_grad = scatter_sum(hidden_near, hidden_far)
    pre_gate = scatter_sum(gate_near, gate_far)
    pre_up = scatter_sum(up_near, up_far)
    activ, gate_grad, up_grad = local_hidden(pre_gate, pre_up, hidden_grad)
    gate_grad, up_grad, activ = gather_rows(gate_grad), gather_rows(up_grad), gather_rows(activ)

    sums = []
    for index in (gate_index, up_index):
        held = None
        for begin, end in ((0, 2), (2, 4), (4, 6), (6, 7)):
            held = entry_sums(x, index, 256, begin, end, held)
        sums.append(held)
    part = input_grads(to_hid, split_wide.T, gate_grad, up_grad, w_gate, w_up)
    input_grad = scatter_sum_hid(part).astype(BF16)
    down_part = down_bins(split_narrow, *activ, grad, down_index)
    down_sum = sum_hid(down_part.astype(BF16))
    table_part = jnp.concatenate([table_sums(*gate_grad, sums[0]), table_sums(*up_grad, sums[1])], axis=0)
    table_sum = sum_inp(table_part.astype(BF16))
    scale = 1.0 / TOKENS
    return input_grad, table_sum[:ENTRIES] * scale, table_sum[ENTRIES:] * scale, down_sum * scale


def solution(mesh):
    in_specs = (
        P(None, "inp"),
        P(None, "inp"),
        P("inp", "hid"),
        P("inp", "hid"),
        P("hid", "inp"),
        P(None, "hid"),
        P(None, "hid"),
        P(None, "inp"),
    )
    out_specs = (P("hid", "inp"), P(None, "hid"), P(None, "hid"), P(None, "inp"))
    return jax.shard_map(shards, mesh=mesh, in_specs=in_specs, out_specs=out_specs, check_vma=False)
```

```python
import functools

import jax
import jax.numpy as jnp
from jax import lax
from jax.experimental import pallas as pl
from jax.experimental.pallas import tpu as pltpu
from jax.sharding import PartitionSpec as P

BF16 = jnp.bfloat16
F32 = jnp.float32
I32 = jnp.int32
ENTRIES = 16
TOKENS = 128
LANES = 128
HBM_BYTES_PER_US = 3_000_000


def params(mib=60):
    return pltpu.CompilerParams(vmem_limit_bytes=mib * 1024 * 1024)


def cost(us):
    return pl.CostEstimate(flops=0, bytes_accessed=int(us * HBM_BYTES_PER_US), transcendentals=0)


def shape(dims, dtype):
    return jax.ShapeDtypeStruct(dims, dtype)


def whole(dims):
    return pl.BlockSpec(dims, lambda i: (0,) * len(dims))


def dot(a, b):
    return jnp.dot(a, b, preferred_element_type=F32)


def dot_nt(a, b):
    return lax.dot_general(a, b, (((1,), (1,)), ((), ())), preferred_element_type=F32)


def dot_tn(a, b):
    return lax.dot_general(a, b, (((0,), (0,)), ((), ())), preferred_element_type=F32)


def iotas(size):
    return lax.broadcasted_iota(I32, (size, size), 0), lax.broadcasted_iota(I32, (size, size), 1)


def one_hot(hits, dtype=BF16):
    return jnp.where(hits, 1.0, 0.0).astype(dtype)


def split_matrix(block):
    source, target = iotas(block)
    half = block // 2
    return one_hot(source == jnp.where(target < half, 2 * target, 2 * (target - half) + 1))


def merge_matrix(block, dtype=BF16):
    source, target = iotas(block)
    half = block // 2
    return one_hot(target == jnp.where(source < half, 2 * source, 2 * (source - half) + 1), dtype)


def token_of(row, core):
    return (((row >> 3) & 7) * 2 + (core ^ (row >> 6))) * 8 + (row & 7)


def to_rows(core):
    row, token = iotas(TOKENS)
    return one_hot(token == token_of(row, core))


def to_owners(core, hid):
    owned, row = iotas(TOKENS)
    bits = ((owned >> 6) & 1) | ((owned >> 4) & 2) | ((owned >> 2) & 4) | (owned & 8)
    return one_hot(token_of(row, core) == (bits ^ hid) * 8 + (owned & 7))


SCALAR = pl.BlockSpec(memory_space=pltpu.SMEM)
ANYWHERE = pl.BlockSpec(memory_space=pl.ANY)


def lookup(low, high, entry):
    at = entry & 7
    from_low = jnp.take_along_axis(low, at, axis=0, mode="promise_in_bounds")
    from_high = jnp.take_along_axis(high, at, axis=0, mode="promise_in_bounds")
    return jnp.where(entry >= 8, from_high, from_low)


def decode_block(index_ref, table_ref, weight_ref):
    words, cols = index_ref.shape

    def tile(j, carry):
        at = pl.ds(pl.multiple_of(j * LANES, LANES), LANES)
        low, high = table_ref[0:8, at], table_ref[8:16, at]
        for row in range(0, words, 16):
            even, odd = [], []
            for part in (row, row + 8):
                word = index_ref[part : part + 8, at]
                even.append(lookup(low, high, word & 15))
                odd.append(lookup(low, high, (word >> 4) & 15))
            weight_ref[row : row + 16, at] = jnp.concatenate(even, axis=0).astype(BF16)
            weight_ref[words + row : words + row + 16, at] = jnp.concatenate(odd, axis=0).astype(BF16)
        return carry

    lax.fori_loop(0, cols // LANES, tile, 0)


def forward_down_kernel(place_ref, grad_ref, index_ref, table_ref, near_ref, far_ref, ordered_ref, weight_ref):
    @pl.when(pl.program_id(0) == 0)
    def _():
        ordered_ref[...] = dot(to_rows(place_ref[0]), grad_ref[...]).astype(BF16)

    decode_block(index_ref, table_ref, weight_ref)
    hidden = dot_nt(ordered_ref[...], weight_ref[...])
    hidden = jnp.dot(
        hidden, merge_matrix(hidden.shape[1], F32), precision=lax.Precision.HIGHEST, preferred_element_type=F32
    )
    near_ref[...] = hidden[: TOKENS // 2]
    far_ref[...] = hidden[TOKENS // 2 :]


def forward_down(place, grad, index, table):
    words, width = index.shape
    block = 256
    half = TOKENS // 2
    return pl.pallas_call(
        forward_down_kernel,
        grid=(pl.cdiv(2 * words, block),),
        in_specs=[
            SCALAR,
            whole((TOKENS, width)),
            pl.BlockSpec((block // 2, width), lambda i: (i, 0)),
            whole((ENTRIES, width)),
        ],
        out_specs=[
            pl.BlockSpec((half, block), lambda i: (0, i)),
            pl.BlockSpec((half, block), lambda i: (0, i)),
            whole((TOKENS, width)),
        ],
        out_shape=[
            shape((half, 2 * words), F32),
            shape((half, 2 * words), F32),
            shape((TOKENS, width), BF16),
        ],
        scratch_shapes=[pltpu.VMEM((block, width), BF16)],
        compiler_params=params(),
        cost_estimate=cost(5),
        name="forward_down",
    )(place, grad, index, table)


def forward_up_kernel(first, *refs):
    if first:
        place_ref, x_ref, index_ref, table_ref, near_ref, far_ref, weight_ref, ordered_ref, sum_ref = refs
        x = dot(to_rows(place_ref[0]), x_ref[...]).astype(BF16)
        x = dot(x, split_matrix(x.shape[1])).astype(BF16)
        ordered_ref[...] = x
    else:
        x_ref, index_ref, table_ref, near_ref, far_ref, weight_ref, sum_ref = refs
        x = x_ref[...]
    decode_block(index_ref, table_ref, weight_ref)
    step = pl.program_id(0)

    @pl.when(step == 0)
    def _():
        sum_ref[...] = jnp.zeros_like(sum_ref)

    sum_ref[...] += dot(x, weight_ref[...])

    @pl.when(step == pl.num_programs(0) - 1)
    def _():
        near_ref[...] = sum_ref[: TOKENS // 2, :]
        far_ref[...] = sum_ref[TOKENS // 2 :, :]


def forward_up(place, x, index, table):
    first = place is not None
    words, width = index.shape
    block = 256
    half = TOKENS // 2
    by_column = pl.BlockSpec((TOKENS, block), lambda i: (0, i))
    return pl.pallas_call(
        functools.partial(forward_up_kernel, first),
        grid=(2 * words // block,),
        in_specs=[SCALAR] * first
        + [by_column, pl.BlockSpec((block // 2, width), lambda i: (i, 0)), whole((ENTRIES, width))],
        out_specs=[whole((half, width)), whole((half, width)), pl.BlockSpec((block, width), lambda i: (i, 0))]
        + [by_column] * first,
        out_shape=[shape((half, width), F32), shape((half, width), F32), shape((2 * words, width), BF16)]
        + [shape((TOKENS, 2 * words), BF16)] * first,
        scratch_shapes=[pltpu.VMEM((TOKENS, width), F32)],
        compiler_params=params(),
        cost_estimate=cost(5),
        name="forward_gate" if first else "forward_up",
    )(*([place] * first + [x, index, table]))


def entry_sums_kernel(x_ref, index_ref, after_ref, out_ref, entry_ref):
    words = index_ref.shape[0]
    half = 128
    for row in range(0, words, 16):
        word = index_ref[row : row + 16, :]
        at = row // half * 2 * half + row % half
        entry_ref[at : at + 16, :] = (word & 15).astype(jnp.int16)
        entry_ref[at + half : at + half + 16, :] = ((word >> 4) & 15).astype(jnp.int16)
    one, zero = jnp.ones((), BF16), jnp.zeros((), BF16)
    for entry in range(ENTRIES):
        chosen = jnp.where(entry_ref[...] == jnp.int16(entry), one, zero)
        out_ref[entry] = dot(x_ref[...], chosen).astype(BF16)


def entry_sums(x, index, after):
    words, width = index.shape
    wide = 256
    return pl.pallas_call(
        entry_sums_kernel,
        grid=(pl.cdiv(width, wide),),
        in_specs=[whole((TOKENS, 2 * words)), pl.BlockSpec((words, wide), lambda i: (0, i)), ANYWHERE],
        out_specs=pl.BlockSpec((ENTRIES, TOKENS, wide), lambda i: (0, 0, i)),
        out_shape=shape((ENTRIES, TOKENS, width), BF16),
        scratch_shapes=[pltpu.VMEM((2 * words, wide), jnp.int16)],
        compiler_params=params(),
        cost_estimate=cost(11),
        name="entry_sums",
    )(x, index, after)


def table_sums_kernel(near_ref, far_ref, sums_ref, after_ref, out_ref, grad_ref):
    entry = pl.program_id(0)

    @pl.when(entry == 0)
    def _():
        grad_ref[: TOKENS // 2, :] = near_ref[...].astype(F32)
        grad_ref[TOKENS // 2 :, :] = far_ref[...].astype(F32)

    product = sums_ref[0].astype(F32) * grad_ref[...]
    out_ref[pl.ds(entry, 1), :] = jnp.sum(product, axis=0, keepdims=True)


def table_sums(near, far, part, sums, after):
    width = sums.shape[2]
    half = TOKENS // 2
    return pl.pallas_call(
        table_sums_kernel,
        grid=(ENTRIES,),
        in_specs=[
            pl.BlockSpec((half, width), lambda i: (0, part)),
            pl.BlockSpec((half, width), lambda i: (0, part)),
            pl.BlockSpec((1, TOKENS, width), lambda i: (i, 0, 0)),
            ANYWHERE,
        ],
        out_specs=whole((ENTRIES, width)),
        out_shape=shape((ENTRIES, width), F32),
        scratch_shapes=[pltpu.VMEM((TOKENS, width), F32)],
        compiler_params=params(),
        cost_estimate=cost(3),
        name="table_sums",
    )(near, far, sums, after)


def down_bins_kernel(near_ref, far_ref, grad_ref, index_ref, out_ref, activ_ref, wgrad_ref):
    block = 128
    half = block // 2
    words, wide = index_ref.shape

    @pl.when(pl.program_id(0) == 0)
    def _():
        for at in range(0, 2 * words, block):
            cols = slice(at, at + block)
            activ = jnp.concatenate([near_ref[:, cols], far_ref[:, cols]], axis=0)
            activ_ref[:, cols] = dot(activ, split_matrix(block)).astype(BF16)

    wgrad_ref[...] = dot_tn(activ_ref[...], grad_ref[...]).astype(BF16)
    zero = jnp.zeros((), BF16)
    for lane in range(0, wide, LANES):
        cols = slice(lane, lane + LANES)

        def add_block(i, totals):
            part = [None] * ENTRIES
            for row in range(0, half, 16):
                word = index_ref[pl.ds(pl.multiple_of(i * half + row, 16), 16), cols]
                for entries, offset in ((word & 15, 0), ((word >> 4) & 15, half)):
                    entries = entries.astype(jnp.int16)
                    grads = wgrad_ref[pl.ds(pl.multiple_of(i * block + offset + row, 16), 16), cols]
                    for entry in range(ENTRIES):
                        chosen = jnp.where(entries == jnp.int16(entry), grads, zero)
                        part[entry] = chosen if part[entry] is None else part[entry] + chosen
            done = []
            for entry in range(ENTRIES):
                both = part[entry].astype(F32)
                done.append(totals[entry] + both[:8] + both[8:])
            return tuple(done)

        start = tuple(jnp.zeros((8, LANES), F32) for _ in range(ENTRIES))
        totals = lax.fori_loop(0, 2 * words // block, add_block, start)
        for entry in range(ENTRIES):
            out_ref[entry : entry + 1, cols] = jnp.sum(totals[entry], axis=0, keepdims=True)


def down_bins(near, far, part, grad, index):
    words, width = index.shape
    wide = 256
    half = TOKENS // 2
    return pl.pallas_call(
        down_bins_kernel,
        grid=(width // wide,),
        in_specs=[
            pl.BlockSpec((half, 2 * words), lambda i: (0, part)),
            pl.BlockSpec((half, 2 * words), lambda i: (0, part)),
            pl.BlockSpec((TOKENS, wide), lambda i: (0, i)),
            pl.BlockSpec((words, wide), lambda i: (0, i)),
        ],
        out_specs=pl.BlockSpec((ENTRIES, wide), lambda i: (0, i)),
        out_shape=shape((ENTRIES, width), F32),
        scratch_shapes=[pltpu.VMEM((TOKENS, 2 * words), BF16), pltpu.VMEM((2 * words, wide), BF16)],
        compiler_params=params(),
        cost_estimate=cost(10),
        name="down_bins",
    )(near, far, grad, index)


def input_grad_kernel(place_ref, gn_ref, gf_ref, un_ref, uf_ref, wg_ref, wu_ref, after_ref, out_ref):
    gate = jnp.concatenate([gn_ref[...], gf_ref[...]], axis=0)
    up = jnp.concatenate([un_ref[...], uf_ref[...]], axis=0)
    part = (dot_nt(gate, wg_ref[...]) + dot_nt(up, wu_ref[...])).astype(BF16)
    part = dot(to_owners(place_ref[0], place_ref[1]), part).astype(BF16)
    out_ref[...] = dot(part, merge_matrix(part.shape[1])).astype(BF16)


def input_grads(place, near, far, w_gate, w_up, after):
    rows, width = w_gate.shape
    block = 256
    half = TOKENS // 2
    gate = pl.BlockSpec((half, width), lambda i: (0, 0))
    up = pl.BlockSpec((half, width), lambda i: (0, 1))
    weights = pl.BlockSpec((block, width), lambda i: (i, 0))
    return pl.pallas_call(
        input_grad_kernel,
        grid=(rows // block,),
        in_specs=[SCALAR, gate, gate, up, up, weights, weights, ANYWHERE],
        out_specs=pl.BlockSpec((TOKENS, block), lambda i: (0, i)),
        out_shape=shape((TOKENS, rows), BF16),
        compiler_params=params(),
        cost_estimate=cost(3.5),
        name="input_grad",
    )(place, near, far, near, far, w_gate, w_up, after)


ONE_CORE = [[2 * place + core for place in range(8)] for core in range(2)]


def other_core(array):
    return lax.ppermute(array, "inp", [(i, i ^ 1) for i in range(16)])


def exchange_inp(pieces):
    return lax.all_to_all(pieces, "inp", 0, 0, tiled=True, axis_index_groups=ONE_CORE)


def copies(array, count):
    return jnp.broadcast_to(array[None], (count,) + array.shape)


def total(arrays):
    return functools.reduce(jnp.add, [a.astype(F32) for a in arrays])


def sum_inp(gate, up, core):
    own = jnp.where(core == 0, gate, up) + other_core(jnp.where(core == 0, up, gate))
    own = total(exchange_inp(copies(own.astype(BF16), 8)))
    other = other_core(own)
    return jnp.where(core == 0, own, other), jnp.where(core == 0, other, own)


def hid_step(bit, rows, bins):
    half = rows.shape[0] // 2
    coarse = lax.reduce_precision(bins, 8, 7)
    sent = jnp.concatenate([rows[half:].astype(BF16), coarse.astype(BF16), (bins - coarse).astype(BF16)], axis=0)
    back = lax.ppermute(sent, "hid", [(i, i ^ bit) for i in range(16)]).astype(F32)
    bins = bins + (back[half : half + ENTRIES] + back[half + ENTRIES :])
    return rows[:half].astype(F32) + back[:half], bins


def local_hidden(pre_gate, pre_up, hidden_grad):
    sig_gate = jax.nn.sigmoid(pre_gate)
    silu_gate = pre_gate * sig_gate
    activ = (silu_gate * pre_up).astype(BF16)
    gate_grad = (hidden_grad * pre_up * sig_gate * (1.0 + pre_gate * (1.0 - sig_gate))).astype(BF16)
    up_grad = (hidden_grad * silu_gate).astype(BF16)
    return activ, gate_grad, up_grad


def shards(inputs, out_grad, gate_index, up_index, down_index, gate_table, up_table, down_table):
    width = gate_index.shape[1]
    core = lax.axis_index("inp") % 2
    place = jnp.stack([core, lax.axis_index("hid")]).astype(I32)

    hidden_near, hidden_far, grad = forward_down(place, out_grad, down_index, down_table)
    hidden_back = other_core(hidden_far)
    gate_near, gate_far, w_gate, x = forward_up(place, inputs, gate_index, gate_table)
    gate_back = other_core(gate_far)
    up_near, up_far, w_up = forward_up(None, x, up_index, up_table)
    up_back = other_core(up_far)
    pair_sums = jnp.concatenate(
        [(gate_near + gate_back).astype(BF16), (up_near + up_back).astype(BF16), (hidden_near + hidden_back).astype(BF16)],
        axis=1,
    ).reshape(8, 8, 3 * width)
    pieces = exchange_inp(pair_sums)
    gate_sums = entry_sums(x, gate_index, pair_sums)
    pieces, gate_sums = lax.optimization_barrier((pieces, gate_sums))
    pre = total(pieces)
    activ, gate_grad, up_grad = local_hidden(pre[:, :width], pre[:, width : 2 * width], pre[:, 2 * width :])
    grads = copies(jnp.concatenate([gate_grad, up_grad, activ], axis=1), 8)
    near = exchange_inp(grads)
    up_sums = entry_sums(x, up_index, grads)
    near, up_sums = lax.optimization_barrier((near, up_sums))
    near = near.reshape(TOKENS // 2, 3 * width)
    activ_near, grad_near = near[:, 2 * width :], near[:, : 2 * width]
    activ_far, grad_far = other_core(activ_near), other_core(grad_near)

    down_sum = down_bins(activ_near, activ_far, 0, grad, down_index)
    part = input_grads(place, grad_near, grad_far, w_gate, w_up, down_sum)
    gate_part = table_sums(grad_near, grad_far, 0, gate_sums, part)
    part, down_sum = hid_step(1, part, down_sum)
    up_part = table_sums(grad_near, grad_far, 1, up_sums, part)
    gate_sum, up_sum = sum_inp(gate_part, up_part, core)
    for bit in (2, 4, 8):
        part, down_sum = hid_step(bit, part, down_sum)
    input_grad = part.astype(BF16)
    scale = 1.0 / TOKENS
    return input_grad, gate_sum * scale, up_sum * scale, down_sum * scale


def solution(mesh):
    in_specs = (
        P(None, "inp"),
        P(None, "inp"),
        P("inp", "hid"),
        P("inp", "hid"),
        P("hid", "inp"),
        P(None, "hid"),
        P(None, "hid"),
        P(None, "inp"),
    )
    out_specs = (P("hid", "inp"), P(None, "hid"), P(None, "hid"), P(None, "inp"))
    return jax.shard_map(shards, mesh=mesh, in_specs=in_specs, out_specs=out_specs, check_vma=False)
```

```python
import functools

import jax
import jax.numpy as jnp
from jax import lax
from jax.experimental import pallas as pl
from jax.experimental.pallas import tpu as pltpu
from jax.sharding import PartitionSpec as P

BF16 = jnp.bfloat16
F32 = jnp.float32
I32 = jnp.int32
ENTRIES = 16
TOKENS = 128
LANES = 128
HBM_BYTES_PER_US = 3_000_000


def params(mib=16):
    return pltpu.CompilerParams(vmem_limit_bytes=mib * 1024 * 1024)


def cost(us):
    return pl.CostEstimate(flops=0, bytes_accessed=int(us * HBM_BYTES_PER_US), transcendentals=0)


def shape(dims, dtype):
    return jax.ShapeDtypeStruct(dims, dtype)


def dot(a, b):
    return jnp.dot(a, b, preferred_element_type=F32)


def dot_nt(a, b):
    return lax.dot_general(a, b, (((1,), (1,)), ((), ())), preferred_element_type=F32)


def dot_tn(a, b):
    return lax.dot_general(a, b, (((0,), (0,)), ((), ())), preferred_element_type=F32)


def iotas(size):
    return lax.broadcasted_iota(I32, (size, size), 0), lax.broadcasted_iota(I32, (size, size), 1)


def one_hot(hits, dtype=BF16):
    return jnp.where(hits, 1.0, 0.0).astype(dtype)


def split_matrix(block):
    source, target = iotas(block)
    half = block // 2
    return one_hot(source == jnp.where(target < half, 2 * target, 2 * (target - half) + 1))


def merge_matrix(block, dtype=BF16):
    source, target = iotas(block)
    half = block // 2
    return one_hot(target == jnp.where(source < half, 2 * source, 2 * (source - half) + 1), dtype)


def token_of(row, core):
    return (((row >> 3) & 7) * 2 + (core ^ (row >> 6))) * 8 + (row & 7)


def to_rows(core):
    row, token = iotas(TOKENS)
    return one_hot(token == token_of(row, core))


def to_owners(core, hid):
    owned, row = iotas(TOKENS)
    bits = ((owned >> 6) & 1) | ((owned >> 4) & 2) | ((owned >> 2) & 4) | (owned & 8)
    return one_hot(token_of(row, core) == (bits ^ hid) * 8 + (owned & 7))


SCALAR = pl.BlockSpec(memory_space=pltpu.SMEM)
ANYWHERE = pl.BlockSpec(memory_space=pl.ANY)
IN_HBM = pl.BlockSpec(memory_space=pltpu.HBM)
IN_VMEM = pl.BlockSpec(memory_space=pltpu.VMEM)
WIDE = 256
HALF = TOKENS // 2


def lookup(low, high, at, is_high):
    from_low = jnp.take_along_axis(low, at, axis=0, mode="promise_in_bounds")
    from_high = jnp.take_along_axis(high, at, axis=0, mode="promise_in_bounds")
    return jnp.where(is_high, from_high, from_low)


def decode_rows(index_ref, table_ref, weight_ref, begin, words):
    def tile(j, carry):
        cols = pl.ds(pl.multiple_of(j * LANES, LANES), LANES)
        low, high = table_ref[0:8, cols], table_ref[8:16, cols]
        for row in range(0, words, 16):
            even, odd = [], []
            for part in (row, row + 8):
                word = index_ref[begin + part : begin + part + 8, cols]
                even.append(lookup(low, high, word & 7, (word & 8) != 0))
                odd.append(lookup(low, high, (word >> 4) & 7, (word & 128) != 0))
            weight_ref[row : row + 16, cols] = jnp.concatenate(even, axis=0).astype(BF16)
            weight_ref[words + row : words + row + 16, cols] = jnp.concatenate(odd, axis=0).astype(BF16)
        return carry

    lax.fori_loop(0, index_ref.shape[1] // LANES, tile, 0)


def blocks_of(size, block):
    return [(at, min(block, size - at)) for at in range(0, size, block)]


def row_copies(from_ref, to_ref, sems, block):
    return [
        pltpu.make_async_copy(from_ref.at[pl.ds(at, rows)], to_ref.at[pl.ds(at, rows)], sems.at[i])
        for i, (at, rows) in enumerate(blocks_of(from_ref.shape[0], block))
    ]


def in_hbm(*arrays):
    return [pltpu.with_memory_space_constraint(each, pltpu.HBM) for each in arrays]


def start_all(copies):
    for each in copies:
        each.start()


def wait_all(copies):
    for each in copies:
        each.wait()


def forward_down_kernel(
    place_ref, raw_hbm, table_hbm, index_hbm, next_hbm, near_ref, far_ref, ordered_hbm, *refs
):
    count = len(next_hbm)
    next_refs = refs[:count]
    raw_ref, table_ref, index_ref, ordered_ref, weight_ref, sems, next_sems, sem = refs[count:]
    words = index_ref.shape[0]
    loads = row_copies(index_hbm, index_ref, sems, LANES)
    small = [pltpu.make_async_copy(raw_hbm, raw_ref, next_sems.at[count])]
    small.append(pltpu.make_async_copy(table_hbm, table_ref, next_sems.at[count + 1]))
    later = [pltpu.make_async_copy(a, b, next_sems.at[i]) for i, (a, b) in enumerate(zip(next_hbm, next_refs))]
    start_all(small + loads + later)
    wait_all(small)
    ordered_ref[...] = dot(to_rows(place_ref[0]), raw_ref[...]).astype(BF16)
    store = pltpu.make_async_copy(ordered_ref, ordered_hbm, sem)
    store.start()
    for load, (at, rows) in zip(loads, blocks_of(words, LANES)):
        load.wait()
        decode_rows(index_ref, table_ref, weight_ref, at, rows)
        hidden = dot_nt(ordered_ref[...], weight_ref[: 2 * rows, :])
        hidden = jnp.dot(hidden, merge_matrix(2 * rows, F32), precision=lax.Precision.HIGHEST, preferred_element_type=F32)
        near_ref[:, 2 * at : 2 * (at + rows)] = hidden[:HALF]
        far_ref[:, 2 * at : 2 * (at + rows)] = hidden[HALF:]
    store.wait()
    wait_all(later)


def forward_down(place, grad, table, index, brought):
    words, width = index.shape
    count = len(brought)

    def kernel(*refs):
        forward_down_kernel(*refs[:4], refs[4 : 4 + count], *refs[4 + count :])

    return pl.pallas_call(
        kernel,
        in_specs=[SCALAR] + [IN_HBM] * (3 + count),
        out_specs=[IN_VMEM, IN_VMEM, IN_HBM] + [IN_VMEM] * count,
        out_shape=[
            pltpu.VMEM((HALF, 2 * words), F32),
            pltpu.VMEM((HALF, 2 * words), F32),
            pltpu.HBM((TOKENS, width), BF16),
        ]
        + [pltpu.VMEM(each.shape, each.dtype) for each in brought],
        scratch_shapes=[
            pltpu.VMEM(grad.shape, BF16),
            pltpu.VMEM(table.shape, F32),
            pltpu.VMEM(index.shape, I32),
            pltpu.VMEM((TOKENS, width), BF16),
            pltpu.VMEM((WIDE, width), BF16),
            pltpu.SemaphoreType.DMA((pl.cdiv(words, LANES),)),
            pltpu.SemaphoreType.DMA((count + 2,)),
            pltpu.SemaphoreType.DMA,
        ],
        compiler_params=params(),
        cost_estimate=cost(5),
        name="forward_down",
    )(place, *in_hbm(grad, table, index, *brought))


def forward_up_kernel(first, *refs):
    if first:
        place_ref, raw_ref, index_ref, table_ref, next_hbm, near_ref, far_ref, weight_hbm = refs[:8]
        x_ref, x_hbm, next_ref, weight_ref, sems, next_sems = refs[8:]
        later = [pltpu.make_async_copy(next_hbm, next_ref, next_sems.at[0])]
        start_all(later)
        x = dot(to_rows(place_ref[0]), raw_ref[...]).astype(BF16)
        for at in range(0, x.shape[1], WIDE):
            x_ref[:, at : at + WIDE] = dot(x[:, at : at + WIDE], split_matrix(WIDE)).astype(BF16)
        later.append(pltpu.make_async_copy(x_ref, x_hbm, next_sems.at[1]))
        start_all(later[1:])
    else:
        x_ref, index_ref, table_ref, near_ref, far_ref, weight_hbm, weight_ref, sems = refs
        later = []
    stores = row_copies(weight_ref, weight_hbm, sems, WIDE)
    for store, at in zip(stores, range(0, index_ref.shape[0], LANES)):
        decode_rows(index_ref, table_ref, weight_ref.at[pl.ds(2 * at, WIDE)], at, LANES)
        store.start()
    for at, cols in blocks_of(index_ref.shape[1], WIDE):
        sums = dot(x_ref[...], weight_ref[:, at : at + cols])
        near_ref[:, at : at + cols] = sums[:HALF]
        far_ref[:, at : at + cols] = sums[HALF:]
    wait_all(stores + later)


def forward_up(place, x, index, table, later_index):
    first = place is not None
    words, width = index.shape
    ordered = (TOKENS, 2 * words)
    return pl.pallas_call(
        functools.partial(forward_up_kernel, first),
        in_specs=[SCALAR] * first + [IN_VMEM] * 3 + [IN_HBM] * first,
        out_specs=[IN_VMEM, IN_VMEM, IN_HBM] + [IN_VMEM, IN_HBM, IN_VMEM] * first,
        out_shape=[
            pltpu.VMEM((HALF, width), F32),
            pltpu.VMEM((HALF, width), F32),
            pltpu.HBM((2 * words, width), BF16),
        ]
        + [pltpu.VMEM(ordered, BF16), pltpu.HBM(ordered, BF16), pltpu.VMEM((words, width), I32)] * first,
        scratch_shapes=[pltpu.VMEM((2 * words, width), BF16), pltpu.SemaphoreType.DMA((2 * words // WIDE,))]
        + [pltpu.SemaphoreType.DMA((2,))] * first,
        compiler_params=params(),
        cost_estimate=cost(5),
        name="forward_gate" if first else "forward_up",
    )(*([place] * first + [x, index, table] + in_hbm(*[later_index] * first)))


def entry_sums_kernel(x_ref, index_ref, after_ref, out_ref, entry_ref):
    words = index_ref.shape[0]
    for row in range(0, words, 16):
        word = index_ref[row : row + 16, :]
        to = row // LANES * WIDE + row % LANES
        entry_ref[to : to + 16, :] = (word & 15).astype(jnp.int16)
        entry_ref[to + LANES : to + LANES + 16, :] = ((word >> 4) & 15).astype(jnp.int16)
    one, zero = jnp.ones((), BF16), jnp.zeros((), BF16)
    for entry in range(ENTRIES):
        chosen = jnp.where(entry_ref[...] == jnp.int16(entry), one, zero)
        out_ref[entry] = dot(x_ref[...], chosen).astype(BF16)


def entry_sums(x, index, after):
    words, width = index.shape
    return pl.pallas_call(
        entry_sums_kernel,
        grid=(pl.cdiv(width, WIDE),),
        in_specs=[
            pl.BlockSpec((TOKENS, 2 * words), lambda i: (0, 0)),
            pl.BlockSpec((words, WIDE), lambda i: (0, i)),
            ANYWHERE,
        ],
        out_specs=pl.BlockSpec((ENTRIES, TOKENS, WIDE), lambda i: (0, 0, i)),
        out_shape=shape((ENTRIES, TOKENS, width), BF16),
        scratch_shapes=[pltpu.VMEM((2 * words, WIDE), jnp.int16)],
        compiler_params=params(60),
        cost_estimate=cost(11),
        name="entry_sums",
    )(x, index, after)


def table_sums_kernel(part, near_ref, far_ref, sums_hbm, after_ref, out_ref, grad_ref, sums_ref, sems):
    count = ENTRIES // sems.shape[0]
    loads = row_copies(sums_hbm, sums_ref, sems, count)
    start_all(loads)
    width = sums_ref.shape[2]
    grad_ref[:HALF, :] = near_ref[:, part * width : (part + 1) * width].astype(F32)
    grad_ref[HALF:, :] = far_ref[:, part * width : (part + 1) * width].astype(F32)
    for load, begin in zip(loads, range(0, ENTRIES, count)):
        load.wait()

        def tile(j, carry, begin=begin):
            cols = pl.ds(pl.multiple_of(j * LANES, LANES), LANES)
            rows = []
            for entry in range(begin, begin + count):
                acc = None
                for row in range(0, TOKENS, 16):
                    product = sums_ref[entry, row : row + 16, cols].astype(F32) * grad_ref[row : row + 16, cols]
                    acc = product if acc is None else acc + product
                rows.append(jnp.sum(acc, axis=0, keepdims=True))
            out_ref[begin : begin + count, cols] = jnp.concatenate(rows, axis=0)
            return carry

        lax.fori_loop(0, width // LANES, tile, 0)


def table_sums(near, far, part, sums, after):
    width = sums.shape[2]
    return pl.pallas_call(
        functools.partial(table_sums_kernel, part),
        in_specs=[IN_VMEM, IN_VMEM, IN_HBM, ANYWHERE],
        out_specs=IN_VMEM,
        out_shape=pltpu.VMEM((ENTRIES, width), F32),
        scratch_shapes=[
            pltpu.VMEM((TOKENS, width), F32),
            pltpu.VMEM(sums.shape, BF16),
            pltpu.SemaphoreType.DMA((4,)),
        ],
        compiler_params=params(),
        cost_estimate=cost(4.5),
        name="table_sums",
    )(near, far, *in_hbm(sums), after)


def down_bins_kernel(near_ref, far_ref, grad_hbm, index_hbm, next_hbm, out_ref, next_refs, *scratch):
    grad_ref, index_ref, activ_ref, wgrad_ref, sems = scratch
    loads = [pltpu.make_async_copy(grad_hbm, grad_ref, sems.at[0])]
    loads.append(pltpu.make_async_copy(index_hbm, index_ref, sems.at[1]))
    loads += [pltpu.make_async_copy(a, b, sems.at[2 + i]) for i, (a, b) in enumerate(zip(next_hbm, next_refs))]
    start_all(loads)
    block = LANES
    half = block // 2
    words, width = index_ref.shape
    split = split_matrix(block)
    for at in range(0, 2 * words, block):
        cols = slice(at, at + block)
        activ = jnp.concatenate([near_ref[:, cols], far_ref[:, cols]], axis=0)
        activ_ref[:, cols] = dot(activ, split).astype(BF16)
    wait_all(loads[:1])
    for at in range(0, width, WIDE):
        wgrad_ref[:, at : at + WIDE] = dot_tn(activ_ref[...], grad_ref[:, at : at + WIDE]).astype(BF16)
    wait_all(loads[1:2])
    zero = jnp.zeros((), BF16)

    def lanes(j, carry):
        cols = pl.ds(pl.multiple_of(j * LANES, LANES), LANES)

        def add_block(i, totals):
            part = [None] * ENTRIES
            for row in range(0, half, 16):
                word = index_ref[pl.ds(pl.multiple_of(i * half + row, 16), 16), cols].astype(jnp.int16)
                for entries, offset in ((word & 15, 0), ((word >> 4) & 15, half)):
                    grads = wgrad_ref[pl.ds(pl.multiple_of(i * block + offset + row, 16), 16), cols]
                    for entry in range(ENTRIES):
                        chosen = jnp.where(entries == jnp.int16(entry), grads, zero)
                        part[entry] = chosen if part[entry] is None else part[entry] + chosen
            done = []
            for entry in range(ENTRIES):
                both = part[entry].astype(F32)
                done.append(totals[entry] + both[:8] + both[8:])
            return tuple(done)

        start = tuple(jnp.zeros((8, LANES), F32) for _ in range(ENTRIES))
        totals = lax.fori_loop(0, 2 * words // block, add_block, start)
        out_ref[:, cols] = jnp.concatenate([jnp.sum(each, axis=0, keepdims=True) for each in totals], axis=0)
        return carry

    lax.fori_loop(0, width // LANES, lanes, 0)
    wait_all(loads[2:])


def down_bins(near, far, grad, index, brought):
    words, width = index.shape
    count = len(brought)

    def kernel(*refs):
        out = 4 + count
        down_bins_kernel(*refs[:4], refs[4:out], refs[out], refs[out + 1 : out + 1 + count], *refs[out + 1 + count :])

    return pl.pallas_call(
        kernel,
        in_specs=[IN_VMEM] * 2 + [IN_HBM] * (2 + count),
        out_specs=[IN_VMEM] * (1 + count),
        out_shape=[pltpu.VMEM((ENTRIES, width), F32)] + [pltpu.VMEM(each.shape, each.dtype) for each in brought],
        scratch_shapes=[
            pltpu.VMEM((TOKENS, width), BF16),
            pltpu.VMEM((words, width), I32),
            pltpu.VMEM((TOKENS, 2 * words), BF16),
            pltpu.VMEM((2 * words, width), BF16),
            pltpu.SemaphoreType.DMA((2 + count,)),
        ],
        compiler_params=params(),
        cost_estimate=cost(10),
        name="down_bins",
    )(near, far, *in_hbm(grad, index, *brought))


def put_bins(bins, sent_ref):
    coarse = bins.astype(BF16)
    sent_ref[:ENTRIES] = coarse
    sent_ref[ENTRIES : 2 * ENTRIES] = (bins - coarse.astype(F32)).astype(BF16)


def input_grad_kernel(
    place_ref, near_ref, far_ref, wg_ref, wu_ref, bins_ref, kept_ref, sent_ref
):
    rows, width = wg_ref.shape
    gate = jnp.concatenate([near_ref[:, :width], far_ref[:, :width]], axis=0)
    up = jnp.concatenate([near_ref[:, width:], far_ref[:, width:]], axis=0)
    order = to_owners(place_ref[0], place_ref[1])
    merge = merge_matrix(WIDE)
    for at in range(0, rows, WIDE):
        part = (dot_nt(gate, wg_ref[at : at + WIDE, :]) + dot_nt(up, wu_ref[at : at + WIDE, :])).astype(BF16)
        part = dot(dot(order, part).astype(BF16), merge)
        kept_ref[:, at : at + WIDE] = part[:HALF]
        sent_ref[2 * ENTRIES :, at : at + WIDE] = part[HALF:].astype(BF16)
    put_bins(bins_ref[...], sent_ref)


def input_grads(place, near, far, w_gate, w_up, bins):
    width = w_gate.shape[0]
    return pl.pallas_call(
        input_grad_kernel,
        in_specs=[SCALAR] + [IN_VMEM] * 5,
        out_specs=[IN_VMEM] * 2,
        out_shape=[pltpu.VMEM((HALF, width), F32), pltpu.VMEM((2 * ENTRIES + HALF, width), BF16)],
        compiler_params=params(),
        cost_estimate=cost(3.5),
        name="input_grad",
    )(place, near, far, w_gate, w_up, bins)


def add_received_kernel(kept_ref, bins_ref, back_ref, rows_ref, sums_ref, sent_ref):
    bins = bins_ref[...] + (back_ref[:ENTRIES].astype(F32) + back_ref[ENTRIES : 2 * ENTRIES].astype(F32))
    rows = kept_ref[...] + back_ref[2 * ENTRIES :].astype(F32)
    rows_ref[...] = rows[: rows_ref.shape[0]]
    sums_ref[...] = bins
    put_bins(bins, sent_ref)
    sent_ref[2 * ENTRIES :] = rows[rows.shape[0] - sent_ref.shape[0] + 2 * ENTRIES :].astype(BF16)


def add_received(kept, bins, back):
    rows, width = kept.shape
    half = max(rows // 2, 16)
    return pl.pallas_call(
        add_received_kernel,
        in_specs=[IN_VMEM] * 3,
        out_specs=[IN_VMEM] * 3,
        out_shape=[
            pltpu.VMEM((half, width), F32),
            pltpu.VMEM(bins.shape, F32),
            pltpu.VMEM((2 * ENTRIES + half, width), BF16),
        ],
        compiler_params=params(),
        cost_estimate=cost(0.7),
        name="add_received",
    )(kept, bins, back)


ONE_CORE = [[2 * place + core for place in range(8)] for core in range(2)]


def other_core(array):
    return lax.ppermute(array, "inp", [(i, i ^ 1) for i in range(16)])


def exchange_inp(pieces):
    return lax.all_to_all(pieces, "inp", 0, 0, tiled=True, axis_index_groups=ONE_CORE)


def copies(array, count):
    return jnp.broadcast_to(array[None], (count,) + array.shape)


def total(arrays):
    return functools.reduce(jnp.add, [a.astype(F32) for a in arrays])


def sum_inp(gate, up, core):
    own = jnp.where(core == 0, gate, up) + other_core(jnp.where(core == 0, up, gate))
    own = total(exchange_inp(copies(own.astype(BF16), 8)))
    other = other_core(own)
    return jnp.where(core == 0, own, other), jnp.where(core == 0, other, own)


def other_hid(array, bit):
    return lax.ppermute(array, "hid", [(i, i ^ bit) for i in range(16)])


def local_hidden(pre_gate, pre_up, hidden_grad):
    sig_gate = jax.nn.sigmoid(pre_gate)
    silu_gate = pre_gate * sig_gate
    activ = (silu_gate * pre_up).astype(BF16)
    gate_grad = (hidden_grad * pre_up * sig_gate * (1.0 + pre_gate * (1.0 - sig_gate))).astype(BF16)
    up_grad = (hidden_grad * silu_gate).astype(BF16)
    return activ, gate_grad, up_grad


def shards(inputs, out_grad, gate_index, up_index, down_index, gate_table, up_table, down_table):
    width = gate_index.shape[1]
    core = lax.axis_index("inp") % 2
    place = jnp.stack([core, lax.axis_index("hid")]).astype(I32)

    hidden_near, hidden_far, grad, x, gate_words, gate_lookup, up_lookup = forward_down(
        place, out_grad, down_table, down_index, (inputs, gate_index, gate_table, up_table)
    )
    hidden_back = other_core(hidden_far)
    gate_near, gate_far, w_gate, x_near, x, up_words = forward_up(place, x, gate_words, gate_lookup, up_index)
    gate_back = other_core(gate_far)
    up_near, up_far, w_up = forward_up(None, x_near, up_words, up_lookup, None)
    up_back = other_core(up_far)
    pair_sums = jnp.concatenate(
        [(gate_near + gate_back).astype(BF16), (up_near + up_back).astype(BF16), (hidden_near + hidden_back).astype(BF16)],
        axis=1,
    ).reshape(8, 8, 3 * width)
    pieces = exchange_inp(pair_sums)
    gate_sums = entry_sums(x, gate_index, pair_sums)
    pieces, gate_sums = lax.optimization_barrier((pieces, gate_sums))
    pre = total(pieces)
    activ, gate_grad, up_grad = local_hidden(pre[:, :width], pre[:, width : 2 * width], pre[:, 2 * width :])
    grads = copies(jnp.concatenate([gate_grad, up_grad, activ], axis=1), 8)
    near = exchange_inp(grads)
    up_sums = entry_sums(x, up_index, grads)
    near, up_sums = lax.optimization_barrier((near, up_sums))
    near = near.reshape(TOKENS // 2, 3 * width)
    activ_near, grad_near = near[:, 2 * width :], near[:, : 2 * width]
    activ_far, grad_far = other_core(activ_near), other_core(grad_near)

    down_sum, w_gate, w_up = down_bins(activ_near, activ_far, grad, down_index, (w_gate, w_up))
    kept, sent = input_grads(place, grad_near, grad_far, w_gate, w_up, down_sum)
    gate_part = table_sums(grad_near, grad_far, 0, gate_sums, sent)
    kept, down_sum, sent = add_received(kept, down_sum, other_hid(sent, 1))
    up_part = table_sums(grad_near, grad_far, 1, up_sums, sent)
    gate_sum, up_sum = sum_inp(gate_part, up_part, core)
    kept, down_sum, sent = add_received(kept, down_sum, other_hid(sent, 2))
    kept, down_sum, sent = add_received(kept, down_sum, other_hid(sent, 4))
    back = other_hid(sent, 8).astype(F32)
    input_grad = (kept[:8] + back[2 * ENTRIES + 8 :]).astype(BF16)
    down_sum = down_sum + (back[:ENTRIES] + back[ENTRIES : 2 * ENTRIES])
    scale = 1.0 / TOKENS
    return input_grad, gate_sum * scale, up_sum * scale, down_sum * scale


def solution(mesh):
    in_specs = (
        P(None, "inp"),
        P(None, "inp"),
        P("inp", "hid"),
        P("inp", "hid"),
        P("hid", "inp"),
        P(None, "hid"),
        P(None, "hid"),
        P(None, "inp"),
    )
    out_specs = (P("hid", "inp"), P(None, "hid"), P(None, "hid"), P(None, "inp"))
    return jax.shard_map(shards, mesh=mesh, in_specs=in_specs, out_specs=out_specs, check_vma=False)
```

```python
import functools

import jax
import jax.numpy as jnp
from jax import lax
from jax.experimental import pallas as pl
from jax.experimental.pallas import tpu as pltpu
from jax.sharding import PartitionSpec as P

BF16 = jnp.bfloat16
F32 = jnp.float32
I32 = jnp.int32
ENTRIES = 16
TOKENS = 128
LANES = 128
HBM_BYTES_PER_US = 3_000_000


def params(mib=16):
    return pltpu.CompilerParams(vmem_limit_bytes=mib * 1024 * 1024)


def cost(us):
    return pl.CostEstimate(flops=0, bytes_accessed=int(us * HBM_BYTES_PER_US), transcendentals=0)


def shape(dims, dtype):
    return jax.ShapeDtypeStruct(dims, dtype)


def dot(a, b):
    return jnp.dot(a, b, preferred_element_type=F32)


def dot_nt(a, b):
    return lax.dot_general(a, b, (((1,), (1,)), ((), ())), preferred_element_type=F32)


def dot_tn(a, b):
    return lax.dot_general(a, b, (((0,), (0,)), ((), ())), preferred_element_type=F32)


def iotas(size):
    return lax.broadcasted_iota(I32, (size, size), 0), lax.broadcasted_iota(I32, (size, size), 1)


def one_hot(hits):
    return jnp.where(hits, 1.0, 0.0).astype(BF16)


def split_matrix(block):
    source, target = iotas(block)
    half = block // 2
    return one_hot(source == jnp.where(target < half, 2 * target, 2 * (target - half) + 1))


def merge_matrix(block):
    source, target = iotas(block)
    half = block // 2
    return one_hot(target == jnp.where(source < half, 2 * source, 2 * (source - half) + 1))


def token_of(row, core):
    return (((row >> 3) & 7) * 2 + (core ^ (row >> 6))) * 8 + (row & 7)


def to_rows(core):
    row, token = iotas(TOKENS)
    return one_hot(token == token_of(row, core))


def to_owners(core, hid):
    owned, row = iotas(TOKENS)
    bits = ((owned >> 6) & 1) | ((owned >> 4) & 2) | ((owned >> 2) & 4) | (owned & 8)
    return one_hot(token_of(row, core) == (bits ^ hid) * 8 + (owned & 7))


SCALAR = pl.BlockSpec(memory_space=pltpu.SMEM)
ANYWHERE = pl.BlockSpec(memory_space=pl.ANY)
IN_HBM = pl.BlockSpec(memory_space=pltpu.HBM)
IN_VMEM = pl.BlockSpec(memory_space=pltpu.VMEM)
WIDE = 256
HALF = TOKENS // 2


def lookup(low, high, at, is_high):
    from_low = jnp.take_along_axis(low, at, axis=0, mode="promise_in_bounds")
    from_high = jnp.take_along_axis(high, at, axis=0, mode="promise_in_bounds")
    return jnp.where(is_high, from_high, from_low)


def decode_rows(index_ref, table_ref, weight_ref, begin, words):
    def tile(j, carry):
        cols = pl.ds(pl.multiple_of(j * LANES, LANES), LANES)
        low, high = table_ref[0:8, cols], table_ref[8:16, cols]
        for row in range(0, words, 16):
            even, odd = [], []
            for part in (row, row + 8):
                word = index_ref[begin + part : begin + part + 8, cols]
                even.append(lookup(low, high, word & 7, (word & 8) != 0))
                odd.append(lookup(low, high, (word >> 4) & 7, (word & 128) != 0))
            weight_ref[row : row + 16, cols] = jnp.concatenate(even, axis=0).astype(BF16)
            weight_ref[words + row : words + row + 16, cols] = jnp.concatenate(odd, axis=0).astype(BF16)
        return carry

    lax.fori_loop(0, index_ref.shape[1] // LANES, tile, 0)


def blocks_of(size, block):
    return [(at, min(block, size - at)) for at in range(0, size, block)]


def row_copies(from_ref, to_ref, sems, block):
    return [
        pltpu.make_async_copy(from_ref.at[pl.ds(at, rows)], to_ref.at[pl.ds(at, rows)], sems.at[i])
        for i, (at, rows) in enumerate(blocks_of(from_ref.shape[0], block))
    ]


def in_hbm(*arrays):
    return [pltpu.with_memory_space_constraint(each, pltpu.HBM) for each in arrays]


def start_all(copies):
    for each in copies:
        each.start()


def wait_all(copies):
    for each in copies:
        each.wait()


def forward_down_kernel(
    place_ref, raw_hbm, table_hbm, index_hbm, next_hbm, near_ref, far_ref, ordered_hbm, *refs
):
    count = len(next_hbm)
    next_refs = refs[:count]
    raw_ref, table_ref, index_ref, ordered_ref, weight_ref, sems, next_sems, sem = refs[count:]
    words = index_ref.shape[0]
    loads = row_copies(index_hbm, index_ref, sems, LANES)
    small = [pltpu.make_async_copy(raw_hbm, raw_ref, next_sems.at[count])]
    small.append(pltpu.make_async_copy(table_hbm, table_ref, next_sems.at[count + 1]))
    later = [pltpu.make_async_copy(a, b, next_sems.at[i]) for i, (a, b) in enumerate(zip(next_hbm, next_refs))]
    start_all(small + loads + later)
    wait_all(small)
    ordered_ref[...] = dot(to_rows(place_ref[0]), raw_ref[...]).astype(BF16)
    store = pltpu.make_async_copy(ordered_ref, ordered_hbm, sem)
    store.start()
    merge = {rows: merge_matrix(2 * rows) for _, rows in blocks_of(words, LANES)}
    for load, (at, rows) in zip(loads, blocks_of(words, LANES)):
        load.wait()
        decode_rows(index_ref, table_ref, weight_ref, at, rows)
        hidden = dot_nt(ordered_ref[...], weight_ref[: 2 * rows, :])
        coarse = hidden.astype(BF16)
        fine = (hidden - coarse.astype(F32)).astype(BF16)
        hidden = dot(coarse, merge[rows]) + dot(fine, merge[rows])
        near_ref[:, 2 * at : 2 * (at + rows)] = hidden[:HALF]
        far_ref[:, 2 * at : 2 * (at + rows)] = hidden[HALF:]
    store.wait()
    wait_all(later)


def forward_down(place, grad, table, index, brought):
    words, width = index.shape
    count = len(brought)

    def kernel(*refs):
        forward_down_kernel(*refs[:4], refs[4 : 4 + count], *refs[4 + count :])

    return pl.pallas_call(
        kernel,
        in_specs=[SCALAR] + [IN_HBM] * (3 + count),
        out_specs=[IN_VMEM, IN_VMEM, IN_HBM] + [IN_VMEM] * count,
        out_shape=[
            pltpu.VMEM((HALF, 2 * words), F32),
            pltpu.VMEM((HALF, 2 * words), F32),
            pltpu.HBM((TOKENS, width), BF16),
        ]
        + [pltpu.VMEM(each.shape, each.dtype) for each in brought],
        scratch_shapes=[
            pltpu.VMEM(grad.shape, BF16),
            pltpu.VMEM(table.shape, F32),
            pltpu.VMEM(index.shape, I32),
            pltpu.VMEM((TOKENS, width), BF16),
            pltpu.VMEM((WIDE, width), BF16),
            pltpu.SemaphoreType.DMA((pl.cdiv(words, LANES),)),
            pltpu.SemaphoreType.DMA((count + 2,)),
            pltpu.SemaphoreType.DMA,
        ],
        compiler_params=params(),
        cost_estimate=cost(5),
        name="forward_down",
    )(place, *in_hbm(grad, table, index, *brought))


def forward_up_kernel(first, *refs):
    if first:
        place_ref, raw_ref, index_ref, table_ref, next_hbm, near_ref, far_ref, weight_hbm = refs[:8]
        x_ref, x_hbm, next_ref, weight_ref, sems, next_sems = refs[8:]
        later = [pltpu.make_async_copy(next_hbm, next_ref, next_sems.at[0])]
        start_all(later)
        x = dot(to_rows(place_ref[0]), raw_ref[...]).astype(BF16)
        for at in range(0, x.shape[1], WIDE):
            x_ref[:, at : at + WIDE] = dot(x[:, at : at + WIDE], split_matrix(WIDE)).astype(BF16)
        later.append(pltpu.make_async_copy(x_ref, x_hbm, next_sems.at[1]))
        start_all(later[1:])
    else:
        x_ref, index_ref, table_ref, near_ref, far_ref, weight_hbm, weight_ref, sems = refs
        later = []
    stores = row_copies(weight_ref, weight_hbm, sems, WIDE)
    for store, at in zip(stores, range(0, index_ref.shape[0], LANES)):
        decode_rows(index_ref, table_ref, weight_ref.at[pl.ds(2 * at, WIDE)], at, LANES)
        store.start()
    for at, cols in blocks_of(index_ref.shape[1], WIDE):
        sums = dot(x_ref[...], weight_ref[:, at : at + cols])
        near_ref[:, at : at + cols] = sums[:HALF]
        far_ref[:, at : at + cols] = sums[HALF:]
    wait_all(stores + later)


def forward_up(place, x, index, table, later_index):
    first = place is not None
    words, width = index.shape
    ordered = (TOKENS, 2 * words)
    return pl.pallas_call(
        functools.partial(forward_up_kernel, first),
        in_specs=[SCALAR] * first + [IN_VMEM] * 3 + [IN_HBM] * first,
        out_specs=[IN_VMEM, IN_VMEM, IN_HBM] + [IN_VMEM, IN_HBM, IN_VMEM] * first,
        out_shape=[
            pltpu.VMEM((HALF, width), F32),
            pltpu.VMEM((HALF, width), F32),
            pltpu.HBM((2 * words, width), BF16),
        ]
        + [pltpu.VMEM(ordered, BF16), pltpu.HBM(ordered, BF16), pltpu.VMEM((words, width), I32)] * first,
        scratch_shapes=[pltpu.VMEM((2 * words, width), BF16), pltpu.SemaphoreType.DMA((2 * words // WIDE,))]
        + [pltpu.SemaphoreType.DMA((2,))] * first,
        compiler_params=params(),
        cost_estimate=cost(5),
        name="forward_gate" if first else "forward_up",
    )(*([place] * first + [x, index, table] + in_hbm(*[later_index] * first)))


def entry_sums_kernel(x_ref, left_ref, right_ref, last_ref, after_ref, out_ref, entry_ref):
    words = left_ref.shape[0]

    def unpack(half_ref, cols):
        for row in range(0, words, 16):
            word = half_ref[row : row + 16, :]
            to = row // LANES * WIDE + row % LANES
            entry_ref[to : to + 16, cols] = (word & 15).astype(jnp.int16)
            entry_ref[to + LANES : to + LANES + 16, cols] = ((word >> 4) & 15).astype(jnp.int16)

    last = pl.program_id(0) == pl.num_programs(0) - 1
    unpack(left_ref, slice(0, LANES))
    pl.when(jnp.logical_not(last))(lambda: unpack(right_ref, slice(LANES, WIDE)))
    pl.when(last)(lambda: unpack(last_ref, slice(LANES, WIDE)))
    x = x_ref[...]
    one, zero = jnp.ones((), BF16), jnp.zeros((), BF16)
    rest = jnp.sum(x.astype(F32), axis=1, keepdims=True)
    for entry in range(ENTRIES - 1):
        chosen = jnp.where(entry_ref[...] == jnp.int16(entry), one, zero)
        sums = dot(x, chosen)
        out_ref[entry] = sums.astype(BF16)
        rest = rest - sums
    out_ref[ENTRIES - 1] = rest.astype(BF16)


def entry_sums(x, index, first, last_index, last, blocks, after):
    words = index.shape[0]
    limit = index.shape[1] // LANES - 1
    return pl.pallas_call(
        entry_sums_kernel,
        grid=(blocks,),
        in_specs=[
            pl.BlockSpec((TOKENS, 2 * words), lambda i: (0, 0)),
            pl.BlockSpec((words, LANES), lambda i: (0, first + 2 * i)),
            pl.BlockSpec((words, LANES), lambda i: (0, jnp.minimum(first + 2 * i + 1, limit))),
            pl.BlockSpec((words, LANES), lambda i: (0, last)),
            ANYWHERE,
        ],
        out_specs=pl.BlockSpec((ENTRIES, TOKENS, WIDE), lambda i: (0, 0, i)),
        out_shape=shape((ENTRIES, TOKENS, blocks * WIDE), BF16),
        scratch_shapes=[pltpu.VMEM((2 * words, WIDE), jnp.int16)],
        compiler_params=params(60),
        cost_estimate=cost(11),
        name="entry_sums",
    )(x, index, index, last_index, after)


def table_sums_kernel(part, pieces, near_ref, far_ref, *refs):
    sums_hbm = refs[: len(pieces)]
    after_ref, out_ref, grad_ref, sums_ref, sems = refs[len(pieces) :]
    count = ENTRIES // sems.shape[0]
    loads = []
    for i in range(sems.shape[0]):
        entries = pl.ds(i * count, count)
        loads.append([])
        for j, (begin, cols, to) in enumerate(pieces):
            source = sums_hbm[j].at[entries, :, pl.ds(begin, cols)]
            loads[i].append(pltpu.make_async_copy(source, sums_ref.at[entries, :, pl.ds(to, cols)], sems.at[i, j]))
        start_all(loads[i])
    width = sums_ref.shape[2]
    grad_ref[:HALF, :] = near_ref[:, part * width : (part + 1) * width].astype(F32)
    grad_ref[HALF:, :] = far_ref[:, part * width : (part + 1) * width].astype(F32)
    for load, begin in zip(loads, range(0, ENTRIES, count)):
        wait_all(load)

        def tile(j, carry, begin=begin):
            cols = pl.ds(pl.multiple_of(j * LANES, LANES), LANES)
            rows = []
            for entry in range(begin, begin + count):
                acc = None
                for row in range(0, TOKENS, 16):
                    product = sums_ref[entry, row : row + 16, cols].astype(F32) * grad_ref[row : row + 16, cols]
                    acc = product if acc is None else acc + product
                rows.append(jnp.sum(acc, axis=0, keepdims=True))
            out_ref[begin : begin + count, cols] = jnp.concatenate(rows, axis=0)
            return carry

        lax.fori_loop(0, width // LANES, tile, 0)


def table_sums(near, far, part, sums, pieces, after):
    width = sum(cols for _, cols, _ in pieces)
    return pl.pallas_call(
        functools.partial(table_sums_kernel, part, pieces),
        in_specs=[IN_VMEM, IN_VMEM] + [IN_HBM] * len(sums) + [ANYWHERE],
        out_specs=IN_VMEM,
        out_shape=pltpu.VMEM((ENTRIES, width), F32),
        scratch_shapes=[
            pltpu.VMEM((TOKENS, width), F32),
            pltpu.VMEM((ENTRIES, TOKENS, width), BF16),
            pltpu.SemaphoreType.DMA((4, len(pieces))),
        ],
        compiler_params=params(),
        cost_estimate=cost(4.5),
        name="table_sums",
    )(near, far, *in_hbm(*sums), after)


def down_bins_kernel(near_ref, far_ref, grad_hbm, index_hbm, next_hbm, out_ref, next_refs, *scratch):
    grad_ref, index_ref, activ_ref, wgrad_ref, sems = scratch
    loads = [pltpu.make_async_copy(grad_hbm, grad_ref, sems.at[0])]
    loads.append(pltpu.make_async_copy(index_hbm, index_ref, sems.at[1]))
    loads += [pltpu.make_async_copy(a, b, sems.at[2 + i]) for i, (a, b) in enumerate(zip(next_hbm, next_refs))]
    start_all(loads)
    block = LANES
    half = block // 2
    words, width = index_ref.shape
    split = split_matrix(block)
    for at in range(0, 2 * words, block):
        cols = slice(at, at + block)
        activ = jnp.concatenate([near_ref[:, cols], far_ref[:, cols]], axis=0)
        activ_ref[:, cols] = dot(activ, split).astype(BF16)
    wait_all(loads[:1])
    for at in range(0, width, WIDE):
        wgrad_ref[:, at : at + WIDE] = dot_tn(activ_ref[...], grad_ref[:, at : at + WIDE]).astype(BF16)
    wait_all(loads[1:2])
    zero = jnp.zeros((), BF16)

    def lanes(j, carry):
        cols = pl.ds(pl.multiple_of(j * LANES, LANES), LANES)

        def add_block(i, totals):
            part = [None] * ENTRIES
            for row in range(0, half, 16):
                word = index_ref[pl.ds(pl.multiple_of(i * half + row, 16), 16), cols].astype(jnp.int16)
                for entries, offset in ((word & 15, 0), ((word >> 4) & 15, half)):
                    grads = wgrad_ref[pl.ds(pl.multiple_of(i * block + offset + row, 16), 16), cols]
                    for entry in range(ENTRIES):
                        chosen = jnp.where(entries == jnp.int16(entry), grads, zero)
                        part[entry] = chosen if part[entry] is None else part[entry] + chosen
            done = []
            for entry in range(ENTRIES):
                both = part[entry].astype(F32)
                done.append(totals[entry] + both[:8] + both[8:])
            return tuple(done)

        start = tuple(jnp.zeros((8, LANES), F32) for _ in range(ENTRIES))
        totals = lax.fori_loop(0, 2 * words // block, add_block, start)
        out_ref[:, cols] = jnp.concatenate([jnp.sum(each, axis=0, keepdims=True) for each in totals], axis=0)
        return carry

    lax.fori_loop(0, width // LANES, lanes, 0)
    wait_all(loads[2:])


def down_bins(near, far, grad, index, brought):
    words, width = index.shape
    count = len(brought)

    def kernel(*refs):
        out = 4 + count
        down_bins_kernel(*refs[:4], refs[4:out], refs[out], refs[out + 1 : out + 1 + count], *refs[out + 1 + count :])

    return pl.pallas_call(
        kernel,
        in_specs=[IN_VMEM] * 2 + [IN_HBM] * (2 + count),
        out_specs=[IN_VMEM] * (1 + count),
        out_shape=[pltpu.VMEM((ENTRIES, width), F32)] + [pltpu.VMEM(each.shape, each.dtype) for each in brought],
        scratch_shapes=[
            pltpu.VMEM((TOKENS, width), BF16),
            pltpu.VMEM((words, width), I32),
            pltpu.VMEM((TOKENS, 2 * words), BF16),
            pltpu.VMEM((2 * words, width), BF16),
            pltpu.SemaphoreType.DMA((2 + count,)),
        ],
        compiler_params=params(),
        cost_estimate=cost(10),
        name="down_bins",
    )(near, far, *in_hbm(grad, index, *brought))


def put_bins(bins, sent_ref):
    coarse = bins.astype(BF16)
    sent_ref[:ENTRIES] = coarse
    sent_ref[ENTRIES : 2 * ENTRIES] = (bins - coarse.astype(F32)).astype(BF16)


def input_grad_kernel(
    place_ref, near_ref, far_ref, wg_ref, wu_ref, bins_ref, kept_ref, sent_ref
):
    rows, width = wg_ref.shape
    gate = jnp.concatenate([near_ref[:, :width], far_ref[:, :width]], axis=0)
    up = jnp.concatenate([near_ref[:, width:], far_ref[:, width:]], axis=0)
    order = to_owners(place_ref[0], place_ref[1])
    merge = merge_matrix(WIDE)
    for at in range(0, rows, WIDE):
        part = (dot_nt(gate, wg_ref[at : at + WIDE, :]) + dot_nt(up, wu_ref[at : at + WIDE, :])).astype(BF16)
        part = dot(dot(order, part).astype(BF16), merge)
        kept_ref[:, at : at + WIDE] = part[:HALF]
        sent_ref[2 * ENTRIES :, at : at + WIDE] = part[HALF:].astype(BF16)
    put_bins(bins_ref[...], sent_ref)


def input_grads(place, near, far, w_gate, w_up, bins):
    width = w_gate.shape[0]
    return pl.pallas_call(
        input_grad_kernel,
        in_specs=[SCALAR] + [IN_VMEM] * 5,
        out_specs=[IN_VMEM] * 2,
        out_shape=[pltpu.VMEM((HALF, width), F32), pltpu.VMEM((2 * ENTRIES + HALF, width), BF16)],
        compiler_params=params(),
        cost_estimate=cost(3.5),
        name="input_grad",
    )(place, near, far, w_gate, w_up, bins)


def add_received_kernel(kept_ref, bins_ref, back_ref, after_ref, rows_ref, sums_ref, sent_ref):
    bins = bins_ref[...] + (back_ref[:ENTRIES].astype(F32) + back_ref[ENTRIES : 2 * ENTRIES].astype(F32))
    rows = kept_ref[...] + back_ref[2 * ENTRIES :].astype(F32)
    rows_ref[...] = rows[: rows_ref.shape[0]]
    sums_ref[...] = bins
    put_bins(bins, sent_ref)
    sent_ref[2 * ENTRIES :] = rows[rows.shape[0] - sent_ref.shape[0] + 2 * ENTRIES :].astype(BF16)


def add_received(kept, bins, back, after):
    rows, width = kept.shape
    half = max(rows // 2, 16)
    return pl.pallas_call(
        add_received_kernel,
        in_specs=[IN_VMEM] * 3 + [ANYWHERE],
        out_specs=[IN_VMEM] * 3,
        out_shape=[
            pltpu.VMEM((half, width), F32),
            pltpu.VMEM(bins.shape, F32),
            pltpu.VMEM((2 * ENTRIES + half, width), BF16),
        ],
        compiler_params=params(),
        cost_estimate=cost(0.7),
        name="add_received",
    )(kept, bins, back, after)


ONE_CORE = [[2 * place + core for place in range(8)] for core in range(2)]


def other_core(array):
    return lax.ppermute(array, "inp", [(i, i ^ 1) for i in range(16)])


def exchange_inp(pieces):
    return lax.all_to_all(pieces, "inp", 0, 0, tiled=True, axis_index_groups=ONE_CORE)


def copies(array, count):
    return jnp.broadcast_to(array[None], (count,) + array.shape)


def total(arrays):
    return functools.reduce(jnp.add, [a.astype(F32) for a in arrays])


def choose_kernel(place_ref, gate_ref, up_ref, after_ref, own_ref, other_ref):
    gate_here = place_ref[0] == 0
    own_ref[...] = jnp.where(gate_here, gate_ref[...], up_ref[...])
    other_ref[...] = jnp.where(gate_here, up_ref[...], gate_ref[...])


def choose(place, gate, up, after):
    return pl.pallas_call(
        choose_kernel,
        in_specs=[SCALAR, IN_VMEM, IN_VMEM, ANYWHERE],
        out_specs=[IN_VMEM] * 2,
        out_shape=[pltpu.VMEM(gate.shape, F32)] * 2,
        compiler_params=params(),
        cost_estimate=cost(0.7),
        name="choose",
    )(place, gate, up, after)


def add_and_copy_kernel(own_ref, back_ref, after_ref, out_ref):
    both = (own_ref[...] + back_ref[...]).astype(BF16)
    for place in range(out_ref.shape[0]):
        out_ref[place] = both


def add_and_copy(own, back, after):
    return pl.pallas_call(
        add_and_copy_kernel,
        in_specs=[IN_VMEM] * 2 + [ANYWHERE],
        out_specs=IN_VMEM,
        out_shape=shape((8,) + own.shape, BF16),
        compiler_params=params(),
        cost_estimate=cost(0.7),
        name="add_and_copy",
    )(own, back, after)


def other_hid(array, bit):
    return lax.ppermute(array, "hid", [(i, i ^ bit) for i in range(16)])


def local_hidden(pre_gate, pre_up, hidden_grad):
    sig_gate = jax.nn.sigmoid(pre_gate)
    silu_gate = pre_gate * sig_gate
    activ = (silu_gate * pre_up).astype(BF16)
    gate_grad = (hidden_grad * pre_up * sig_gate * (1.0 + pre_gate * (1.0 - sig_gate))).astype(BF16)
    up_grad = (hidden_grad * silu_gate).astype(BF16)
    return activ, gate_grad, up_grad


def shards(inputs, out_grad, gate_index, up_index, down_index, gate_table, up_table, down_table):
    width = gate_index.shape[1]
    core = lax.axis_index("inp") % 2
    place = jnp.stack([core, lax.axis_index("hid")]).astype(I32)

    hidden_near, hidden_far, grad, x, gate_words, gate_lookup, up_lookup = forward_down(
        place, out_grad, down_table, down_index, (inputs, gate_index, gate_table, up_table)
    )
    hidden_back = other_core(hidden_far)
    gate_near, gate_far, w_gate, x_near, x, up_words = forward_up(place, x, gate_words, gate_lookup, up_index)
    gate_back = other_core(gate_far)
    up_near, up_far, w_up = forward_up(None, x_near, up_words, up_lookup, None)
    up_back = other_core(up_far)
    pair_sums = jnp.concatenate(
        [(gate_near + gate_back).astype(BF16), (up_near + up_back).astype(BF16), (hidden_near + hidden_back).astype(BF16)],
        axis=1,
    ).reshape(8, 8, 3 * width)
    pieces = exchange_inp(pair_sums)
    columns = width // LANES
    gate_sums = entry_sums(x, gate_index, 0, up_index, 0, (columns + 1) // 2, pair_sums)
    pieces, gate_sums = lax.optimization_barrier((pieces, gate_sums))
    pre = total(pieces)
    activ, gate_grad, up_grad = local_hidden(pre[:, :width], pre[:, width : 2 * width], pre[:, 2 * width :])
    grads = copies(jnp.concatenate([gate_grad, up_grad, activ], axis=1), 8)
    near = exchange_inp(grads)
    up_sums = entry_sums(x, up_index, 1, up_index, columns - 1, columns // 2, grads)
    near, up_sums = lax.optimization_barrier((near, up_sums))
    near = near.reshape(TOKENS // 2, 3 * width)
    activ_near, grad_near = near[:, 2 * width :], near[:, : 2 * width]
    activ_far, grad_far = other_core(activ_near), other_core(grad_near)

    down_sum, w_gate, w_up = down_bins(activ_near, activ_far, grad, down_index, (w_gate, w_up))
    kept, sent = input_grads(place, grad_near, grad_far, w_gate, w_up, down_sum)
    gate_part = table_sums(grad_near, grad_far, 0, [gate_sums], [(0, width, 0)], sent)
    kept, down_sum, sent = add_received(kept, down_sum, other_hid(sent, 1), gate_part)
    pieces = [(width, LANES, 0), (0, width - LANES, LANES)]
    up_part = table_sums(grad_near, grad_far, 1, [gate_sums, up_sums], pieces, sent)
    kept, down_sum, sent = add_received(kept, down_sum, other_hid(sent, 2), up_part)
    own, other = choose(place, gate_part, up_part, sent)
    back = other_core(other)
    kept, down_sum, sent = add_received(kept, down_sum, other_hid(sent, 4), back)
    own = total(exchange_inp(add_and_copy(own, back, sent)))
    other = other_core(own)
    gate_sum, up_sum = jnp.where(core == 0, own, other), jnp.where(core == 0, other, own)
    back = other_hid(sent, 8).astype(F32)
    input_grad = (kept[:8] + back[2 * ENTRIES + 8 :]).astype(BF16)
    down_sum = down_sum + (back[:ENTRIES] + back[ENTRIES : 2 * ENTRIES])
    scale = 1.0 / TOKENS
    return input_grad, gate_sum * scale, up_sum * scale, down_sum * scale


def solution(mesh):
    in_specs = (
        P(None, "inp"),
        P(None, "inp"),
        P("inp", "hid"),
        P("inp", "hid"),
        P("hid", "inp"),
        P(None, "hid"),
        P(None, "hid"),
        P(None, "inp"),
    )
    out_specs = (P("hid", "inp"), P(None, "hid"), P(None, "hid"), P(None, "inp"))
    return jax.shard_map(shards, mesh=mesh, in_specs=in_specs, out_specs=out_specs, check_vma=False)
```

```python
import functools

import jax
import jax.numpy as jnp
from jax import lax
from jax.experimental import pallas as pl
from jax.experimental.pallas import tpu as pltpu
from jax.sharding import PartitionSpec as P

BF16 = jnp.bfloat16
F32 = jnp.float32
I32 = jnp.int32
ENTRIES = 16
TOKENS = 128
LANES = 128
HBM_BYTES_PER_US = 3_000_000


def params(mib=16):
    return pltpu.CompilerParams(vmem_limit_bytes=mib * 1024 * 1024)


def cost(us):
    return pl.CostEstimate(flops=0, bytes_accessed=int(us * HBM_BYTES_PER_US), transcendentals=0)


def shape(dims, dtype):
    return jax.ShapeDtypeStruct(dims, dtype)


def dot(a, b):
    return jnp.dot(a, b, preferred_element_type=F32)


def dot_nt(a, b):
    return lax.dot_general(a, b, (((1,), (1,)), ((), ())), preferred_element_type=F32)


def dot_tn(a, b):
    return lax.dot_general(a, b, (((0,), (0,)), ((), ())), preferred_element_type=F32)


def iotas(size):
    return lax.broadcasted_iota(I32, (size, size), 0), lax.broadcasted_iota(I32, (size, size), 1)


def one_hot(hits):
    return jnp.where(hits, 1.0, 0.0).astype(BF16)


def split_matrix(block):
    source, target = iotas(block)
    half = block // 2
    return one_hot(source == jnp.where(target < half, 2 * target, 2 * (target - half) + 1))


def merge_matrix(block):
    source, target = iotas(block)
    half = block // 2
    return one_hot(target == jnp.where(source < half, 2 * source, 2 * (source - half) + 1))


def token_of(row, core):
    return (((row >> 3) & 7) * 2 + (core ^ (row >> 6))) * 8 + (row & 7)


def to_rows(core):
    row, token = iotas(TOKENS)
    return one_hot(token == token_of(row, core))


def to_owners(core):
    owned, row = iotas(TOKENS)
    return one_hot(token_of(row, core) == (((owned >> 3) & 3) * 4 + (owned >> 5)) * 8 + (owned & 7))


SCALAR = pl.BlockSpec(memory_space=pltpu.SMEM)
ANYWHERE = pl.BlockSpec(memory_space=pl.ANY)
IN_HBM = pl.BlockSpec(memory_space=pltpu.HBM)
IN_VMEM = pl.BlockSpec(memory_space=pltpu.VMEM)
WIDE = 256
HALF = TOKENS // 2


def lookup(low, high, at, is_high):
    from_low = jnp.take_along_axis(low, at, axis=0, mode="promise_in_bounds")
    from_high = jnp.take_along_axis(high, at, axis=0, mode="promise_in_bounds")
    return jnp.where(is_high, from_high, from_low)


def decode_rows(index_ref, table_ref, weight_ref, begin, words):
    def tile(j, carry):
        cols = pl.ds(pl.multiple_of(j * LANES, LANES), LANES)
        low, high = table_ref[0:8, cols], table_ref[8:16, cols]
        for row in range(0, words, 16):
            even, odd = [], []
            for part in (row, row + 8):
                word = index_ref[begin + part : begin + part + 8, cols]
                even.append(lookup(low, high, word & 7, (word & 8) != 0))
                odd.append(lookup(low, high, (word >> 4) & 7, (word & 128) != 0))
            weight_ref[row : row + 16, cols] = jnp.concatenate(even, axis=0).astype(BF16)
            weight_ref[words + row : words + row + 16, cols] = jnp.concatenate(odd, axis=0).astype(BF16)
        return carry

    lax.fori_loop(0, index_ref.shape[1] // LANES, tile, 0)


def blocks_of(size, block):
    return [(at, min(block, size - at)) for at in range(0, size, block)]


def row_copies(from_ref, to_ref, sems, block):
    return [
        pltpu.make_async_copy(from_ref.at[pl.ds(at, rows)], to_ref.at[pl.ds(at, rows)], sems.at[i])
        for i, (at, rows) in enumerate(blocks_of(from_ref.shape[0], block))
    ]


def in_hbm(*arrays):
    return [pltpu.with_memory_space_constraint(each, pltpu.HBM) for each in arrays]


def start_all(copies):
    for each in copies:
        each.start()


def wait_all(copies):
    for each in copies:
        each.wait()


def forward_down_kernel(
    place_ref, raw_hbm, table_hbm, index_hbm, next_hbm, near_ref, far_ref, ordered_hbm, *refs
):
    count = len(next_hbm)
    next_refs = refs[:count]
    raw_ref, table_ref, index_ref, ordered_ref, weight_ref, sems, next_sems, sem = refs[count:]
    words = index_ref.shape[0]
    loads = row_copies(index_hbm, index_ref, sems, LANES)
    small = [pltpu.make_async_copy(raw_hbm, raw_ref, next_sems.at[count])]
    small.append(pltpu.make_async_copy(table_hbm, table_ref, next_sems.at[count + 1]))
    later = [pltpu.make_async_copy(a, b, next_sems.at[i]) for i, (a, b) in enumerate(zip(next_hbm, next_refs))]
    start_all(small + loads)
    wait_all(small)
    ordered_ref[...] = dot(to_rows(place_ref[0]), raw_ref[...]).astype(BF16)
    store = pltpu.make_async_copy(ordered_ref, ordered_hbm, sem)
    store.start()
    merge = {rows: merge_matrix(2 * rows) for _, rows in blocks_of(words, LANES)}
    for i, (load, (at, rows)) in enumerate(zip(loads, blocks_of(words, LANES))):
        load.wait()
        if i == len(loads) // 2 - 1:
            start_all(later)
        decode_rows(index_ref, table_ref, weight_ref, at, rows)
        hidden = dot_nt(ordered_ref[...], weight_ref[: 2 * rows, :])
        coarse = hidden.astype(BF16)
        fine = (hidden - coarse.astype(F32)).astype(BF16)
        hidden = dot(coarse, merge[rows]) + dot(fine, merge[rows])
        near_ref[:, 2 * at : 2 * (at + rows)] = hidden[:HALF]
        far_ref[:, 2 * at : 2 * (at + rows)] = hidden[HALF:]
    store.wait()
    wait_all(later)


def forward_down(place, grad, table, index, brought):
    words, width = index.shape
    count = len(brought)

    def kernel(*refs):
        forward_down_kernel(*refs[:4], refs[4 : 4 + count], *refs[4 + count :])

    return pl.pallas_call(
        kernel,
        in_specs=[SCALAR] + [IN_HBM] * (3 + count),
        out_specs=[IN_VMEM, IN_VMEM, IN_HBM] + [IN_VMEM] * count,
        out_shape=[
            pltpu.VMEM((HALF, 2 * words), F32),
            pltpu.VMEM((HALF, 2 * words), F32),
            pltpu.HBM((TOKENS, width), BF16),
        ]
        + [pltpu.VMEM(each.shape, each.dtype) for each in brought],
        scratch_shapes=[
            pltpu.VMEM(grad.shape, BF16),
            pltpu.VMEM(table.shape, F32),
            pltpu.VMEM(index.shape, I32),
            pltpu.VMEM((TOKENS, width), BF16),
            pltpu.VMEM((WIDE, width), BF16),
            pltpu.SemaphoreType.DMA((pl.cdiv(words, LANES),)),
            pltpu.SemaphoreType.DMA((count + 2,)),
            pltpu.SemaphoreType.DMA,
        ],
        compiler_params=params(),
        cost_estimate=cost(5),
        name="forward_down",
    )(place, *in_hbm(grad, table, index, *brought))


def forward_up_kernel(first, *refs):
    if first:
        place_ref, raw_ref, index_ref, table_ref, next_hbm, near_ref, far_ref, weight_hbm = refs[:8]
        x_ref, x_hbm, next_ref, weight_ref, sems, next_sems = refs[8:]
        later = [pltpu.make_async_copy(next_hbm, next_ref, next_sems.at[0])]
        start_all(later)
        x = dot(to_rows(place_ref[0]), raw_ref[...]).astype(BF16)
        for at in range(0, x.shape[1], WIDE):
            x_ref[:, at : at + WIDE] = dot(x[:, at : at + WIDE], split_matrix(WIDE)).astype(BF16)
        later.append(pltpu.make_async_copy(x_ref, x_hbm, next_sems.at[1]))
        start_all(later[1:])
    else:
        x_ref, index_ref, table_ref, near_ref, far_ref, weight_hbm, weight_ref, sems = refs
        later = []
    stores = row_copies(weight_ref, weight_hbm, sems, WIDE)
    for store, at in zip(stores, range(0, index_ref.shape[0], LANES)):
        decode_rows(index_ref, table_ref, weight_ref.at[pl.ds(2 * at, WIDE)], at, LANES)
        store.start()
    for at, cols in blocks_of(index_ref.shape[1], WIDE):
        sums = dot(x_ref[...], weight_ref[:, at : at + cols])
        near_ref[:, at : at + cols] = sums[:HALF]
        far_ref[:, at : at + cols] = sums[HALF:]
    wait_all(stores + later)


def forward_up(place, x, index, table, later_index):
    first = place is not None
    words, width = index.shape
    ordered = (TOKENS, 2 * words)
    return pl.pallas_call(
        functools.partial(forward_up_kernel, first),
        in_specs=[SCALAR] * first + [IN_VMEM] * 3 + [IN_HBM] * first,
        out_specs=[IN_VMEM, IN_VMEM, IN_HBM] + [IN_VMEM, IN_HBM, IN_VMEM] * first,
        out_shape=[
            pltpu.VMEM((HALF, width), F32),
            pltpu.VMEM((HALF, width), F32),
            pltpu.HBM((2 * words, width), BF16),
        ]
        + [pltpu.VMEM(ordered, BF16), pltpu.HBM(ordered, BF16), pltpu.VMEM((words, width), I32)] * first,
        scratch_shapes=[pltpu.VMEM((2 * words, width), BF16), pltpu.SemaphoreType.DMA((2 * words // WIDE,))]
        + [pltpu.SemaphoreType.DMA((2,))] * first,
        compiler_params=params(),
        cost_estimate=cost(5),
        name="forward_gate" if first else "forward_up",
    )(*([place] * first + [x, index, table] + in_hbm(*[later_index] * first)))


def entry_sums_kernel(x_ref, left_ref, right_ref, last_ref, after_ref, out_ref, entry_ref):
    words = left_ref.shape[0]

    def unpack(half_ref, cols):
        for row in range(0, words, 16):
            word = half_ref[row : row + 16, :]
            to = row // LANES * WIDE + row % LANES
            entry_ref[to : to + 16, cols] = (word & 15).astype(jnp.int16)
            entry_ref[to + LANES : to + LANES + 16, cols] = ((word >> 4) & 15).astype(jnp.int16)

    last = pl.program_id(0) == pl.num_programs(0) - 1
    unpack(left_ref, slice(0, LANES))
    pl.when(jnp.logical_not(last))(lambda: unpack(right_ref, slice(LANES, WIDE)))
    pl.when(last)(lambda: unpack(last_ref, slice(LANES, WIDE)))
    x = x_ref[...]
    one, zero = jnp.ones((), BF16), jnp.zeros((), BF16)
    rest = jnp.sum(x.astype(F32), axis=1, keepdims=True)
    for entry in range(ENTRIES - 1):
        chosen = jnp.where(entry_ref[...] == jnp.int16(entry), one, zero)
        sums = dot(x, chosen)
        out_ref[entry] = sums.astype(BF16)
        rest = rest - sums
    out_ref[ENTRIES - 1] = rest.astype(BF16)


def entry_sums(x, index, first, last_index, last, blocks, after):
    words = index.shape[0]
    limit = index.shape[1] // LANES - 1
    return pl.pallas_call(
        entry_sums_kernel,
        grid=(blocks,),
        in_specs=[
            pl.BlockSpec((TOKENS, 2 * words), lambda i: (0, 0)),
            pl.BlockSpec((words, LANES), lambda i: (0, first + 2 * i)),
            pl.BlockSpec((words, LANES), lambda i: (0, jnp.minimum(first + 2 * i + 1, limit))),
            pl.BlockSpec((words, LANES), lambda i: (0, last)),
            ANYWHERE,
        ],
        out_specs=pl.BlockSpec((ENTRIES, TOKENS, WIDE), lambda i: (0, 0, i)),
        out_shape=shape((ENTRIES, TOKENS, blocks * WIDE), BF16),
        scratch_shapes=[pltpu.VMEM((2 * words, WIDE), jnp.int16)],
        compiler_params=params(60),
        cost_estimate=cost(11),
        name="entry_sums",
    )(x, index, index, last_index, after)


def table_sums_kernel(part, pieces, near_ref, far_ref, *refs):
    sums_hbm = refs[: len(pieces)]
    after_ref, out_ref, grad_ref, sums_ref, sems = refs[len(pieces) :]
    count = ENTRIES // sems.shape[0]
    loads = []
    for i in range(sems.shape[0]):
        entries = pl.ds(i * count, count)
        loads.append([])
        for j, (begin, cols, to) in enumerate(pieces):
            source = sums_hbm[j].at[entries, :, pl.ds(begin, cols)]
            loads[i].append(pltpu.make_async_copy(source, sums_ref.at[entries, :, pl.ds(to, cols)], sems.at[i, j]))
        start_all(loads[i])
    width = sums_ref.shape[2]
    grad_ref[:HALF, :] = near_ref[:, part * width : (part + 1) * width].astype(F32)
    grad_ref[HALF:, :] = far_ref[:, part * width : (part + 1) * width].astype(F32)
    for load, begin in zip(loads, range(0, ENTRIES, count)):
        wait_all(load)

        def tile(j, carry, begin=begin):
            cols = pl.ds(pl.multiple_of(j * LANES, LANES), LANES)
            rows = []
            for entry in range(begin, begin + count):
                acc = None
                for row in range(0, TOKENS, 16):
                    product = sums_ref[entry, row : row + 16, cols].astype(F32) * grad_ref[row : row + 16, cols]
                    acc = product if acc is None else acc + product
                rows.append(jnp.sum(acc, axis=0, keepdims=True))
            out_ref[begin : begin + count, cols] = jnp.concatenate(rows, axis=0)
            return carry

        lax.fori_loop(0, width // LANES, tile, 0)


def table_sums(near, far, part, sums, pieces, after):
    width = sum(cols for _, cols, _ in pieces)
    return pl.pallas_call(
        functools.partial(table_sums_kernel, part, pieces),
        in_specs=[IN_VMEM, IN_VMEM] + [IN_HBM] * len(sums) + [ANYWHERE],
        out_specs=IN_VMEM,
        out_shape=pltpu.VMEM((ENTRIES, width), F32),
        scratch_shapes=[
            pltpu.VMEM((TOKENS, width), F32),
            pltpu.VMEM((ENTRIES, TOKENS, width), BF16),
            pltpu.SemaphoreType.DMA((4, len(pieces))),
        ],
        compiler_params=params(),
        cost_estimate=cost(4.5),
        name="table_sums",
    )(near, far, *in_hbm(*sums), after)


def down_bins_kernel(near_ref, far_ref, grad_hbm, index_hbm, next_hbm, out_ref, next_refs, *scratch):
    grad_ref, index_ref, activ_ref, wgrad_ref, sems = scratch
    loads = [pltpu.make_async_copy(grad_hbm, grad_ref, sems.at[0])]
    loads.append(pltpu.make_async_copy(index_hbm, index_ref, sems.at[1]))
    loads += [pltpu.make_async_copy(a, b, sems.at[2 + i]) for i, (a, b) in enumerate(zip(next_hbm, next_refs))]
    start_all(loads)
    block = LANES
    half = block // 2
    words, width = index_ref.shape
    split = split_matrix(block)
    for at in range(0, 2 * words, block):
        cols = slice(at, at + block)
        activ = jnp.concatenate([near_ref[:, cols], far_ref[:, cols]], axis=0)
        activ_ref[:, cols] = dot(activ, split).astype(BF16)
    wait_all(loads[:1])
    for at in range(0, width, WIDE):
        wgrad_ref[:, at : at + WIDE] = dot_tn(activ_ref[...], grad_ref[:, at : at + WIDE]).astype(BF16)
    wait_all(loads[1:2])
    zero = jnp.zeros((), BF16)

    def lanes(j, carry):
        cols = pl.ds(pl.multiple_of(j * LANES, LANES), LANES)

        def add_block(i, totals):
            part = [None] * ENTRIES
            for row in range(0, half, 16):
                word = index_ref[pl.ds(pl.multiple_of(i * half + row, 16), 16), cols].astype(jnp.int16)
                for entries, offset in ((word & 15, 0), ((word >> 4) & 15, half)):
                    grads = wgrad_ref[pl.ds(pl.multiple_of(i * block + offset + row, 16), 16), cols]
                    for entry in range(ENTRIES):
                        chosen = jnp.where(entries == jnp.int16(entry), grads, zero)
                        part[entry] = chosen if part[entry] is None else part[entry] + chosen
            done = []
            for entry in range(ENTRIES):
                both = part[entry].astype(F32)
                done.append(totals[entry] + both[:8] + both[8:])
            return tuple(done)

        start = tuple(jnp.zeros((8, LANES), F32) for _ in range(ENTRIES))
        totals = lax.fori_loop(0, 2 * words // block, add_block, start)
        out_ref[:, cols] = jnp.concatenate([jnp.sum(each, axis=0, keepdims=True) for each in totals], axis=0)
        return carry

    lax.fori_loop(0, width // LANES, lanes, 0)
    wait_all(loads[2:])


def down_bins(near, far, grad, index, brought):
    words, width = index.shape
    count = len(brought)

    def kernel(*refs):
        out = 4 + count
        down_bins_kernel(*refs[:4], refs[4:out], refs[out], refs[out + 1 : out + 1 + count], *refs[out + 1 + count :])

    return pl.pallas_call(
        kernel,
        in_specs=[IN_VMEM] * 2 + [IN_HBM] * (2 + count),
        out_specs=[IN_VMEM] * (1 + count),
        out_shape=[pltpu.VMEM((ENTRIES, width), F32)] + [pltpu.VMEM(each.shape, each.dtype) for each in brought],
        scratch_shapes=[
            pltpu.VMEM((TOKENS, width), BF16),
            pltpu.VMEM((words, width), I32),
            pltpu.VMEM((TOKENS, 2 * words), BF16),
            pltpu.VMEM((2 * words, width), BF16),
            pltpu.SemaphoreType.DMA((2 + count,)),
        ],
        compiler_params=params(),
        cost_estimate=cost(10),
        name="down_bins",
    )(near, far, *in_hbm(grad, index, *brought))


def input_grad_kernel(place_ref, near_ref, far_ref, wg_ref, wu_ref, bins_ref, sent_ref):
    pieces = sent_ref.shape[0]
    rows, width = wg_ref.shape
    gate = jnp.concatenate([near_ref[:, :width], far_ref[:, :width]], axis=0)
    up = jnp.concatenate([near_ref[:, width:], far_ref[:, width:]], axis=0)
    order = to_owners(place_ref[0])
    merge = merge_matrix(WIDE)
    count = TOKENS // pieces
    for at in range(0, rows, WIDE):
        part = (dot_nt(gate, wg_ref[at : at + WIDE, :]) + dot_nt(up, wu_ref[at : at + WIDE, :])).astype(BF16)
        part = dot(dot(order, part).astype(BF16), merge).astype(BF16)
        for piece in range(pieces):
            sent_ref[piece, ENTRIES:, at : at + WIDE] = part[piece * count : (piece + 1) * count]
    bins = bins_ref[...].astype(BF16)
    for piece in range(pieces):
        sent_ref[piece, :ENTRIES] = bins


def input_grads(place, near, far, w_gate, w_up, bins):
    width = w_gate.shape[0]
    return pl.pallas_call(
        input_grad_kernel,
        in_specs=[SCALAR] + [IN_VMEM] * 5,
        out_specs=IN_VMEM,
        out_shape=shape((4, ENTRIES + TOKENS // 4, width), BF16),
        compiler_params=params(),
        cost_estimate=cost(3.5),
        name="input_grad",
    )(place, near, far, w_gate, w_up, bins)


def add_along_x_kernel(back_ref, after_ref, sent_ref):
    pieces = back_ref.shape[0]
    sums = back_ref[0].astype(F32)
    for piece in range(1, pieces):
        sums = sums + back_ref[piece].astype(F32)
    bins = sums[:ENTRIES].astype(BF16)
    for piece in range(pieces):
        own = sums[ENTRIES + 8 * piece : ENTRIES + 8 * piece + 8]
        sent_ref[piece, :ENTRIES] = bins
        sent_ref[piece, ENTRIES:] = jnp.concatenate([own, own], axis=0).astype(BF16)


def add_along_x(back, after):
    width = back.shape[2]
    return pl.pallas_call(
        add_along_x_kernel,
        in_specs=[IN_VMEM, ANYWHERE],
        out_specs=IN_VMEM,
        out_shape=shape((4, ENTRIES + 16, width), BF16),
        compiler_params=params(),
        cost_estimate=cost(0.7),
        name="add_along_x",
    )(back, after)


ONE_CORE = [[2 * place + core for place in range(8)] for core in range(2)]


def other_core(array):
    return lax.ppermute(array, "inp", [(i, i ^ 1) for i in range(16)])


def exchange_inp(pieces):
    return lax.all_to_all(pieces, "inp", 0, 0, tiled=True, axis_index_groups=ONE_CORE)


def copies(array, count):
    return jnp.broadcast_to(array[None], (count,) + array.shape)


def total(arrays):
    return functools.reduce(jnp.add, [a.astype(F32) for a in arrays])


def choose_kernel(place_ref, gate_ref, up_ref, after_ref, own_ref, other_ref):
    gate_here = place_ref[0] == 0
    own_ref[...] = jnp.where(gate_here, gate_ref[...], up_ref[...])
    other_ref[...] = jnp.where(gate_here, up_ref[...], gate_ref[...])


def choose(place, gate, up, after):
    return pl.pallas_call(
        choose_kernel,
        in_specs=[SCALAR, IN_VMEM, IN_VMEM, ANYWHERE],
        out_specs=[IN_VMEM] * 2,
        out_shape=[pltpu.VMEM(gate.shape, F32)] * 2,
        compiler_params=params(),
        cost_estimate=cost(0.7),
        name="choose",
    )(place, gate, up, after)


def add_and_copy_kernel(own_ref, back_ref, after_ref, out_ref):
    both = (own_ref[...] + back_ref[...]).astype(BF16)
    for place in range(out_ref.shape[0]):
        out_ref[place] = both


def add_and_copy(own, back, after):
    return pl.pallas_call(
        add_and_copy_kernel,
        in_specs=[IN_VMEM] * 2 + [ANYWHERE],
        out_specs=IN_VMEM,
        out_shape=shape((8,) + own.shape, BF16),
        compiler_params=params(),
        cost_estimate=cost(0.7),
        name="add_and_copy",
    )(own, back, after)


SAME_Z = [[4 * z + x for x in range(4)] for z in range(4)]
SAME_X = [[4 * z + x for z in range(4)] for x in range(4)]


def exchange_hid(pieces, groups):
    return lax.all_to_all(pieces, "hid", 0, 0, tiled=True, axis_index_groups=groups)


def local_hidden(pre_gate, pre_up, hidden_grad):
    sig_gate = jax.nn.sigmoid(pre_gate)
    silu_gate = pre_gate * sig_gate
    activ = (silu_gate * pre_up).astype(BF16)
    gate_grad = (hidden_grad * pre_up * sig_gate * (1.0 + pre_gate * (1.0 - sig_gate))).astype(BF16)
    up_grad = (hidden_grad * silu_gate).astype(BF16)
    return activ, gate_grad, up_grad


def shards(inputs, out_grad, gate_index, up_index, down_index, gate_table, up_table, down_table):
    width = gate_index.shape[1]
    core = lax.axis_index("inp") % 2
    place = jnp.stack([core, lax.axis_index("hid")]).astype(I32)

    hidden_near, hidden_far, grad, x, gate_words, gate_lookup, up_lookup = forward_down(
        place, out_grad, down_table, down_index, (inputs, gate_index, gate_table, up_table)
    )
    hidden_back = other_core(hidden_far)
    gate_near, gate_far, w_gate, x_near, x, up_words = forward_up(place, x, gate_words, gate_lookup, up_index)
    gate_back = other_core(gate_far)
    up_near, up_far, w_up = forward_up(None, x_near, up_words, up_lookup, None)
    up_back = other_core(up_far)
    pair_sums = jnp.concatenate(
        [(gate_near + gate_back).astype(BF16), (up_near + up_back).astype(BF16), (hidden_near + hidden_back).astype(BF16)],
        axis=1,
    ).reshape(8, 8, 3 * width)
    pieces = exchange_inp(pair_sums)
    columns = width // LANES
    gate_sums = entry_sums(x, gate_index, 0, up_index, 0, (columns + 1) // 2, pair_sums)
    pieces, gate_sums = lax.optimization_barrier((pieces, gate_sums))
    pre = total(pieces)
    activ, gate_grad, up_grad = local_hidden(pre[:, :width], pre[:, width : 2 * width], pre[:, 2 * width :])
    grads = copies(jnp.concatenate([gate_grad, up_grad, activ], axis=1), 8)
    near = exchange_inp(grads)
    up_sums = entry_sums(x, up_index, 1, up_index, columns - 1, columns // 2, grads)
    near, up_sums = lax.optimization_barrier((near, up_sums))
    near = near.reshape(TOKENS // 2, 3 * width)
    activ_near, grad_near = near[:, 2 * width :], near[:, : 2 * width]
    activ_far, grad_far = other_core(activ_near), other_core(grad_near)

    down_sum, w_gate, w_up = down_bins(activ_near, activ_far, grad, down_index, (w_gate, w_up))
    sent = input_grads(place, grad_near, grad_far, w_gate, w_up, down_sum)
    back_x = exchange_hid(sent, SAME_Z)
    gate_part = table_sums(grad_near, grad_far, 0, [gate_sums], [(0, width, 0)], sent)
    pieces = [(width, LANES, 0), (0, width - LANES, LANES)]
    up_part = table_sums(grad_near, grad_far, 1, [gate_sums, up_sums], pieces, gate_part)
    own, other = choose(place, gate_part, up_part, up_part)
    own = total(exchange_inp(add_and_copy(own, other_core(other), back_x)))
    other = other_core(own)
    gate_sum, up_sum = jnp.where(core == 0, own, other), jnp.where(core == 0, other, own)
    back = exchange_hid(add_along_x(back_x, own), SAME_X)
    input_grad = total(back[:, ENTRIES : ENTRIES + 8]).astype(BF16)
    down_sum = total(back[:, :ENTRIES])
    scale = 1.0 / TOKENS
    return input_grad, gate_sum * scale, up_sum * scale, down_sum * scale


def solution(mesh):
    in_specs = (
        P(None, "inp"),
        P(None, "inp"),
        P("inp", "hid"),
        P("inp", "hid"),
        P("hid", "inp"),
        P(None, "hid"),
        P(None, "hid"),
        P(None, "inp"),
    )
    out_specs = (P("hid", "inp"), P(None, "hid"), P(None, "hid"), P(None, "inp"))
    return jax.shard_map(shards, mesh=mesh, in_specs=in_specs, out_specs=out_specs, check_vma=False)
```

```python
import functools

import jax
import jax.numpy as jnp
from jax import lax
from jax.experimental import pallas as pl
from jax.experimental.pallas import tpu as pltpu
from jax.sharding import PartitionSpec as P

BF16 = jnp.bfloat16
F32 = jnp.float32
I32 = jnp.int32
ENTRIES = 16
TOKENS = 128
LANES = 128
HBM_BYTES_PER_US = 3_000_000


def params(mib=16):
    return pltpu.CompilerParams(vmem_limit_bytes=mib * 1024 * 1024)


def cost(us):
    return pl.CostEstimate(flops=0, bytes_accessed=int(us * HBM_BYTES_PER_US), transcendentals=0)


def shape(dims, dtype):
    return jax.ShapeDtypeStruct(dims, dtype)


def dot(a, b):
    return jnp.dot(a, b, preferred_element_type=F32)


def dot_nt(a, b):
    return lax.dot_general(a, b, (((1,), (1,)), ((), ())), preferred_element_type=F32)


def dot_tn(a, b):
    return lax.dot_general(a, b, (((0,), (0,)), ((), ())), preferred_element_type=F32)


def iotas(size):
    return lax.broadcasted_iota(I32, (size, size), 0), lax.broadcasted_iota(I32, (size, size), 1)


def one_hot(hits):
    return jnp.where(hits, 1.0, 0.0).astype(BF16)


def split_matrix(block):
    source, target = iotas(block)
    half = block // 2
    return one_hot(source == jnp.where(target < half, 2 * target, 2 * (target - half) + 1))


def merge_matrix(block):
    source, target = iotas(block)
    half = block // 2
    return one_hot(target == jnp.where(source < half, 2 * source, 2 * (source - half) + 1))


def token_of(row, core):
    return (((row >> 3) & 7) * 2 + (core ^ (row >> 6))) * 8 + (row & 7)


def to_rows(core):
    row, token = iotas(TOKENS)
    return one_hot(token == token_of(row, core))


def to_owners(core, hid):
    owned, row = iotas(TOKENS)
    away = ((owned >> 4) & 1) | ((owned >> 2) & 2)
    return one_hot(token_of(row, core) == ((away ^ (hid >> 2)) * 4 + (owned >> 5)) * 8 + (owned & 7))


SCALAR = pl.BlockSpec(memory_space=pltpu.SMEM)
ANYWHERE = pl.BlockSpec(memory_space=pl.ANY)
IN_HBM = pl.BlockSpec(memory_space=pltpu.HBM)
IN_VMEM = pl.BlockSpec(memory_space=pltpu.VMEM)
WIDE = 256
HALF = TOKENS // 2


def lookup(low, high, at, is_high):
    from_low = jnp.take_along_axis(low, at, axis=0, mode="promise_in_bounds")
    from_high = jnp.take_along_axis(high, at, axis=0, mode="promise_in_bounds")
    return jnp.where(is_high, from_high, from_low)


def decode_rows(index_ref, table_ref, weight_ref, begin, words):
    def tile(j, carry):
        cols = pl.ds(pl.multiple_of(j * LANES, LANES), LANES)
        low, high = table_ref[0:8, cols], table_ref[8:16, cols]
        for row in range(0, words, 16):
            even, odd = [], []
            for part in (row, row + 8):
                word = index_ref[begin + part : begin + part + 8, cols]
                even.append(lookup(low, high, word & 7, (word & 8) != 0))
                odd.append(lookup(low, high, (word >> 4) & 7, (word & 128) != 0))
            weight_ref[row : row + 16, cols] = jnp.concatenate(even, axis=0).astype(BF16)
            weight_ref[words + row : words + row + 16, cols] = jnp.concatenate(odd, axis=0).astype(BF16)
        return carry

    lax.fori_loop(0, index_ref.shape[1] // LANES, tile, 0)


def blocks_of(size, block):
    return [(at, min(block, size - at)) for at in range(0, size, block)]


def row_copies(from_ref, to_ref, sems, block):
    return [
        pltpu.make_async_copy(from_ref.at[pl.ds(at, rows)], to_ref.at[pl.ds(at, rows)], sems.at[i])
        for i, (at, rows) in enumerate(blocks_of(from_ref.shape[0], block))
    ]


def in_hbm(*arrays):
    return [pltpu.with_memory_space_constraint(each, pltpu.HBM) for each in arrays]


def start_all(copies):
    for each in copies:
        each.start()


def wait_all(copies):
    for each in copies:
        each.wait()


def forward_down_kernel(
    place_ref, raw_hbm, table_hbm, index_hbm, next_hbm, near_ref, far_ref, ordered_hbm, *refs
):
    count = len(next_hbm)
    next_refs = refs[:count]
    raw_ref, table_ref, index_ref, ordered_ref, weight_ref, sems, next_sems, sem = refs[count:]
    words = index_ref.shape[0]
    loads = row_copies(index_hbm, index_ref, sems, LANES)
    small = [pltpu.make_async_copy(raw_hbm, raw_ref, next_sems.at[count])]
    small.append(pltpu.make_async_copy(table_hbm, table_ref, next_sems.at[count + 1]))
    later = [pltpu.make_async_copy(a, b, next_sems.at[i]) for i, (a, b) in enumerate(zip(next_hbm, next_refs))]
    start_all(small + loads)
    wait_all(small)
    ordered_ref[...] = dot(to_rows(place_ref[0]), raw_ref[...]).astype(BF16)
    store = pltpu.make_async_copy(ordered_ref, ordered_hbm, sem)
    store.start()
    for i, (load, (at, rows)) in enumerate(zip(loads, blocks_of(words, LANES))):
        load.wait()
        if i == len(loads) // 2 - 1:
            start_all(later)
        decode_rows(index_ref, table_ref, weight_ref.at[pl.ds(2 * at, 2 * rows)], at, rows)
    merge = {rows: merge_matrix(2 * rows) for _, rows in blocks_of(words, LANES)}
    for at, rows in blocks_of(words, LANES):
        cols = slice(2 * at, 2 * (at + rows))
        hidden = dot_nt(ordered_ref[...], weight_ref[cols, :])
        coarse = hidden.astype(BF16)
        fine = (hidden - coarse.astype(F32)).astype(BF16)
        hidden = dot(coarse, merge[rows]) + dot(fine, merge[rows])
        near_ref[:, cols] = hidden[:HALF]
        far_ref[:, cols] = hidden[HALF:]
    store.wait()
    wait_all(later)


def forward_down(place, grad, table, index, brought):
    words, width = index.shape
    count = len(brought)

    def kernel(*refs):
        forward_down_kernel(*refs[:4], refs[4 : 4 + count], *refs[4 + count :])

    return pl.pallas_call(
        kernel,
        in_specs=[SCALAR] + [IN_HBM] * (3 + count),
        out_specs=[IN_VMEM, IN_VMEM, IN_HBM] + [IN_VMEM] * count,
        out_shape=[
            pltpu.VMEM((HALF, 2 * words), F32),
            pltpu.VMEM((HALF, 2 * words), F32),
            pltpu.HBM((TOKENS, width), BF16),
        ]
        + [pltpu.VMEM(each.shape, each.dtype) for each in brought],
        scratch_shapes=[
            pltpu.VMEM(grad.shape, BF16),
            pltpu.VMEM(table.shape, F32),
            pltpu.VMEM(index.shape, I32),
            pltpu.VMEM((TOKENS, width), BF16),
            pltpu.VMEM((2 * words, width), BF16),
            pltpu.SemaphoreType.DMA((pl.cdiv(words, LANES),)),
            pltpu.SemaphoreType.DMA((count + 2,)),
            pltpu.SemaphoreType.DMA,
        ],
        compiler_params=params(),
        cost_estimate=cost(5),
        name="forward_down",
    )(place, *in_hbm(grad, table, index, *brought))


def forward_up_kernel(first, *refs):
    if first:
        place_ref, raw_ref, index_ref, table_ref, next_hbm, near_ref, far_ref, weight_hbm = refs[:8]
        x_ref, x_hbm, next_ref, weight_ref, sems, next_sems = refs[8:]
        later = [pltpu.make_async_copy(next_hbm, next_ref, next_sems.at[0])]
        start_all(later)
        x = dot(to_rows(place_ref[0]), raw_ref[...]).astype(BF16)
        for at in range(0, x.shape[1], WIDE):
            x_ref[:, at : at + WIDE] = dot(x[:, at : at + WIDE], split_matrix(WIDE)).astype(BF16)
        later.append(pltpu.make_async_copy(x_ref, x_hbm, next_sems.at[1]))
        start_all(later[1:])
    else:
        x_ref, index_ref, table_ref, near_ref, far_ref, weight_hbm, weight_ref, sems = refs
        later = []
    stores = row_copies(weight_ref, weight_hbm, sems, WIDE)
    for store, at in zip(stores, range(0, index_ref.shape[0], LANES)):
        decode_rows(index_ref, table_ref, weight_ref.at[pl.ds(2 * at, WIDE)], at, LANES)
        store.start()
    for at, cols in blocks_of(index_ref.shape[1], WIDE):
        sums = dot(x_ref[...], weight_ref[:, at : at + cols])
        near_ref[:, at : at + cols] = sums[:HALF]
        far_ref[:, at : at + cols] = sums[HALF:]
    wait_all(stores + later)


def forward_up(place, x, index, table, later_index):
    first = place is not None
    words, width = index.shape
    ordered = (TOKENS, 2 * words)
    return pl.pallas_call(
        functools.partial(forward_up_kernel, first),
        in_specs=[SCALAR] * first + [IN_VMEM] * 3 + [IN_HBM] * first,
        out_specs=[IN_VMEM, IN_VMEM, IN_HBM] + [IN_VMEM, IN_HBM, IN_VMEM] * first,
        out_shape=[
            pltpu.VMEM((HALF, width), F32),
            pltpu.VMEM((HALF, width), F32),
            pltpu.HBM((2 * words, width), BF16),
        ]
        + [pltpu.VMEM(ordered, BF16), pltpu.HBM(ordered, BF16), pltpu.VMEM((words, width), I32)] * first,
        scratch_shapes=[pltpu.VMEM((2 * words, width), BF16), pltpu.SemaphoreType.DMA((2 * words // WIDE,))]
        + [pltpu.SemaphoreType.DMA((2,))] * first,
        compiler_params=params(),
        cost_estimate=cost(5),
        name="forward_gate" if first else "forward_up",
    )(*([place] * first + [x, index, table] + in_hbm(*[later_index] * first)))


def entry_sums_kernel(x_ref, left_ref, right_ref, last_ref, after_ref, out_ref, entry_ref):
    words = left_ref.shape[0]

    def unpack(half_ref, cols):
        for row in range(0, words, 16):
            word = half_ref[row : row + 16, :]
            to = row // LANES * WIDE + row % LANES
            entry_ref[to : to + 16, cols] = (word & 15).astype(jnp.int16)
            entry_ref[to + LANES : to + LANES + 16, cols] = ((word >> 4) & 15).astype(jnp.int16)

    last = pl.program_id(0) == pl.num_programs(0) - 1
    unpack(left_ref, slice(0, LANES))
    pl.when(jnp.logical_not(last))(lambda: unpack(right_ref, slice(LANES, WIDE)))
    pl.when(last)(lambda: unpack(last_ref, slice(LANES, WIDE)))
    x = x_ref[...]
    one, zero = jnp.ones((), BF16), jnp.zeros((), BF16)
    rest = jnp.sum(x.astype(F32), axis=1, keepdims=True)
    for entry in range(ENTRIES - 1):
        chosen = jnp.where(entry_ref[...] == jnp.int16(entry), one, zero)
        sums = dot(x, chosen)
        out_ref[entry] = sums.astype(BF16)
        rest = rest - sums
    out_ref[ENTRIES - 1] = rest.astype(BF16)


def entry_sums(x, index, first, last_index, last, blocks, after):
    words = index.shape[0]
    limit = index.shape[1] // LANES - 1
    return pl.pallas_call(
        entry_sums_kernel,
        grid=(blocks,),
        in_specs=[
            pl.BlockSpec((TOKENS, 2 * words), lambda i: (0, 0)),
            pl.BlockSpec((words, LANES), lambda i: (0, first + 2 * i)),
            pl.BlockSpec((words, LANES), lambda i: (0, jnp.minimum(first + 2 * i + 1, limit))),
            pl.BlockSpec((words, LANES), lambda i: (0, last)),
            ANYWHERE,
        ],
        out_specs=pl.BlockSpec((ENTRIES, TOKENS, WIDE), lambda i: (0, 0, i)),
        out_shape=shape((ENTRIES, TOKENS, blocks * WIDE), BF16),
        scratch_shapes=[pltpu.VMEM((2 * words, WIDE), jnp.int16)],
        compiler_params=params(60),
        cost_estimate=cost(11),
        name="entry_sums",
    )(x, index, index, last_index, after)


def table_sums_kernel(part, pieces, near_ref, far_ref, *refs):
    sums_hbm = refs[: len(pieces)]
    after_ref, out_ref, grad_ref, sums_ref, sems = refs[len(pieces) :]
    count = ENTRIES // sems.shape[0]
    loads = []
    for i in range(sems.shape[0]):
        entries = pl.ds(i * count, count)
        loads.append([])
        for j, (begin, cols, to) in enumerate(pieces):
            source = sums_hbm[j].at[entries, :, pl.ds(begin, cols)]
            loads[i].append(pltpu.make_async_copy(source, sums_ref.at[entries, :, pl.ds(to, cols)], sems.at[i, j]))
        start_all(loads[i])
    width = sums_ref.shape[2]
    grad_ref[:HALF, :] = near_ref[:, part * width : (part + 1) * width].astype(F32)
    grad_ref[HALF:, :] = far_ref[:, part * width : (part + 1) * width].astype(F32)
    for load, begin in zip(loads, range(0, ENTRIES, count)):
        wait_all(load)

        def tile(j, carry, begin=begin):
            cols = pl.ds(pl.multiple_of(j * LANES, LANES), LANES)
            rows = []
            for entry in range(begin, begin + count):
                acc = None
                for row in range(0, TOKENS, 16):
                    product = sums_ref[entry, row : row + 16, cols].astype(F32) * grad_ref[row : row + 16, cols]
                    acc = product if acc is None else acc + product
                rows.append(jnp.sum(acc, axis=0, keepdims=True))
            out_ref[begin : begin + count, cols] = jnp.concatenate(rows, axis=0)
            return carry

        lax.fori_loop(0, width // LANES, tile, 0)


def table_sums(near, far, part, sums, pieces, after):
    width = sum(cols for _, cols, _ in pieces)
    return pl.pallas_call(
        functools.partial(table_sums_kernel, part, pieces),
        in_specs=[IN_VMEM, IN_VMEM] + [IN_HBM] * len(sums) + [ANYWHERE],
        out_specs=IN_VMEM,
        out_shape=pltpu.VMEM((ENTRIES, width), F32),
        scratch_shapes=[
            pltpu.VMEM((TOKENS, width), F32),
            pltpu.VMEM((ENTRIES, TOKENS, width), BF16),
            pltpu.SemaphoreType.DMA((4, len(pieces))),
        ],
        compiler_params=params(),
        cost_estimate=cost(4.5),
        name="table_sums",
    )(near, far, *in_hbm(*sums), after)


def down_bins_kernel(near_ref, far_ref, grad_hbm, index_hbm, next_hbm, out_ref, next_refs, *scratch):
    grad_ref, index_ref, activ_ref, wgrad_ref, sems = scratch
    loads = [pltpu.make_async_copy(grad_hbm, grad_ref, sems.at[0])]
    loads.append(pltpu.make_async_copy(index_hbm, index_ref, sems.at[1]))
    loads += [pltpu.make_async_copy(a, b, sems.at[2 + i]) for i, (a, b) in enumerate(zip(next_hbm, next_refs))]
    start_all(loads)
    block = LANES
    half = block // 2
    words, width = index_ref.shape
    split = split_matrix(block)
    for at in range(0, 2 * words, block):
        cols = slice(at, at + block)
        activ = jnp.concatenate([near_ref[:, cols], far_ref[:, cols]], axis=0)
        activ_ref[:, cols] = dot(activ, split).astype(BF16)
    wait_all(loads[:1])
    for at in range(0, width, WIDE):
        wgrad_ref[:, at : at + WIDE] = dot_tn(activ_ref[...], grad_ref[:, at : at + WIDE]).astype(BF16)
    wait_all(loads[1:2])
    zero = jnp.zeros((), BF16)

    def lanes(j, carry):
        cols = pl.ds(pl.multiple_of(j * LANES, LANES), LANES)

        def add_block(i, totals):
            part = [None] * ENTRIES
            for row in range(0, half, 16):
                word = index_ref[pl.ds(pl.multiple_of(i * half + row, 16), 16), cols].astype(jnp.int16)
                for entries, offset in ((word & 15, 0), ((word >> 4) & 15, half)):
                    grads = wgrad_ref[pl.ds(pl.multiple_of(i * block + offset + row, 16), 16), cols]
                    for entry in range(ENTRIES):
                        chosen = jnp.where(entries == jnp.int16(entry), grads, zero)
                        part[entry] = chosen if part[entry] is None else part[entry] + chosen
            done = []
            for entry in range(ENTRIES):
                both = part[entry].astype(F32)
                done.append(totals[entry] + both[:8] + both[8:])
            return tuple(done)

        start = tuple(jnp.zeros((8, LANES), F32) for _ in range(ENTRIES))
        totals = lax.fori_loop(0, 2 * words // block, add_block, start)
        out_ref[:, cols] = jnp.concatenate([jnp.sum(each, axis=0, keepdims=True) for each in totals], axis=0)
        return carry

    lax.fori_loop(0, width // LANES, lanes, 0)
    wait_all(loads[2:])


def down_bins(near, far, grad, index, brought):
    words, width = index.shape
    count = len(brought)

    def kernel(*refs):
        out = 4 + count
        down_bins_kernel(*refs[:4], refs[4:out], refs[out], refs[out + 1 : out + 1 + count], *refs[out + 1 + count :])

    return pl.pallas_call(
        kernel,
        in_specs=[IN_VMEM] * 2 + [IN_HBM] * (2 + count),
        out_specs=[IN_VMEM] * (1 + count),
        out_shape=[pltpu.VMEM((ENTRIES, width), F32)] + [pltpu.VMEM(each.shape, each.dtype) for each in brought],
        scratch_shapes=[
            pltpu.VMEM((TOKENS, width), BF16),
            pltpu.VMEM((words, width), I32),
            pltpu.VMEM((TOKENS, 2 * words), BF16),
            pltpu.VMEM((2 * words, width), BF16),
            pltpu.SemaphoreType.DMA((2 + count,)),
        ],
        compiler_params=params(),
        cost_estimate=cost(10),
        name="down_bins",
    )(near, far, *in_hbm(grad, index, *brought))


def input_grad_kernel(place_ref, near_ref, far_ref, wg_ref, wu_ref, bins_ref, sent_ref):
    pieces = sent_ref.shape[0]
    rows, width = wg_ref.shape
    gate = jnp.concatenate([near_ref[:, :width], far_ref[:, :width]], axis=0)
    up = jnp.concatenate([near_ref[:, width:], far_ref[:, width:]], axis=0)
    order = to_owners(place_ref[0], place_ref[1])
    merge = merge_matrix(WIDE)
    count = TOKENS // pieces

    def product(i, carry):
        at = pl.ds(pl.multiple_of(i * WIDE, WIDE), WIDE)
        part = (dot_nt(gate, wg_ref[at, :]) + dot_nt(up, wu_ref[at, :])).astype(BF16)
        part = dot(dot(order, part).astype(BF16), merge).astype(BF16)
        for piece in range(pieces):
            sent_ref[piece, ENTRIES:, at] = part[piece * count : (piece + 1) * count]
        return carry

    lax.fori_loop(0, rows // WIDE, product, 0)
    bins = bins_ref[...].astype(BF16)
    for piece in range(pieces):
        sent_ref[piece, :ENTRIES] = bins


def input_grads(place, near, far, w_gate, w_up, bins):
    width = w_gate.shape[0]
    return pl.pallas_call(
        input_grad_kernel,
        in_specs=[SCALAR] + [IN_VMEM] * 5,
        out_specs=IN_VMEM,
        out_shape=shape((4, ENTRIES + TOKENS // 4, width), BF16),
        compiler_params=params(),
        cost_estimate=cost(3.5),
        name="input_grad",
    )(place, near, far, w_gate, w_up, bins)


def put_bins(bins, sent_ref):
    coarse = bins.astype(BF16)
    sent_ref[:ENTRIES] = coarse
    sent_ref[ENTRIES : 2 * ENTRIES] = (bins - coarse.astype(F32)).astype(BF16)


def add_along_x_kernel(back_ref, after_ref, kept_ref, bins_ref, sent_ref):
    sums = back_ref[0].astype(F32)
    for piece in range(1, back_ref.shape[0]):
        sums = sums + back_ref[piece].astype(F32)
    half = kept_ref.shape[0]
    kept_ref[...] = sums[ENTRIES : ENTRIES + half]
    bins_ref[...] = sums[:ENTRIES]
    put_bins(sums[:ENTRIES], sent_ref)
    sent_ref[2 * ENTRIES :] = sums[ENTRIES + half :].astype(BF16)


def add_along_x(back, after):
    half, width = (back.shape[1] - ENTRIES) // 2, back.shape[2]
    return pl.pallas_call(
        add_along_x_kernel,
        in_specs=[IN_VMEM, ANYWHERE],
        out_specs=[IN_VMEM] * 3,
        out_shape=[
            pltpu.VMEM((half, width), F32),
            pltpu.VMEM((ENTRIES, width), F32),
            pltpu.VMEM((2 * ENTRIES + half, width), BF16),
        ],
        compiler_params=params(),
        cost_estimate=cost(0.7),
        name="add_along_x",
    )(back, after)


def add_along_z_kernel(kept_ref, bins_ref, back_ref, after_ref, rows_ref, sums_ref, sent_ref):
    bins = bins_ref[...] + (back_ref[:ENTRIES].astype(F32) + back_ref[ENTRIES : 2 * ENTRIES].astype(F32))
    rows = kept_ref[...] + back_ref[2 * ENTRIES :].astype(F32)
    rows_ref[...] = rows
    sums_ref[...] = bins
    put_bins(bins, sent_ref)
    sent_ref[2 * ENTRIES :] = rows.astype(BF16)


def add_along_z(kept, bins, back, after):
    rows, width = kept.shape
    return pl.pallas_call(
        add_along_z_kernel,
        in_specs=[IN_VMEM] * 3 + [ANYWHERE],
        out_specs=[IN_VMEM] * 3,
        out_shape=[
            pltpu.VMEM((rows, width), F32),
            pltpu.VMEM(bins.shape, F32),
            pltpu.VMEM((2 * ENTRIES + rows, width), BF16),
        ],
        compiler_params=params(),
        cost_estimate=cost(0.7),
        name="add_along_z",
    )(kept, bins, back, after)


ONE_CORE = [[2 * place + core for place in range(8)] for core in range(2)]


def other_core(array):
    return lax.ppermute(array, "inp", [(i, i ^ 1) for i in range(16)])


def exchange_inp(pieces):
    return lax.all_to_all(pieces, "inp", 0, 0, tiled=True, axis_index_groups=ONE_CORE)


def copies(array, count):
    return jnp.broadcast_to(array[None], (count,) + array.shape)


def total(arrays):
    return functools.reduce(jnp.add, [a.astype(F32) for a in arrays])


def choose_kernel(place_ref, gate_ref, up_ref, after_ref, own_ref, other_ref):
    gate_here = place_ref[0] == 0
    own_ref[...] = jnp.where(gate_here, gate_ref[...], up_ref[...])
    other_ref[...] = jnp.where(gate_here, up_ref[...], gate_ref[...])


def choose(place, gate, up, after):
    return pl.pallas_call(
        choose_kernel,
        in_specs=[SCALAR, IN_VMEM, IN_VMEM, ANYWHERE],
        out_specs=[IN_VMEM] * 2,
        out_shape=[pltpu.VMEM(gate.shape, F32)] * 2,
        compiler_params=params(),
        cost_estimate=cost(0.7),
        name="choose",
    )(place, gate, up, after)


def add_and_copy_kernel(own_ref, back_ref, after_ref, out_ref):
    both = (own_ref[...] + back_ref[...]).astype(BF16)
    for place in range(out_ref.shape[0]):
        out_ref[place] = both


def add_and_copy(own, back, after):
    return pl.pallas_call(
        add_and_copy_kernel,
        in_specs=[IN_VMEM] * 2 + [ANYWHERE],
        out_specs=IN_VMEM,
        out_shape=shape((8,) + own.shape, BF16),
        compiler_params=params(),
        cost_estimate=cost(0.7),
        name="add_and_copy",
    )(own, back, after)


SAME_Z = [[4 * z + x for x in range(4)] for z in range(4)]


def exchange_x(pieces):
    return lax.all_to_all(pieces, "hid", 0, 0, tiled=True, axis_index_groups=SAME_Z)


def other_hid(array, bit):
    return lax.ppermute(array, "hid", [(i, i ^ bit) for i in range(16)])


def local_hidden(pre_gate, pre_up, hidden_grad):
    sig_gate = jax.nn.sigmoid(pre_gate)
    silu_gate = pre_gate * sig_gate
    activ = (silu_gate * pre_up).astype(BF16)
    gate_grad = (hidden_grad * pre_up * sig_gate * (1.0 + pre_gate * (1.0 - sig_gate))).astype(BF16)
    up_grad = (hidden_grad * silu_gate).astype(BF16)
    return activ, gate_grad, up_grad


def shards(inputs, out_grad, gate_index, up_index, down_index, gate_table, up_table, down_table):
    width = gate_index.shape[1]
    core = lax.axis_index("inp") % 2
    place = jnp.stack([core, lax.axis_index("hid")]).astype(I32)

    hidden_near, hidden_far, grad, x, gate_words, gate_lookup, up_lookup = forward_down(
        place, out_grad, down_table, down_index, (inputs, gate_index, gate_table, up_table)
    )
    hidden_back = other_core(hidden_far)
    gate_near, gate_far, w_gate, x_near, x, up_words = forward_up(place, x, gate_words, gate_lookup, up_index)
    gate_back = other_core(gate_far)
    up_near, up_far, w_up = forward_up(None, x_near, up_words, up_lookup, None)
    up_back = other_core(up_far)
    pair_sums = jnp.concatenate(
        [(gate_near + gate_back).astype(BF16), (up_near + up_back).astype(BF16), (hidden_near + hidden_back).astype(BF16)],
        axis=1,
    ).reshape(8, 8, 3 * width)
    pieces = exchange_inp(pair_sums)
    columns = width // LANES
    gate_sums = entry_sums(x, gate_index, 0, up_index, 0, (columns + 1) // 2, pair_sums)
    pieces, gate_sums = lax.optimization_barrier((pieces, gate_sums))
    pre = total(pieces)
    activ, gate_grad, up_grad = local_hidden(pre[:, :width], pre[:, width : 2 * width], pre[:, 2 * width :])
    grads = copies(jnp.concatenate([gate_grad, up_grad, activ], axis=1), 8)
    near = exchange_inp(grads)
    up_sums = entry_sums(x, up_index, 1, up_index, columns - 1, columns // 2, grads)
    near, up_sums = lax.optimization_barrier((near, up_sums))
    near = near.reshape(TOKENS // 2, 3 * width)
    activ_near, grad_near = near[:, 2 * width :], near[:, : 2 * width]
    activ_far, grad_far = other_core(activ_near), other_core(grad_near)

    down_sum, w_gate, w_up = down_bins(activ_near, activ_far, grad, down_index, (w_gate, w_up))
    sent = input_grads(place, grad_near, grad_far, w_gate, w_up, down_sum)
    gate_part = table_sums(grad_near, grad_far, 0, [gate_sums], [(0, width, 0)], sent)
    kept, bins, sent = add_along_x(exchange_x(sent), gate_part)
    pieces = [(width, LANES, 0), (0, width - LANES, LANES)]
    up_part = table_sums(grad_near, grad_far, 1, [gate_sums, up_sums], pieces, sent)
    kept, bins, sent = add_along_z(kept, bins, other_hid(sent, 4), up_part)
    own, other = choose(place, gate_part, up_part, up_part)
    own = total(exchange_inp(add_and_copy(own, other_core(other), sent)))
    other = other_core(own)
    gate_sum, up_sum = jnp.where(core == 0, own, other), jnp.where(core == 0, other, own)
    back = other_hid(sent, 8).astype(F32)
    input_grad = (kept[:8] + back[2 * ENTRIES + 8 :]).astype(BF16)
    down_sum = bins + (back[:ENTRIES] + back[ENTRIES : 2 * ENTRIES])
    scale = 1.0 / TOKENS
    return input_grad, gate_sum * scale, up_sum * scale, down_sum * scale


def solution(mesh):
    in_specs = (
        P(None, "inp"),
        P(None, "inp"),
        P("inp", "hid"),
        P("inp", "hid"),
        P("hid", "inp"),
        P(None, "hid"),
        P(None, "hid"),
        P(None, "inp"),
    )
    out_specs = (P("hid", "inp"), P(None, "hid"), P(None, "hid"), P(None, "inp"))
    return jax.shard_map(shards, mesh=mesh, in_specs=in_specs, out_specs=out_specs, check_vma=False)
```

```python
import functools

import jax
import jax.numpy as jnp
from jax import lax
from jax.experimental import pallas as pl
from jax.experimental.pallas import tpu as pltpu
from jax.sharding import PartitionSpec as P

BF16 = jnp.bfloat16
F32 = jnp.float32
I32 = jnp.int32
ENTRIES = 16
TOKENS = 128
LANES = 128
HBM_BYTES_PER_US = 3_000_000


def params(mib=16):
    return pltpu.CompilerParams(vmem_limit_bytes=mib * 1024 * 1024)


def cost(us):
    return pl.CostEstimate(flops=0, bytes_accessed=int(us * HBM_BYTES_PER_US), transcendentals=0)


def shape(dims, dtype):
    return jax.ShapeDtypeStruct(dims, dtype)


def dot(a, b):
    return jnp.dot(a, b, preferred_element_type=F32)


def dot_nt(a, b):
    return lax.dot_general(a, b, (((1,), (1,)), ((), ())), preferred_element_type=F32)


def dot_tn(a, b):
    return lax.dot_general(a, b, (((0,), (0,)), ((), ())), preferred_element_type=F32)


def iotas(size):
    return lax.broadcasted_iota(I32, (size, size), 0), lax.broadcasted_iota(I32, (size, size), 1)


def one_hot(hits):
    return jnp.where(hits, 1.0, 0.0).astype(BF16)


def split_matrix(block):
    source, target = iotas(block)
    half = block // 2
    return one_hot(source == jnp.where(target < half, 2 * target, 2 * (target - half) + 1))


def merge_matrix(block):
    source, target = iotas(block)
    half = block // 2
    return one_hot(target == jnp.where(source < half, 2 * source, 2 * (source - half) + 1))


def token_of(row, core):
    return (((row >> 3) & 7) * 2 + (core ^ (row >> 6))) * 8 + (row & 7)


def to_rows(core):
    row, token = iotas(TOKENS)
    return one_hot(token == token_of(row, core))


def to_owners(core, hid):
    owned, row = iotas(TOKENS)
    bits = ((owned >> 4) & 4) | ((owned >> 2) & 8) | ((owned >> 4) & 1) | ((owned >> 2) & 2)
    return one_hot(token_of(row, core) == (bits ^ hid) * 8 + (owned & 7))


SCALAR = pl.BlockSpec(memory_space=pltpu.SMEM)
ANYWHERE = pl.BlockSpec(memory_space=pl.ANY)
IN_HBM = pl.BlockSpec(memory_space=pltpu.HBM)
IN_VMEM = pl.BlockSpec(memory_space=pltpu.VMEM)
WIDE = 256
HALF = TOKENS // 2


def lookup(low, high, at, is_high):
    from_low = jnp.take_along_axis(low, at, axis=0, mode="promise_in_bounds")
    from_high = jnp.take_along_axis(high, at, axis=0, mode="promise_in_bounds")
    return jnp.where(is_high, from_high, from_low)


def decode_rows(index_ref, table_ref, weight_ref, begin, words):
    def tile(j, carry):
        cols = pl.ds(pl.multiple_of(j * LANES, LANES), LANES)
        low, high = table_ref[0:8, cols], table_ref[8:16, cols]
        for row in range(0, words, 16):
            even, odd = [], []
            for part in (row, row + 8):
                word = index_ref[begin + part : begin + part + 8, cols]
                even.append(lookup(low, high, word & 7, (word & 8) != 0))
                odd.append(lookup(low, high, (word >> 4) & 7, (word & 128) != 0))
            weight_ref[row : row + 16, cols] = jnp.concatenate(even, axis=0).astype(BF16)
            weight_ref[words + row : words + row + 16, cols] = jnp.concatenate(odd, axis=0).astype(BF16)
        return carry

    lax.fori_loop(0, index_ref.shape[1] // LANES, tile, 0)


def blocks_of(size, block):
    return [(at, min(block, size - at)) for at in range(0, size, block)]


def row_copies(from_ref, to_ref, sems, block):
    return [
        pltpu.make_async_copy(from_ref.at[pl.ds(at, rows)], to_ref.at[pl.ds(at, rows)], sems.at[i])
        for i, (at, rows) in enumerate(blocks_of(from_ref.shape[0], block))
    ]


def in_hbm(*arrays):
    return [pltpu.with_memory_space_constraint(each, pltpu.HBM) for each in arrays]


def start_all(copies):
    for each in copies:
        each.start()


def wait_all(copies):
    for each in copies:
        each.wait()


def forward_down_kernel(
    place_ref, raw_hbm, table_hbm, index_hbm, next_hbm, near_ref, far_ref, ordered_hbm, *refs
):
    count = len(next_hbm)
    next_refs = refs[:count]
    raw_ref, table_ref, index_ref, ordered_ref, weight_ref, sems, next_sems, sem = refs[count:]
    words = index_ref.shape[0]
    loads = row_copies(index_hbm, index_ref, sems, LANES)
    small = [pltpu.make_async_copy(raw_hbm, raw_ref, next_sems.at[count])]
    small.append(pltpu.make_async_copy(table_hbm, table_ref, next_sems.at[count + 1]))
    later = [pltpu.make_async_copy(a, b, next_sems.at[i]) for i, (a, b) in enumerate(zip(next_hbm, next_refs))]
    start_all(small + loads)
    wait_all(small)
    ordered_ref[...] = dot(to_rows(place_ref[0]), raw_ref[...]).astype(BF16)
    store = pltpu.make_async_copy(ordered_ref, ordered_hbm, sem)
    store.start()
    for i, (load, (at, rows)) in enumerate(zip(loads, blocks_of(words, LANES))):
        load.wait()
        if i == len(loads) // 2 - 1:
            start_all(later)
        decode_rows(index_ref, table_ref, weight_ref.at[pl.ds(2 * at, 2 * rows)], at, rows)
    merge = {rows: merge_matrix(2 * rows) for _, rows in blocks_of(words, LANES)}
    for at, rows in blocks_of(words, LANES):
        cols = slice(2 * at, 2 * (at + rows))
        hidden = dot_nt(ordered_ref[...], weight_ref[cols, :])
        coarse = hidden.astype(BF16)
        fine = (hidden - coarse.astype(F32)).astype(BF16)
        hidden = dot(coarse, merge[rows]) + dot(fine, merge[rows])
        near_ref[:, cols] = hidden[:HALF]
        far_ref[:, cols] = hidden[HALF:]
    store.wait()
    wait_all(later)


def forward_down(place, grad, table, index, brought):
    words, width = index.shape
    count = len(brought)

    def kernel(*refs):
        forward_down_kernel(*refs[:4], refs[4 : 4 + count], *refs[4 + count :])

    return pl.pallas_call(
        kernel,
        in_specs=[SCALAR] + [IN_HBM] * (3 + count),
        out_specs=[IN_VMEM, IN_VMEM, IN_HBM] + [IN_VMEM] * count,
        out_shape=[
            pltpu.VMEM((HALF, 2 * words), F32),
            pltpu.VMEM((HALF, 2 * words), F32),
            pltpu.HBM((TOKENS, width), BF16),
        ]
        + [pltpu.VMEM(each.shape, each.dtype) for each in brought],
        scratch_shapes=[
            pltpu.VMEM(grad.shape, BF16),
            pltpu.VMEM(table.shape, F32),
            pltpu.VMEM(index.shape, I32),
            pltpu.VMEM((TOKENS, width), BF16),
            pltpu.VMEM((2 * words, width), BF16),
            pltpu.SemaphoreType.DMA((pl.cdiv(words, LANES),)),
            pltpu.SemaphoreType.DMA((count + 2,)),
            pltpu.SemaphoreType.DMA,
        ],
        compiler_params=params(),
        cost_estimate=cost(5),
        name="forward_down",
    )(place, *in_hbm(grad, table, index, *brought))


def forward_up_kernel(first, *refs):
    if first:
        place_ref, raw_ref, index_ref, table_ref, next_hbm, near_ref, far_ref, weight_hbm = refs[:8]
        x_ref, x_hbm, next_ref, weight_ref, sems, next_sems = refs[8:]
        later = [pltpu.make_async_copy(next_hbm, next_ref, next_sems.at[0])]
        start_all(later)
        x = dot(to_rows(place_ref[0]), raw_ref[...]).astype(BF16)
        for at in range(0, x.shape[1], WIDE):
            x_ref[:, at : at + WIDE] = dot(x[:, at : at + WIDE], split_matrix(WIDE)).astype(BF16)
        later.append(pltpu.make_async_copy(x_ref, x_hbm, next_sems.at[1]))
        start_all(later[1:])
    else:
        x_ref, index_ref, table_ref, near_ref, far_ref, weight_hbm, weight_ref, sems = refs
        later = []
    stores = row_copies(weight_ref, weight_hbm, sems, WIDE)
    for store, at in zip(stores, range(0, index_ref.shape[0], LANES)):
        decode_rows(index_ref, table_ref, weight_ref.at[pl.ds(2 * at, WIDE)], at, LANES)
        store.start()
    for at, cols in blocks_of(index_ref.shape[1], WIDE):
        sums = dot(x_ref[...], weight_ref[:, at : at + cols])
        near_ref[:, at : at + cols] = sums[:HALF]
        far_ref[:, at : at + cols] = sums[HALF:]
    wait_all(stores + later)


def forward_up(place, x, index, table, later_index):
    first = place is not None
    words, width = index.shape
    ordered = (TOKENS, 2 * words)
    return pl.pallas_call(
        functools.partial(forward_up_kernel, first),
        in_specs=[SCALAR] * first + [IN_VMEM] * 3 + [IN_HBM] * first,
        out_specs=[IN_VMEM, IN_VMEM, IN_HBM] + [IN_VMEM, IN_HBM, IN_VMEM] * first,
        out_shape=[
            pltpu.VMEM((HALF, width), F32),
            pltpu.VMEM((HALF, width), F32),
            pltpu.HBM((2 * words, width), BF16),
        ]
        + [pltpu.VMEM(ordered, BF16), pltpu.HBM(ordered, BF16), pltpu.VMEM((words, width), I32)] * first,
        scratch_shapes=[pltpu.VMEM((2 * words, width), BF16), pltpu.SemaphoreType.DMA((2 * words // WIDE,))]
        + [pltpu.SemaphoreType.DMA((2,))] * first,
        compiler_params=params(),
        cost_estimate=cost(5),
        name="forward_gate" if first else "forward_up",
    )(*([place] * first + [x, index, table] + in_hbm(*[later_index] * first)))


def entry_sums_kernel(x_ref, left_ref, right_ref, last_ref, after_ref, out_ref, entry_ref):
    words = left_ref.shape[0]

    def unpack(half_ref, cols):
        for row in range(0, words, 16):
            word = half_ref[row : row + 16, :]
            to = row // LANES * WIDE + row % LANES
            entry_ref[to : to + 16, cols] = (word & 15).astype(jnp.int16)
            entry_ref[to + LANES : to + LANES + 16, cols] = ((word >> 4) & 15).astype(jnp.int16)

    last = pl.program_id(0) == pl.num_programs(0) - 1
    unpack(left_ref, slice(0, LANES))
    pl.when(jnp.logical_not(last))(lambda: unpack(right_ref, slice(LANES, WIDE)))
    pl.when(last)(lambda: unpack(last_ref, slice(LANES, WIDE)))
    x = x_ref[...]
    one, zero = jnp.ones((), BF16), jnp.zeros((), BF16)
    rest = jnp.sum(x.astype(F32), axis=1, keepdims=True)
    for entry in range(ENTRIES - 1):
        chosen = jnp.where(entry_ref[...] == jnp.int16(entry), one, zero)
        sums = dot(x, chosen)
        out_ref[entry] = sums.astype(BF16)
        rest = rest - sums
    out_ref[ENTRIES - 1] = rest.astype(BF16)


def entry_sums(x, index, first, last_index, last, blocks, after):
    words = index.shape[0]
    limit = index.shape[1] // LANES - 1
    return pl.pallas_call(
        entry_sums_kernel,
        grid=(blocks,),
        in_specs=[
            pl.BlockSpec((TOKENS, 2 * words), lambda i: (0, 0)),
            pl.BlockSpec((words, LANES), lambda i: (0, first + 2 * i)),
            pl.BlockSpec((words, LANES), lambda i: (0, jnp.minimum(first + 2 * i + 1, limit))),
            pl.BlockSpec((words, LANES), lambda i: (0, last)),
            ANYWHERE,
        ],
        out_specs=pl.BlockSpec((ENTRIES, TOKENS, WIDE), lambda i: (0, 0, i)),
        out_shape=shape((ENTRIES, TOKENS, blocks * WIDE), BF16),
        scratch_shapes=[pltpu.VMEM((2 * words, WIDE), jnp.int16)],
        compiler_params=params(60),
        cost_estimate=cost(11),
        name="entry_sums",
    )(x, index, index, last_index, after)


def table_sums_kernel(part, pieces, near_ref, far_ref, *refs):
    sums_hbm = refs[: len(pieces)]
    after_ref, out_ref, grad_ref, sums_ref, sems = refs[len(pieces) :]
    count = ENTRIES // sems.shape[0]
    loads = []
    for i in range(sems.shape[0]):
        entries = pl.ds(i * count, count)
        loads.append([])
        for j, (begin, cols, to) in enumerate(pieces):
            source = sums_hbm[j].at[entries, :, pl.ds(begin, cols)]
            loads[i].append(pltpu.make_async_copy(source, sums_ref.at[entries, :, pl.ds(to, cols)], sems.at[i, j]))
        start_all(loads[i])
    width = sums_ref.shape[2]
    grad_ref[:HALF, :] = near_ref[:, part * width : (part + 1) * width].astype(F32)
    grad_ref[HALF:, :] = far_ref[:, part * width : (part + 1) * width].astype(F32)
    for load, begin in zip(loads, range(0, ENTRIES, count)):
        wait_all(load)

        def tile(j, carry, begin=begin):
            cols = pl.ds(pl.multiple_of(j * LANES, LANES), LANES)
            rows = []
            for entry in range(begin, begin + count):
                acc = None
                for row in range(0, TOKENS, 16):
                    product = sums_ref[entry, row : row + 16, cols].astype(F32) * grad_ref[row : row + 16, cols]
                    acc = product if acc is None else acc + product
                rows.append(jnp.sum(acc, axis=0, keepdims=True))
            out_ref[begin : begin + count, cols] = jnp.concatenate(rows, axis=0)
            return carry

        lax.fori_loop(0, width // LANES, tile, 0)


def table_sums(near, far, part, sums, pieces, after):
    width = sum(cols for _, cols, _ in pieces)
    return pl.pallas_call(
        functools.partial(table_sums_kernel, part, pieces),
        in_specs=[IN_VMEM, IN_VMEM] + [IN_HBM] * len(sums) + [ANYWHERE],
        out_specs=IN_VMEM,
        out_shape=pltpu.VMEM((ENTRIES, width), F32),
        scratch_shapes=[
            pltpu.VMEM((TOKENS, width), F32),
            pltpu.VMEM((ENTRIES, TOKENS, width), BF16),
            pltpu.SemaphoreType.DMA((4, len(pieces))),
        ],
        compiler_params=params(),
        cost_estimate=cost(4.5),
        name="table_sums",
    )(near, far, *in_hbm(*sums), after)


def down_bins_kernel(near_ref, far_ref, grad_hbm, index_hbm, next_hbm, out_ref, next_refs, *scratch):
    grad_ref, index_ref, activ_ref, wgrad_ref, sems = scratch
    loads = [pltpu.make_async_copy(grad_hbm, grad_ref, sems.at[0])]
    loads.append(pltpu.make_async_copy(index_hbm, index_ref, sems.at[1]))
    loads += [pltpu.make_async_copy(a, b, sems.at[2 + i]) for i, (a, b) in enumerate(zip(next_hbm, next_refs))]
    start_all(loads)
    block = LANES
    half = block // 2
    words, width = index_ref.shape
    split = split_matrix(block)
    for at in range(0, 2 * words, block):
        cols = slice(at, at + block)
        activ = jnp.concatenate([near_ref[:, cols], far_ref[:, cols]], axis=0)
        activ_ref[:, cols] = dot(activ, split).astype(BF16)
    wait_all(loads[:1])
    for at in range(0, width, WIDE):
        wgrad_ref[:, at : at + WIDE] = dot_tn(activ_ref[...], grad_ref[:, at : at + WIDE]).astype(BF16)
    wait_all(loads[1:2])
    zero = jnp.zeros((), BF16)

    def lanes(j, carry):
        cols = pl.ds(pl.multiple_of(j * LANES, LANES), LANES)

        def add_block(i, totals):
            part = [None] * ENTRIES
            for row in range(0, half, 16):
                word = index_ref[pl.ds(pl.multiple_of(i * half + row, 16), 16), cols].astype(jnp.int16)
                for entries, offset in ((word & 15, 0), ((word >> 4) & 15, half)):
                    grads = wgrad_ref[pl.ds(pl.multiple_of(i * block + offset + row, 16), 16), cols]
                    for entry in range(ENTRIES):
                        chosen = jnp.where(entries == jnp.int16(entry), grads, zero)
                        part[entry] = chosen if part[entry] is None else part[entry] + chosen
            done = []
            for entry in range(ENTRIES):
                both = part[entry].astype(F32)
                done.append(totals[entry] + both[:8] + both[8:])
            return tuple(done)

        start = tuple(jnp.zeros((8, LANES), F32) for _ in range(ENTRIES))
        totals = lax.fori_loop(0, 2 * words // block, add_block, start)
        out_ref[:, cols] = jnp.concatenate([jnp.sum(each, axis=0, keepdims=True) for each in totals], axis=0)
        return carry

    lax.fori_loop(0, width // LANES, lanes, 0)
    wait_all(loads[2:])


def down_bins(near, far, grad, index, brought):
    words, width = index.shape
    count = len(brought)

    def kernel(*refs):
        out = 4 + count
        down_bins_kernel(*refs[:4], refs[4:out], refs[out], refs[out + 1 : out + 1 + count], *refs[out + 1 + count :])

    return pl.pallas_call(
        kernel,
        in_specs=[IN_VMEM] * 2 + [IN_HBM] * (2 + count),
        out_specs=[IN_VMEM] * (1 + count),
        out_shape=[pltpu.VMEM((ENTRIES, width), F32)] + [pltpu.VMEM(each.shape, each.dtype) for each in brought],
        scratch_shapes=[
            pltpu.VMEM((TOKENS, width), BF16),
            pltpu.VMEM((words, width), I32),
            pltpu.VMEM((TOKENS, 2 * words), BF16),
            pltpu.VMEM((2 * words, width), BF16),
            pltpu.SemaphoreType.DMA((2 + count,)),
        ],
        compiler_params=params(),
        cost_estimate=cost(10),
        name="down_bins",
    )(near, far, *in_hbm(grad, index, *brought))


def put_bins(bins, sent_ref):
    coarse = bins.astype(BF16)
    sent_ref[:ENTRIES] = coarse
    sent_ref[ENTRIES : 2 * ENTRIES] = (bins - coarse.astype(F32)).astype(BF16)


def input_grad_kernel(
    place_ref, near_ref, far_ref, wg_ref, wu_ref, bins_ref, kept_ref, sent_ref
):
    rows, width = wg_ref.shape
    gate = jnp.concatenate([near_ref[:, :width], far_ref[:, :width]], axis=0)
    up = jnp.concatenate([near_ref[:, width:], far_ref[:, width:]], axis=0)
    order = to_owners(place_ref[0], place_ref[1])
    merge = merge_matrix(WIDE)

    def product(i, carry):
        at = pl.ds(pl.multiple_of(i * WIDE, WIDE), WIDE)
        part = (dot_nt(gate, wg_ref[at, :]) + dot_nt(up, wu_ref[at, :])).astype(BF16)
        part = dot(dot(order, part).astype(BF16), merge)
        kept_ref[:, at] = part[:HALF]
        sent_ref[2 * ENTRIES :, at] = part[HALF:].astype(BF16)
        return carry

    lax.fori_loop(0, rows // WIDE, product, 0)
    put_bins(bins_ref[...], sent_ref)


def input_grads(place, near, far, w_gate, w_up, bins):
    width = w_gate.shape[0]
    return pl.pallas_call(
        input_grad_kernel,
        in_specs=[SCALAR] + [IN_VMEM] * 5,
        out_specs=[IN_VMEM] * 2,
        out_shape=[pltpu.VMEM((HALF, width), F32), pltpu.VMEM((2 * ENTRIES + HALF, width), BF16)],
        compiler_params=params(),
        cost_estimate=cost(3.5),
        name="input_grad",
    )(place, near, far, w_gate, w_up, bins)


def add_received_kernel(kept_ref, bins_ref, back_ref, after_ref, rows_ref, sums_ref, sent_ref):
    bins = bins_ref[...] + (back_ref[:ENTRIES].astype(F32) + back_ref[ENTRIES : 2 * ENTRIES].astype(F32))
    rows = kept_ref[...] + back_ref[2 * ENTRIES :].astype(F32)
    rows_ref[...] = rows[: rows_ref.shape[0]]
    sums_ref[...] = bins
    put_bins(bins, sent_ref)
    sent_ref[2 * ENTRIES :] = rows[rows.shape[0] - sent_ref.shape[0] + 2 * ENTRIES :].astype(BF16)


def add_received(kept, bins, back, after):
    rows, width = kept.shape
    half = max(rows // 2, 16)
    return pl.pallas_call(
        add_received_kernel,
        in_specs=[IN_VMEM] * 3 + [ANYWHERE],
        out_specs=[IN_VMEM] * 3,
        out_shape=[
            pltpu.VMEM((half, width), F32),
            pltpu.VMEM(bins.shape, F32),
            pltpu.VMEM((2 * ENTRIES + half, width), BF16),
        ],
        compiler_params=params(),
        cost_estimate=cost(0.7),
        name="add_received",
    )(kept, bins, back, after)


ONE_CORE = [[2 * place + core for place in range(8)] for core in range(2)]


def other_core(array):
    return lax.ppermute(array, "inp", [(i, i ^ 1) for i in range(16)])


def exchange_inp(pieces):
    return lax.all_to_all(pieces, "inp", 0, 0, tiled=True, axis_index_groups=ONE_CORE)


def copies(array, count):
    return jnp.broadcast_to(array[None], (count,) + array.shape)


def total(arrays):
    return functools.reduce(jnp.add, [a.astype(F32) for a in arrays])


def choose_kernel(place_ref, gate_ref, up_ref, after_ref, own_ref, other_ref):
    gate_here = place_ref[0] == 0
    own_ref[...] = jnp.where(gate_here, gate_ref[...], up_ref[...])
    other_ref[...] = jnp.where(gate_here, up_ref[...], gate_ref[...])


def choose(place, gate, up, after):
    return pl.pallas_call(
        choose_kernel,
        in_specs=[SCALAR, IN_VMEM, IN_VMEM, ANYWHERE],
        out_specs=[IN_VMEM] * 2,
        out_shape=[pltpu.VMEM(gate.shape, F32)] * 2,
        compiler_params=params(),
        cost_estimate=cost(0.7),
        name="choose",
    )(place, gate, up, after)


def add_and_copy_kernel(own_ref, back_ref, after_ref, out_ref):
    both = (own_ref[...] + back_ref[...]).astype(BF16)
    for place in range(out_ref.shape[0]):
        out_ref[place] = both


def add_and_copy(own, back, after):
    return pl.pallas_call(
        add_and_copy_kernel,
        in_specs=[IN_VMEM] * 2 + [ANYWHERE],
        out_specs=IN_VMEM,
        out_shape=shape((8,) + own.shape, BF16),
        compiler_params=params(),
        cost_estimate=cost(0.7),
        name="add_and_copy",
    )(own, back, after)


def other_hid(array, bit):
    return lax.ppermute(array, "hid", [(i, i ^ bit) for i in range(16)])


def local_hidden(pre_gate, pre_up, hidden_grad):
    sig_gate = jax.nn.sigmoid(pre_gate)
    silu_gate = pre_gate * sig_gate
    activ = (silu_gate * pre_up).astype(BF16)
    gate_grad = (hidden_grad * pre_up * sig_gate * (1.0 + pre_gate * (1.0 - sig_gate))).astype(BF16)
    up_grad = (hidden_grad * silu_gate).astype(BF16)
    return activ, gate_grad, up_grad


def shards(inputs, out_grad, gate_index, up_index, down_index, gate_table, up_table, down_table):
    width = gate_index.shape[1]
    core = lax.axis_index("inp") % 2
    place = jnp.stack([core, lax.axis_index("hid")]).astype(I32)

    hidden_near, hidden_far, grad, x, gate_words, gate_lookup, up_lookup = forward_down(
        place, out_grad, down_table, down_index, (inputs, gate_index, gate_table, up_table)
    )
    hidden_back = other_core(hidden_far)
    gate_near, gate_far, w_gate, x_near, x, up_words = forward_up(place, x, gate_words, gate_lookup, up_index)
    gate_back = other_core(gate_far)
    up_near, up_far, w_up = forward_up(None, x_near, up_words, up_lookup, None)
    up_back = other_core(up_far)
    pair_sums = jnp.concatenate(
        [(gate_near + gate_back).astype(BF16), (up_near + up_back).astype(BF16), (hidden_near + hidden_back).astype(BF16)],
        axis=1,
    ).reshape(8, 8, 3 * width)
    pieces = exchange_inp(pair_sums)
    columns = width // LANES
    gate_sums = entry_sums(x, gate_index, 0, up_index, 0, (columns + 1) // 2, pair_sums)
    pieces, gate_sums = lax.optimization_barrier((pieces, gate_sums))
    pre = total(pieces)
    activ, gate_grad, up_grad = local_hidden(pre[:, :width], pre[:, width : 2 * width], pre[:, 2 * width :])
    grads = copies(jnp.concatenate([gate_grad, up_grad, activ], axis=1), 8)
    near = exchange_inp(grads)
    up_sums = entry_sums(x, up_index, 1, up_index, columns - 1, columns // 2, grads)
    near, up_sums = lax.optimization_barrier((near, up_sums))
    near = near.reshape(TOKENS // 2, 3 * width)
    activ_near, grad_near = near[:, 2 * width :], near[:, : 2 * width]
    activ_far, grad_far = other_core(activ_near), other_core(grad_near)

    down_sum, w_gate, w_up = down_bins(activ_near, activ_far, grad, down_index, (w_gate, w_up))
    kept, sent = input_grads(place, grad_near, grad_far, w_gate, w_up, down_sum)
    gate_part = table_sums(grad_near, grad_far, 0, [gate_sums], [(0, width, 0)], sent)
    kept, down_sum, sent = add_received(kept, down_sum, other_hid(sent, 4), gate_part)
    pieces = [(width, LANES, 0), (0, width - LANES, LANES)]
    up_part = table_sums(grad_near, grad_far, 1, [gate_sums, up_sums], pieces, sent)
    kept, down_sum, sent = add_received(kept, down_sum, other_hid(sent, 8), up_part)
    own, other = choose(place, gate_part, up_part, sent)
    own = total(exchange_inp(add_and_copy(own, other_core(other), up_part)))
    other = other_core(own)
    gate_sum, up_sum = jnp.where(core == 0, own, other), jnp.where(core == 0, other, own)
    kept, down_sum, sent = add_received(kept, down_sum, other_hid(sent, 1), sent)
    back = other_hid(sent, 2).astype(F32)
    input_grad = (kept[:8] + back[2 * ENTRIES + 8 :]).astype(BF16)
    down_sum = down_sum + (back[:ENTRIES] + back[ENTRIES : 2 * ENTRIES])
    scale = 1.0 / TOKENS
    return input_grad, gate_sum * scale, up_sum * scale, down_sum * scale


def solution(mesh):
    in_specs = (
        P(None, "inp"),
        P(None, "inp"),
        P("inp", "hid"),
        P("inp", "hid"),
        P("hid", "inp"),
        P(None, "hid"),
        P(None, "hid"),
        P(None, "inp"),
    )
    out_specs = (P("hid", "inp"), P(None, "hid"), P(None, "hid"), P(None, "inp"))
    return jax.shard_map(shards, mesh=mesh, in_specs=in_specs, out_specs=out_specs, check_vma=False)
```

```python
import functools

import jax
import jax.numpy as jnp
from jax import lax
from jax.experimental import pallas as pl
from jax.experimental.pallas import tpu as pltpu
from jax.sharding import PartitionSpec as P

BF16 = jnp.bfloat16
F32 = jnp.float32
I32 = jnp.int32
ENTRIES = 16
TOKENS = 128
LANES = 128
HBM_BYTES_PER_US = 3_000_000


def params(mib=16):
    return pltpu.CompilerParams(vmem_limit_bytes=mib * 1024 * 1024)


def cost(us):
    return pl.CostEstimate(flops=0, bytes_accessed=int(us * HBM_BYTES_PER_US), transcendentals=0)


def shape(dims, dtype):
    return jax.ShapeDtypeStruct(dims, dtype)


def dot(a, b):
    return jnp.dot(a, b, preferred_element_type=F32)


def dot_nt(a, b):
    return lax.dot_general(a, b, (((1,), (1,)), ((), ())), preferred_element_type=F32)


def dot_tn(a, b):
    return lax.dot_general(a, b, (((0,), (0,)), ((), ())), preferred_element_type=F32)


def iotas(size):
    return lax.broadcasted_iota(I32, (size, size), 0), lax.broadcasted_iota(I32, (size, size), 1)


def one_hot(hits):
    return jnp.where(hits, 1.0, 0.0).astype(BF16)


def split_matrix(block):
    source, target = iotas(block)
    half = block // 2
    return one_hot(source == jnp.where(target < half, 2 * target, 2 * (target - half) + 1))


def merge_matrix(block):
    source, target = iotas(block)
    half = block // 2
    return one_hot(target == jnp.where(source < half, 2 * source, 2 * (source - half) + 1))


def token_of(row, core):
    return (((row >> 3) & 7) * 2 + (core ^ (row >> 6))) * 8 + (row & 7)


def to_rows(core):
    row, token = iotas(TOKENS)
    return one_hot(token == token_of(row, core))


def to_owners(core, hid):
    owned, row = iotas(TOKENS)
    bits = ((owned >> 6) & 1) | ((owned >> 3) & 4) | ((owned >> 1) & 8) | ((owned >> 2) & 2)
    return one_hot(token_of(row, core) == (bits ^ hid) * 8 + (owned & 7))


SCALAR = pl.BlockSpec(memory_space=pltpu.SMEM)
ANYWHERE = pl.BlockSpec(memory_space=pl.ANY)
IN_HBM = pl.BlockSpec(memory_space=pltpu.HBM)
IN_VMEM = pl.BlockSpec(memory_space=pltpu.VMEM)
WIDE = 256
HALF = TOKENS // 2


def lookup(low, high, at, is_high):
    from_low = jnp.take_along_axis(low, at, axis=0, mode="promise_in_bounds")
    from_high = jnp.take_along_axis(high, at, axis=0, mode="promise_in_bounds")
    return jnp.where(is_high, from_high, from_low)


def decode_rows(index_ref, table_ref, weight_ref, begin, words):
    def tile(j, carry):
        cols = pl.ds(pl.multiple_of(j * LANES, LANES), LANES)
        low, high = table_ref[0:8, cols], table_ref[8:16, cols]
        for row in range(0, words, 16):
            even, odd = [], []
            for part in (row, row + 8):
                word = index_ref[begin + part : begin + part + 8, cols]
                even.append(lookup(low, high, word & 7, (word & 8) != 0))
                odd.append(lookup(low, high, (word >> 4) & 7, (word & 128) != 0))
            weight_ref[row : row + 16, cols] = jnp.concatenate(even, axis=0).astype(BF16)
            weight_ref[words + row : words + row + 16, cols] = jnp.concatenate(odd, axis=0).astype(BF16)
        return carry

    lax.fori_loop(0, index_ref.shape[1] // LANES, tile, 0)


def blocks_of(size, block):
    return [(at, min(block, size - at)) for at in range(0, size, block)]


def row_copies(from_ref, to_ref, sems, block):
    return [
        pltpu.make_async_copy(from_ref.at[pl.ds(at, rows)], to_ref.at[pl.ds(at, rows)], sems.at[i])
        for i, (at, rows) in enumerate(blocks_of(from_ref.shape[0], block))
    ]


def in_hbm(*arrays):
    return [pltpu.with_memory_space_constraint(each, pltpu.HBM) for each in arrays]


def start_all(copies):
    for each in copies:
        each.start()


def wait_all(copies):
    for each in copies:
        each.wait()


def forward_down_kernel(
    place_ref, raw_hbm, table_hbm, index_hbm, next_hbm, near_ref, far_ref, ordered_hbm, *refs
):
    count = len(next_hbm)
    next_refs = refs[:count]
    raw_ref, table_ref, index_ref, ordered_ref, weight_ref, sems, next_sems, sem = refs[count:]
    words = index_ref.shape[0]
    loads = row_copies(index_hbm, index_ref, sems, LANES)
    small = [pltpu.make_async_copy(raw_hbm, raw_ref, next_sems.at[count])]
    small.append(pltpu.make_async_copy(table_hbm, table_ref, next_sems.at[count + 1]))
    later = [pltpu.make_async_copy(a, b, next_sems.at[i]) for i, (a, b) in enumerate(zip(next_hbm, next_refs))]
    start_all(small + loads)
    wait_all(small)
    ordered_ref[...] = dot(to_rows(place_ref[0]), raw_ref[...]).astype(BF16)
    store = pltpu.make_async_copy(ordered_ref, ordered_hbm, sem)
    store.start()
    for i, (load, (at, rows)) in enumerate(zip(loads, blocks_of(words, LANES))):
        load.wait()
        if i == len(loads) // 2 - 1:
            start_all(later)
        decode_rows(index_ref, table_ref, weight_ref.at[pl.ds(2 * at, 2 * rows)], at, rows)
    merge = {rows: merge_matrix(2 * rows) for _, rows in blocks_of(words, LANES)}
    for at, rows in blocks_of(words, LANES):
        cols = slice(2 * at, 2 * (at + rows))
        hidden = dot_nt(ordered_ref[...], weight_ref[cols, :])
        coarse = hidden.astype(BF16)
        fine = (hidden - coarse.astype(F32)).astype(BF16)
        hidden = dot(coarse, merge[rows]) + dot(fine, merge[rows])
        near_ref[:, cols] = hidden[:HALF]
        far_ref[:, cols] = hidden[HALF:]
    store.wait()
    wait_all(later)


def forward_down(place, grad, table, index, brought):
    words, width = index.shape
    count = len(brought)

    def kernel(*refs):
        forward_down_kernel(*refs[:4], refs[4 : 4 + count], *refs[4 + count :])

    return pl.pallas_call(
        kernel,
        in_specs=[SCALAR] + [IN_HBM] * (3 + count),
        out_specs=[IN_VMEM, IN_VMEM, IN_HBM] + [IN_VMEM] * count,
        out_shape=[
            pltpu.VMEM((HALF, 2 * words), F32),
            pltpu.VMEM((HALF, 2 * words), F32),
            pltpu.HBM((TOKENS, width), BF16),
        ]
        + [pltpu.VMEM(each.shape, each.dtype) for each in brought],
        scratch_shapes=[
            pltpu.VMEM(grad.shape, BF16),
            pltpu.VMEM(table.shape, F32),
            pltpu.VMEM(index.shape, I32),
            pltpu.VMEM((TOKENS, width), BF16),
            pltpu.VMEM((2 * words, width), BF16),
            pltpu.SemaphoreType.DMA((pl.cdiv(words, LANES),)),
            pltpu.SemaphoreType.DMA((count + 2,)),
            pltpu.SemaphoreType.DMA,
        ],
        compiler_params=params(),
        cost_estimate=cost(5),
        name="forward_down",
    )(place, *in_hbm(grad, table, index, *brought))


def forward_up_kernel(first, *refs):
    if first:
        place_ref, raw_ref, index_ref, table_ref, next_hbm, near_ref, far_ref, weight_hbm = refs[:8]
        x_ref, x_hbm, next_ref, weight_ref, sems, next_sems = refs[8:]
        later = [pltpu.make_async_copy(next_hbm, next_ref, next_sems.at[0])]
        start_all(later)
        x = dot(to_rows(place_ref[0]), raw_ref[...]).astype(BF16)
        for at in range(0, x.shape[1], WIDE):
            x_ref[:, at : at + WIDE] = dot(x[:, at : at + WIDE], split_matrix(WIDE)).astype(BF16)
        later.append(pltpu.make_async_copy(x_ref, x_hbm, next_sems.at[1]))
        start_all(later[1:])
    else:
        x_ref, index_ref, table_ref, near_ref, far_ref, weight_hbm, weight_ref, sems = refs
        later = []
    stores = row_copies(weight_ref, weight_hbm, sems, WIDE)
    for store, at in zip(stores, range(0, index_ref.shape[0], LANES)):
        decode_rows(index_ref, table_ref, weight_ref.at[pl.ds(2 * at, WIDE)], at, LANES)
        store.start()
    for at, cols in blocks_of(index_ref.shape[1], WIDE):
        sums = dot(x_ref[...], weight_ref[:, at : at + cols])
        near_ref[:, at : at + cols] = sums[:HALF]
        far_ref[:, at : at + cols] = sums[HALF:]
    wait_all(stores + later)


def forward_up(place, x, index, table, later_index):
    first = place is not None
    words, width = index.shape
    ordered = (TOKENS, 2 * words)
    return pl.pallas_call(
        functools.partial(forward_up_kernel, first),
        in_specs=[SCALAR] * first + [IN_VMEM] * 3 + [IN_HBM] * first,
        out_specs=[IN_VMEM, IN_VMEM, IN_HBM] + [IN_VMEM, IN_HBM, IN_VMEM] * first,
        out_shape=[
            pltpu.VMEM((HALF, width), F32),
            pltpu.VMEM((HALF, width), F32),
            pltpu.HBM((2 * words, width), BF16),
        ]
        + [pltpu.VMEM(ordered, BF16), pltpu.HBM(ordered, BF16), pltpu.VMEM((words, width), I32)] * first,
        scratch_shapes=[pltpu.VMEM((2 * words, width), BF16), pltpu.SemaphoreType.DMA((2 * words // WIDE,))]
        + [pltpu.SemaphoreType.DMA((2,))] * first,
        compiler_params=params(),
        cost_estimate=cost(5),
        name="forward_gate" if first else "forward_up",
    )(*([place] * first + [x, index, table] + in_hbm(*[later_index] * first)))


def entry_sums_kernel(x_ref, left_ref, right_ref, last_ref, after_ref, out_ref, entry_ref):
    words = left_ref.shape[0]

    def unpack(half_ref, cols):
        for row in range(0, words, 16):
            word = half_ref[row : row + 16, :]
            to = row // LANES * WIDE + row % LANES
            entry_ref[to : to + 16, cols] = (word & 15).astype(jnp.int16)
            entry_ref[to + LANES : to + LANES + 16, cols] = ((word >> 4) & 15).astype(jnp.int16)

    last = pl.program_id(0) == pl.num_programs(0) - 1
    unpack(left_ref, slice(0, LANES))
    pl.when(jnp.logical_not(last))(lambda: unpack(right_ref, slice(LANES, WIDE)))
    pl.when(last)(lambda: unpack(last_ref, slice(LANES, WIDE)))
    x = x_ref[...]
    one, zero = jnp.ones((), BF16), jnp.zeros((), BF16)
    rest = jnp.sum(x.astype(F32), axis=1, keepdims=True)
    for entry in range(ENTRIES - 1):
        chosen = jnp.where(entry_ref[...] == jnp.int16(entry), one, zero)
        sums = dot(x, chosen)
        out_ref[entry] = sums.astype(BF16)
        rest = rest - sums
    out_ref[ENTRIES - 1] = rest.astype(BF16)


def entry_sums(x, index, first, last_index, last, blocks, after):
    words = index.shape[0]
    limit = index.shape[1] // LANES - 1
    return pl.pallas_call(
        entry_sums_kernel,
        grid=(blocks,),
        in_specs=[
            pl.BlockSpec((TOKENS, 2 * words), lambda i: (0, 0)),
            pl.BlockSpec((words, LANES), lambda i: (0, first + 2 * i)),
            pl.BlockSpec((words, LANES), lambda i: (0, jnp.minimum(first + 2 * i + 1, limit))),
            pl.BlockSpec((words, LANES), lambda i: (0, last)),
            ANYWHERE,
        ],
        out_specs=pl.BlockSpec((ENTRIES, TOKENS, WIDE), lambda i: (0, 0, i)),
        out_shape=shape((ENTRIES, TOKENS, blocks * WIDE), BF16),
        scratch_shapes=[pltpu.VMEM((2 * words, WIDE), jnp.int16)],
        compiler_params=params(60),
        cost_estimate=cost(11),
        name="entry_sums",
    )(x, index, index, last_index, after)


def table_sums_kernel(part, pieces, near_ref, far_ref, *refs):
    sums_hbm = refs[: len(pieces)]
    after_ref, out_ref, grad_ref, sums_ref, sems = refs[len(pieces) :]
    count = ENTRIES // sems.shape[0]
    loads = []
    for i in range(sems.shape[0]):
        entries = pl.ds(i * count, count)
        loads.append([])
        for j, (begin, cols, to) in enumerate(pieces):
            source = sums_hbm[j].at[entries, :, pl.ds(begin, cols)]
            loads[i].append(pltpu.make_async_copy(source, sums_ref.at[entries, :, pl.ds(to, cols)], sems.at[i, j]))
        start_all(loads[i])
    width = sums_ref.shape[2]
    grad_ref[:HALF, :] = near_ref[:, part * width : (part + 1) * width].astype(F32)
    grad_ref[HALF:, :] = far_ref[:, part * width : (part + 1) * width].astype(F32)
    for load, begin in zip(loads, range(0, ENTRIES, count)):
        wait_all(load)

        def tile(j, carry, begin=begin):
            cols = pl.ds(pl.multiple_of(j * LANES, LANES), LANES)
            rows = []
            for entry in range(begin, begin + count):
                acc = None
                for row in range(0, TOKENS, 16):
                    product = sums_ref[entry, row : row + 16, cols].astype(F32) * grad_ref[row : row + 16, cols]
                    acc = product if acc is None else acc + product
                rows.append(jnp.sum(acc, axis=0, keepdims=True))
            out_ref[begin : begin + count, cols] = jnp.concatenate(rows, axis=0)
            return carry

        lax.fori_loop(0, width // LANES, tile, 0)


def table_sums(near, far, part, sums, pieces, after):
    width = sum(cols for _, cols, _ in pieces)
    return pl.pallas_call(
        functools.partial(table_sums_kernel, part, pieces),
        in_specs=[IN_VMEM, IN_VMEM] + [IN_HBM] * len(sums) + [ANYWHERE],
        out_specs=IN_VMEM,
        out_shape=pltpu.VMEM((ENTRIES, width), F32),
        scratch_shapes=[
            pltpu.VMEM((TOKENS, width), F32),
            pltpu.VMEM((ENTRIES, TOKENS, width), BF16),
            pltpu.SemaphoreType.DMA((4, len(pieces))),
        ],
        compiler_params=params(),
        cost_estimate=cost(4.5),
        name="table_sums",
    )(near, far, *in_hbm(*sums), after)


def down_bins_kernel(near_ref, far_ref, grad_hbm, index_hbm, next_hbm, out_ref, next_refs, *scratch):
    grad_ref, index_ref, activ_ref, wgrad_ref, sems = scratch
    loads = [pltpu.make_async_copy(grad_hbm, grad_ref, sems.at[0])]
    loads.append(pltpu.make_async_copy(index_hbm, index_ref, sems.at[1]))
    loads += [pltpu.make_async_copy(a, b, sems.at[2 + i]) for i, (a, b) in enumerate(zip(next_hbm, next_refs))]
    start_all(loads)
    block = LANES
    half = block // 2
    words, width = index_ref.shape
    split = split_matrix(block)
    for at in range(0, 2 * words, block):
        cols = slice(at, at + block)
        activ = jnp.concatenate([near_ref[:, cols], far_ref[:, cols]], axis=0)
        activ_ref[:, cols] = dot(activ, split).astype(BF16)
    wait_all(loads[:1])
    for at in range(0, width, WIDE):
        wgrad_ref[:, at : at + WIDE] = dot_tn(activ_ref[...], grad_ref[:, at : at + WIDE]).astype(BF16)
    wait_all(loads[1:2])
    zero = jnp.zeros((), BF16)

    def lanes(j, carry):
        cols = pl.ds(pl.multiple_of(j * LANES, LANES), LANES)

        def add_block(i, totals):
            part = [None] * ENTRIES
            for row in range(0, half, 16):
                word = index_ref[pl.ds(pl.multiple_of(i * half + row, 16), 16), cols].astype(jnp.int16)
                for entries, offset in ((word & 15, 0), ((word >> 4) & 15, half)):
                    grads = wgrad_ref[pl.ds(pl.multiple_of(i * block + offset + row, 16), 16), cols]
                    for entry in range(ENTRIES):
                        chosen = jnp.where(entries == jnp.int16(entry), grads, zero)
                        part[entry] = chosen if part[entry] is None else part[entry] + chosen
            done = []
            for entry in range(ENTRIES):
                both = part[entry].astype(F32)
                done.append(totals[entry] + both[:8] + both[8:])
            return tuple(done)

        start = tuple(jnp.zeros((8, LANES), F32) for _ in range(ENTRIES))
        totals = lax.fori_loop(0, 2 * words // block, add_block, start)
        out_ref[:, cols] = jnp.concatenate([jnp.sum(each, axis=0, keepdims=True) for each in totals], axis=0)
        return carry

    lax.fori_loop(0, width // LANES, lanes, 0)
    wait_all(loads[2:])


def down_bins(near, far, grad, index, brought):
    words, width = index.shape
    count = len(brought)

    def kernel(*refs):
        out = 4 + count
        down_bins_kernel(*refs[:4], refs[4:out], refs[out], refs[out + 1 : out + 1 + count], *refs[out + 1 + count :])

    return pl.pallas_call(
        kernel,
        in_specs=[IN_VMEM] * 2 + [IN_HBM] * (2 + count),
        out_specs=[IN_VMEM] * (1 + count),
        out_shape=[pltpu.VMEM((ENTRIES, width), F32)] + [pltpu.VMEM(each.shape, each.dtype) for each in brought],
        scratch_shapes=[
            pltpu.VMEM((TOKENS, width), BF16),
            pltpu.VMEM((words, width), I32),
            pltpu.VMEM((TOKENS, 2 * words), BF16),
            pltpu.VMEM((2 * words, width), BF16),
            pltpu.SemaphoreType.DMA((2 + count,)),
        ],
        compiler_params=params(),
        cost_estimate=cost(10),
        name="down_bins",
    )(near, far, *in_hbm(grad, index, *brought))


def input_grad_kernel(
    place_ref, near_ref, far_ref, wg_ref, wu_ref, bins_ref, kept_ref, sent_ref
):
    rows, width = wg_ref.shape
    gate = jnp.concatenate([near_ref[:, :width], far_ref[:, :width]], axis=0)
    up = jnp.concatenate([near_ref[:, width:], far_ref[:, width:]], axis=0)
    order = to_owners(place_ref[0], place_ref[1])
    merge = merge_matrix(WIDE)

    def product(i, carry):
        at = pl.ds(pl.multiple_of(i * WIDE, WIDE), WIDE)
        part = (dot_nt(gate, wg_ref[at, :]) + dot_nt(up, wu_ref[at, :])).astype(BF16)
        part = dot(dot(order, part).astype(BF16), merge)
        kept_ref[:, at] = part[:HALF]
        sent_ref[ENTRIES:, at] = part[HALF:].astype(BF16)
        return carry

    lax.fori_loop(0, rows // WIDE, product, 0)
    sent_ref[:ENTRIES] = bins_ref[...].astype(BF16)


def input_grads(place, near, far, w_gate, w_up, bins):
    width = w_gate.shape[0]
    return pl.pallas_call(
        input_grad_kernel,
        in_specs=[SCALAR] + [IN_VMEM] * 5,
        out_specs=[IN_VMEM] * 2,
        out_shape=[pltpu.VMEM((HALF, width), F32), pltpu.VMEM((ENTRIES + HALF, width), BF16)],
        compiler_params=params(),
        cost_estimate=cost(3.5),
        name="input_grad",
    )(place, near, far, w_gate, w_up, bins)


def add_received_kernel(kept_ref, bins_ref, back_ref, after_ref, rows_ref, sums_ref, sent_ref):
    bins = bins_ref[...] + back_ref[:ENTRIES].astype(F32)
    rows = kept_ref[...] + back_ref[ENTRIES:].astype(F32)
    rows_ref[...] = rows[: rows_ref.shape[0]]
    sums_ref[...] = bins
    sent_ref[:ENTRIES] = bins.astype(BF16)
    sent_ref[ENTRIES:] = rows[rows.shape[0] - sent_ref.shape[0] + ENTRIES :].astype(BF16)


def add_received(kept, bins, back, after):
    rows, width = kept.shape
    half = max(rows // 2, 16)
    return pl.pallas_call(
        add_received_kernel,
        in_specs=[IN_VMEM] * 3 + [ANYWHERE],
        out_specs=[IN_VMEM] * 3,
        out_shape=[
            pltpu.VMEM((half, width), F32),
            pltpu.VMEM(bins.shape, F32),
            pltpu.VMEM((ENTRIES + half, width), BF16),
        ],
        compiler_params=params(),
        cost_estimate=cost(0.7),
        name="add_received",
    )(kept, bins, back, after)


def add_places_kernel(pieces_ref, after_ref, out_ref):
    sums = pieces_ref[0].astype(F32)
    for place in range(1, pieces_ref.shape[0]):
        sums = sums + pieces_ref[place].astype(F32)
    out_ref[...] = sums


def add_places(pieces, after):
    return pl.pallas_call(
        add_places_kernel,
        in_specs=[IN_VMEM, ANYWHERE],
        out_specs=IN_VMEM,
        out_shape=pltpu.VMEM(pieces.shape[1:], F32),
        compiler_params=params(),
        cost_estimate=cost(0.7),
        name="add_places",
    )(pieces, after)


def finish_kernel(place_ref, kept_ref, bins_ref, back_ref, own_ref, other_ref, grad_ref, gate_ref, up_ref, down_ref):
    scale = 1.0 / TOKENS
    back = back_ref[...].astype(F32)
    grad_ref[...] = (kept_ref[:8] + back[ENTRIES + 8 :]).astype(BF16)
    down_ref[...] = (bins_ref[...] + back[:ENTRIES]) * scale
    gate_here = place_ref[0] == 0
    gate_ref[...] = jnp.where(gate_here, own_ref[...], other_ref[...]) * scale
    up_ref[...] = jnp.where(gate_here, other_ref[...], own_ref[...]) * scale


def finish(place, kept, bins, back, own, other):
    return pl.pallas_call(
        finish_kernel,
        in_specs=[SCALAR] + [IN_VMEM] * 5,
        out_specs=[IN_VMEM] * 4,
        out_shape=[shape((8, kept.shape[1]), BF16), shape(own.shape, F32), shape(own.shape, F32), shape(bins.shape, F32)],
        compiler_params=params(),
        cost_estimate=cost(0.7),
        name="finish",
    )(place, kept, bins, back, own, other)


ONE_CORE = [[2 * place + core for place in range(8)] for core in range(2)]


def other_core(array):
    return lax.ppermute(array, "inp", [(i, i ^ 1) for i in range(16)])


def exchange_inp(pieces):
    return lax.all_to_all(pieces, "inp", 0, 0, tiled=True, axis_index_groups=ONE_CORE)


def copies(array, count):
    return jnp.broadcast_to(array[None], (count,) + array.shape)


def total(arrays):
    return functools.reduce(jnp.add, [a.astype(F32) for a in arrays])


def choose_kernel(place_ref, gate_ref, up_ref, after_ref, own_ref, other_ref):
    gate_here = place_ref[0] == 0
    own_ref[...] = jnp.where(gate_here, gate_ref[...], up_ref[...])
    other_ref[...] = jnp.where(gate_here, up_ref[...], gate_ref[...])


def choose(place, gate, up, after):
    return pl.pallas_call(
        choose_kernel,
        in_specs=[SCALAR, IN_VMEM, IN_VMEM, ANYWHERE],
        out_specs=[IN_VMEM] * 2,
        out_shape=[pltpu.VMEM(gate.shape, F32)] * 2,
        compiler_params=params(),
        cost_estimate=cost(0.7),
        name="choose",
    )(place, gate, up, after)


def add_and_copy_kernel(own_ref, back_ref, after_ref, out_ref):
    both = (own_ref[...] + back_ref[...]).astype(BF16)
    for place in range(out_ref.shape[0]):
        out_ref[place] = both


def add_and_copy(own, back, after):
    return pl.pallas_call(
        add_and_copy_kernel,
        in_specs=[IN_VMEM] * 2 + [ANYWHERE],
        out_specs=IN_VMEM,
        out_shape=shape((8,) + own.shape, BF16),
        compiler_params=params(),
        cost_estimate=cost(0.7),
        name="add_and_copy",
    )(own, back, after)


def other_hid(array, bit):
    return lax.ppermute(array, "hid", [(i, i ^ bit) for i in range(16)])


def local_hidden(pre_gate, pre_up, hidden_grad):
    sig_gate = jax.nn.sigmoid(pre_gate)
    silu_gate = pre_gate * sig_gate
    activ = (silu_gate * pre_up).astype(BF16)
    gate_grad = (hidden_grad * pre_up * sig_gate * (1.0 + pre_gate * (1.0 - sig_gate))).astype(BF16)
    up_grad = (hidden_grad * silu_gate).astype(BF16)
    return activ, gate_grad, up_grad


def shards(inputs, out_grad, gate_index, up_index, down_index, gate_table, up_table, down_table):
    width = gate_index.shape[1]
    core = lax.axis_index("inp") % 2
    place = jnp.stack([core, lax.axis_index("hid")]).astype(I32)

    hidden_near, hidden_far, grad, x, gate_words, gate_lookup, up_lookup = forward_down(
        place, out_grad, down_table, down_index, (inputs, gate_index, gate_table, up_table)
    )
    hidden_back = other_core(hidden_far)
    gate_near, gate_far, w_gate, x_near, x, up_words = forward_up(place, x, gate_words, gate_lookup, up_index)
    gate_back = other_core(gate_far)
    up_near, up_far, w_up = forward_up(None, x_near, up_words, up_lookup, None)
    up_back = other_core(up_far)
    pair_sums = jnp.concatenate(
        [(gate_near + gate_back).astype(BF16), (up_near + up_back).astype(BF16), (hidden_near + hidden_back).astype(BF16)],
        axis=1,
    ).reshape(8, 8, 3 * width)
    pieces = exchange_inp(pair_sums)
    columns = width // LANES
    gate_sums = entry_sums(x, gate_index, 0, up_index, 0, (columns + 1) // 2, pair_sums)
    pieces, gate_sums = lax.optimization_barrier((pieces, gate_sums))
    pre = total(pieces)
    activ, gate_grad, up_grad = local_hidden(pre[:, :width], pre[:, width : 2 * width], pre[:, 2 * width :])
    grads = copies(jnp.concatenate([gate_grad, up_grad, activ], axis=1), 8)
    near = exchange_inp(grads)
    up_sums = entry_sums(x, up_index, 1, up_index, columns - 1, columns // 2, grads)
    near, up_sums = lax.optimization_barrier((near, up_sums))
    near = near.reshape(TOKENS // 2, 3 * width)
    activ_near, grad_near = near[:, 2 * width :], near[:, : 2 * width]
    activ_far, grad_far = other_core(activ_near), other_core(grad_near)

    down_sum, w_gate, w_up = down_bins(activ_near, activ_far, grad, down_index, (w_gate, w_up))
    kept, sent = input_grads(place, grad_near, grad_far, w_gate, w_up, down_sum)
    gate_part = table_sums(grad_near, grad_far, 0, [gate_sums], [(0, width, 0)], sent)
    kept, down_sum, sent = add_received(kept, down_sum, other_hid(sent, 1), gate_part)
    pieces = [(width, LANES, 0), (0, width - LANES, LANES)]
    up_part = table_sums(grad_near, grad_far, 1, [gate_sums, up_sums], pieces, sent)
    kept, down_sum, sent = add_received(kept, down_sum, other_hid(sent, 4), up_part)
    own, other = choose(place, gate_part, up_part, sent)
    back = other_core(other)
    kept, down_sum, sent = add_received(kept, down_sum, other_hid(sent, 8), back)
    last = other_hid(sent, 2)
    own = add_places(exchange_inp(add_and_copy(own, back, sent)), last)
    return tuple(finish(place, kept, down_sum, last, own, other_core(own)))


def solution(mesh):
    in_specs = (
        P(None, "inp"),
        P(None, "inp"),
        P("inp", "hid"),
        P("inp", "hid"),
        P("hid", "inp"),
        P(None, "hid"),
        P(None, "hid"),
        P(None, "inp"),
    )
    out_specs = (P("hid", "inp"), P(None, "hid"), P(None, "hid"), P(None, "inp"))
    return jax.shard_map(shards, mesh=mesh, in_specs=in_specs, out_specs=out_specs, check_vma=False)
```
